32 devices in a mesh: dp: 16 (over z, y, x), tensor: 2 (over core).
Axes of the slice: x: 2, y: 2, z: 4, core: 2. Of those that a mesh axis runs over, the one named last changes fastest.
Arguments:
- patches: bfloat16 [16, 16, 32, 1024], P('dp'), may hold values from -6 to 6
- counts: int32 [16, 16], replicated, may hold values from 1 to 32, 256 in all within a row
- doc_ids: int32 [16, 256], P('dp'), may hold values from 0 to 3, never falling along the last dimension, each value on 1 to 128 neighbouring positions
- w_query: bfloat16 [1024, 1024], P('dp', 'tensor'), may hold values from -0.1875 to 0.1875
- w_key: bfloat16 [1024, 1024], P('dp', 'tensor'), may hold values from -0.1875 to 0.1875
- w_value: bfloat16 [1024, 1024], P('dp', 'tensor'), may hold values from -0.1875 to 0.1875
- w_output: bfloat16 [1024, 1024], P('tensor', 'dp'), may hold values from -0.75 to 0.75
- w_gate: bfloat16 [1024, 2816], P('dp', 'tensor'), may hold values from -0.1875 to 0.1875
- w_up: bfloat16 [1024, 2816], P('dp', 'tensor'), may hold values from -0.1875 to 0.1875
- w_down: bfloat16 [2816, 1024], P('tensor', 'dp'), may hold values from -0.109375 to 0.109375
- gain_attn: bfloat16 [1024], P('dp'), may hold values from 0.25 to 1.75
- gain_ffn: bfloat16 [1024], P('dp'), may hold values from 0.25 to 1.75
- cotangent: bfloat16 [16, 16, 32, 1024], P('dp'), may hold values from -6 to 6
Outputs:
- outputs: bfloat16 [16, 16, 32, 1024], P('dp')
- input_grad: bfloat16 [16, 16, 32, 1024], P('dp')
- grad_w_query: float32 [1024, 1024], P('dp', 'tensor')
- grad_w_key: float32 [1024, 1024], P('dp', 'tensor')
- grad_w_value: float32 [1024, 1024], P('dp', 'tensor')
- grad_w_output: float32 [1024, 1024], P('tensor', 'dp')
- grad_w_gate: float32 [1024, 2816], P('dp', 'tensor')
- grad_w_up: float32 [1024, 2816], P('dp', 'tensor')
- grad_w_down: float32 [2816, 1024], P('tensor', 'dp')
- grad_gain_attn: float32 [1024], P('dp')
- grad_gain_ffn: float32 [1024], P('dp')
The draws below stay inside these ranges and needn't reach their ends.
Inputs may be any that keep to these rules, and one draw needn't show every extreme that they name: Each row of counts sums to 256 and its largest entry is 32. `doc_ids`: along each row the document numbers never fall; a document holds 1 to 128 patches of a row, and one holds exactly that many.
All inputs are finite; a program needn't handle non-finite values.
Results may differ from the reference program's by a relative error of at most 0.017.
Values may be sent and summed in bfloat16 or wider, within the bound.
No kernel may reach another device: no remote copies, remote signals or barrier semaphores. Data moves between devices by JAX's collectives and lax.ppermute only.
A program may use at most 128 MiB of HBM per device.

```python
import math
import jax
import jax.numpy as jnp
import numpy as np
from jax import lax

D = 1024
H = 16
DH = 64
FF = 2816
TOK_DEV = 256
DOCS = 4
SLOT = 32
N_DP = 16


def steps_of(own_key, extent, shards, least, top_value):
    factor_of = 1.0
    for dim, blocks in shards:
        draws = jax.random.uniform(jax.random.fold_in(jax.random.fold_in(own_key, 6), dim), (blocks,), jnp.float32, least / len(shards), top_value / len(shards))
        factor_of = factor_of * jnp.repeat(jnp.exp(draws), extent[dim] // blocks).reshape((-1,) + (1,) * (len(extent) - 1 - dim))
    return factor_of


def length_profile(count, total, bound, lean):
    weights = [(1 << 20) // math.isqrt(standing ** lean) + 1 for standing in range(2, count + 1)]
    rest, given = total - bound - (count - 1), [1] * (count - 1)
    while rest > 0:
        movable = [i for i in range(count - 1) if given[i] < bound]
        pool, remaining = sum([weights[i] for i in movable]), rest
        for i in movable:
            more = min(bound - given[i], max(1, remaining * weights[i] // pool), rest)
            given[i] = given[i] + more
            rest = rest - more
    return np.array([bound] + given)


def ragged(own_key, amount, total, most, lean):
    if amount == 2:
        one = jax.random.randint(own_key, (), max(1, total - most), min(most, total - 1) + 1)
        return jnp.stack([one, total - one])
    tallies = jnp.asarray(length_profile(amount, total, most, lean), jnp.int32)
    pairs = (amount - 1) // 2
    giver, receiver = tallies[1:1 + 2 * pairs:2], tallies[2:2 + 2 * pairs:2]
    margin = jnp.minimum(giver - 1, most - receiver)
    shifted = jax.random.randint(jax.random.fold_in(own_key, 1), (pairs,), 0, 1 << 20) % (margin + 1)
    tallies = tallies.at[1:1 + 2 * pairs:2].set(giver - shifted).at[2:2 + 2 * pairs:2].set(receiver + shifted)
    return tallies[jax.random.permutation(jax.random.fold_in(own_key, 2), amount)]


def normal_values(stream_key, dims, width, most, cuts=(), kind=jnp.bfloat16):
    entries = width * jax.random.normal(stream_key, dims, jnp.float32)
    if cuts:
        entries = entries * steps_of(stream_key, dims, cuts, -0.22, 0.18)
    return jnp.clip(entries, -most, most).astype(kind)


def setup_inputs(seed: int = 0) -> dict:
    keys = jax.random.split(jax.random.key(seed), 14)
    return {
        "patches": normal_values(keys[0], (N_DP, N_DP, SLOT, D), 1.0, 6.0, ((0, 16),)),
        "counts": jax.vmap(lambda own: ragged(own, N_DP, TOK_DEV, SLOT, 1))(jax.random.split(keys[1], N_DP)).reshape((N_DP, N_DP)).astype(jnp.int32),
        "doc_ids": jax.vmap(lambda own: jnp.searchsorted(jnp.cumsum(ragged(own, DOCS, TOK_DEV, TOK_DEV // 2, 0)), jnp.arange(TOK_DEV), side="right"))(jax.random.split(keys[2], N_DP)).reshape((N_DP, TOK_DEV)).astype(jnp.int32),
        "w_query": normal_values(keys[3], (D, D), D ** -0.5, 0.1875, ((0, 16), (1, 2))),
        "w_key": normal_values(keys[4], (D, D), D ** -0.5, 0.1875, ((0, 16), (1, 2))),
        "w_value": normal_values(keys[5], (D, D), D ** -0.5, 0.1875, ((0, 16), (1, 2))),
        "w_output": normal_values(keys[6], (D, D), DH ** -0.5, 0.75, ((0, 2), (1, 16))),
        "w_gate": normal_values(keys[7], (D, FF), D ** -0.5, 0.1875, ((0, 16), (1, 2))),
        "w_up": normal_values(keys[8], (D, FF), D ** -0.5, 0.1875, ((0, 16), (1, 2))),
        "w_down": normal_values(keys[9], (FF, D), FF ** -0.5, 0.109375, ((0, 2), (1, 16))),
        "gain_attn": jnp.clip(1.0 + 0.15 * jax.random.normal(keys[10], (D,), jnp.float32), 0.25, 1.75).astype(jnp.bfloat16),
        "gain_ffn": jnp.clip(1.0 + 0.15 * jax.random.normal(keys[11], (D,), jnp.float32), 0.25, 1.75).astype(jnp.bfloat16),
        "cotangent": normal_values(keys[12], (N_DP, N_DP, SLOT, D), 1.0, 6.0, ((0, 16),)),
    }


eps = 1e-05
masked_score = -1e+30
highest = lax.Precision.HIGHEST

@jax.custom_vjp
def low(v):
    return lax.optimization_barrier(v.astype(jnp.bfloat16)).astype(jnp.float32)

@jax.custom_vjp
def low_back(v):
    return v

def low_keep(v):
    return (low(v), None)

def low_pass(kept, grad):
    return (grad,)

def back_keep(v):
    return (v, None)

def back_low(kept, grad):
    return (low(grad),)
low.defvjp(low_keep, low_pass)
low_back.defvjp(back_keep, back_low)

def matmul(left, right):
    return jnp.dot(left, right, precision=highest)

def rms_normed(values, gain):
    return values * lax.rsqrt(lax.optimization_barrier(jnp.mean(values * values, axis=-1, keepdims=True)) + eps) * gain

def layout(counts):
    offsets = jnp.cumsum(counts, axis=1) - counts
    position = jnp.arange(TOK_DEV, dtype=jnp.int32)
    reached = offsets[:, None, :] <= position[None, :, None]
    source = lax.optimization_barrier(jnp.sum(reached.astype(jnp.int32), axis=2)) - 1
    first_slot = lax.optimization_barrier(jnp.max(jnp.where(reached, offsets[:, None, :], 0), axis=2))
    return (offsets, source, position[None, :] - first_slot)

def row_layer(row_in, doc_row, w_query, w_key, w_value, w_output, w_gate, w_up, w_down, gain_attn, gain_ffn):
    tok_count = row_in.shape[0]
    normed = low(rms_normed(row_in, gain_attn))
    query_mat = low(low_back(matmul(normed, w_query))).reshape(tok_count, H, DH)
    key_mat = low(low_back(matmul(normed, w_key))).reshape(tok_count, H, DH)
    value_mat = low(low_back(matmul(normed, w_value))).reshape(tok_count, H, DH)
    raw_scores = jnp.einsum('thd,shd->hts', query_mat, key_mat, precision=highest) * DH ** (-0.5)
    raw_scores = low_back(raw_scores)
    position = jnp.arange(tok_count)
    visible = (doc_row[:, None] == doc_row[None, :]) & (position[None, :] <= position[:, None])
    chances = low(jax.nn.softmax(jnp.where(visible[None], raw_scores, masked_score), axis=-1))
    attended = jnp.einsum('hts,shd->thd', chances, value_mat, precision=highest).reshape(tok_count, H * DH)
    attended = low(low_back(attended))
    hidden = row_in + low_back(matmul(attended, w_output))
    normed_ffn = low(rms_normed(hidden, gain_ffn))
    gate_pre = low_back(matmul(normed_ffn, w_gate))
    up_proj = low_back(matmul(normed_ffn, w_up))
    product = low(jax.nn.silu(gate_pre) * up_proj)
    return hidden + low_back(matmul(product, w_down))

def reference(patches, counts, doc_ids, w_query, w_key, w_value, w_output, w_gate, w_up, w_down, gain_attn, gain_ffn, cotangent):
    offsets, source, slot_of = layout(counts)
    row_ids = jnp.arange(N_DP, dtype=jnp.int32)[:, None]
    places = jnp.arange(SLOT, dtype=jnp.int32)
    back_index = jnp.minimum(offsets[:, :, None] + places[None, None, :], TOK_DEV - 1)
    back_valid = places[None, None, :] < counts[:, :, None]

    def forward(patch_vals, wq_f, wk_f, wv_f, wo_f, wg_f, wu_f, wd_f, ga_f, gf_f):
        balanced = patch_vals[source, row_ids, slot_of]
        params = (wq_f, wk_f, wv_f, wo_f, wg_f, wu_f, wd_f, ga_f, gf_f)

        def one_row(pair):
            return jax.checkpoint(row_layer)(pair[0], pair[1], *params)
        result = lax.map(one_row, (balanced, doc_ids))
        picked = result[row_ids[:, :, None], back_index]
        picked = jnp.where(back_valid[..., None], picked, jnp.zeros_like(picked))
        return jnp.transpose(picked, (1, 0, 2, 3))
    floats = tuple((item.astype(jnp.float32) for item in (patches, w_query, w_key, w_value, w_output, w_gate, w_up, w_down, gain_attn, gain_ffn)))
    outputs, pull = jax.vjp(forward, *floats)
    grads = pull(cotangent.astype(jnp.float32))
    return (outputs.astype(jnp.bfloat16), grads[0].astype(jnp.bfloat16), grads[1], grads[2], grads[3], grads[4], grads[5], grads[6], grads[7], grads[8], grads[9])
```

```python
import jax
import jax.numpy as jnp
import numpy as np
from jax import lax
from jax.sharding import Mesh, PartitionSpec as P

DH = 64
eps = 1e-05
masked_score = -1e30
bf16 = jnp.bfloat16
f32 = jnp.float32

DP = ("z", "yh", "yl", "xh", "xl")
FAR = ("z", "yh", "xh")
NEAR = ("yl", "xl")
CORE = "c"


def mm(left, right):
    return lax.dot_general(left, right, (((1,), (0,)), ((), ())), preferred_element_type=f32)


def mm_t(left, right):
    return lax.dot_general(left, right, (((1,), (1,)), ((), ())), preferred_element_type=f32)


def outer_sum(left, right):
    return lax.dot_general(left, right, (((0,), (0,)), ((), ())), preferred_element_type=f32)


def swap(value):
    return lax.ppermute(value, CORE, [(0, 1), (1, 0)])


def near(value, k):
    return lax.ppermute(value, NEAR, [(i, i ^ k) for i in range(4)])


def gather_near(value):
    return jnp.concatenate([value] + [near(value, k) for k in (1, 2, 3)], axis=0)


def scatter_near(partial):
    low = partial.astype(bf16)
    total = partial[0]
    for k in (1, 2, 3):
        total = total + near(low[k], k).astype(f32)
    return total


def inverse_root(values):
    return lax.rsqrt(jnp.mean(values * values, axis=-1, keepdims=True) + eps)


def natural_rows(weight, far_sizes, rows):
    nz, nyh, nxh = far_sizes
    if nyh * nxh == 1:
        return weight
    cols = weight.shape[-1]
    split = weight.reshape(nz, nyh, nxh, 2, 2, rows, cols)
    return split.transpose(0, 1, 3, 2, 4, 5, 6).reshape(-1, cols)


def far_rows(weight, far_sizes, rows):
    nz, nyh, nxh = far_sizes
    if nyh * nxh == 1:
        return weight
    cols = weight.shape[-1]
    split = weight.reshape(nz, nyh, 2, nxh, 2, rows, cols)
    return split.transpose(0, 1, 3, 2, 4, 5, 6).reshape(-1, cols)


def spread_pack(pieces):
    rows = pieces[0].shape[0]
    blocks = [p.reshape(rows, 4, -1) for p in pieces]
    return jnp.concatenate(blocks, axis=-1).transpose(1, 0, 2)


def body(patches, counts, doc_ids, w_query, w_key, w_value, w_output, w_gate, w_up, w_down, gain_attn, gain_ffn, cotangent):
    core = lax.axis_index(CORE)
    my_row = lax.axis_index(DP)
    peers, slot_cap, width = patches.shape[1:]
    half_width = width // 2
    tok_count = doc_ids.shape[1]
    toks = tok_count // 2
    rows = w_query.shape[0]
    far_sizes = tuple(lax.axis_size(a) for a in FAR)
    score_scale = DH ** (-0.5)
    heads_part = w_query.shape[1] // 4
    ff_part = w_gate.shape[1] // 4
    ff_pad = -(-ff_part // 128) * 128

    gain_a = gain_attn.astype(f32)[:, None]
    gain_f = gain_ffn.astype(f32)[:, None]

    def scaled(weight, gain):
        return (weight.astype(f32) * gain).astype(bf16)

    attn_pack = spread_pack([scaled(w_query, gain_a), scaled(w_key, gain_a), scaled(w_value, gain_a), w_output.T])

    def padded(weight):
        quarter = weight.reshape(rows, 4, ff_part)
        return jnp.pad(quarter, ((0, 0), (0, 0), (0, ff_pad - ff_part))).reshape(rows, -1)

    ffn_pack = spread_pack([padded(scaled(w_gate, gain_f)), padded(scaled(w_up, gain_f)), padded(w_down.T)])

    def exchange(pack):
        moved = lax.all_to_all(pack, NEAR, 0, 0, tiled=True)
        flat = moved.reshape(4 * rows, -1)
        whole = lax.all_gather(flat, FAR, axis=0, tiled=True)
        return natural_rows(whole, far_sizes, rows)

    def half_features(blocks):
        return lax.dynamic_slice_in_dim(blocks, core * half_width, half_width, 2)

    def to_rows(blocks):
        return lax.all_to_all(half_features(blocks[0]), DP, 0, 0, tiled=True).reshape(peers * slot_cap, half_width)

    received = to_rows(patches)
    attn_own = exchange(attn_pack)
    arrived = to_rows(cotangent)
    ffn_own = exchange(ffn_pack)
    attn_oth = swap(attn_own)
    ffn_oth = swap(ffn_own)

    my_counts = lax.dynamic_index_in_dim(counts, my_row, 0, keepdims=False)
    offsets = jnp.cumsum(my_counts) - my_counts
    slots = jnp.arange(slot_cap, dtype=jnp.int32)
    slot_token = jnp.where(slots[None, :] < my_counts[:, None], offsets[:, None] + slots[None, :], -1).reshape(-1)
    token_ids = jnp.arange(tok_count, dtype=jnp.int32)
    place = (token_ids[:, None] == slot_token[None, :]).astype(bf16)

    def join_features(own, other):
        first = jnp.where(core == 0, own, other)
        second = jnp.where(core == 0, other, own)
        return jnp.concatenate([first, second], axis=-1)

    def collect(slots_in):
        mine = mm(place, slots_in).astype(bf16)
        own = lax.dynamic_slice_in_dim(mine, core * toks, toks, 0)
        give = lax.dynamic_slice_in_dim(mine, (1 - core) * toks, toks, 0)
        return join_features(own, swap(give))

    def deliver(values):
        own = lax.dynamic_slice_in_dim(values, core * half_width, half_width, 1)
        give = lax.dynamic_slice_in_dim(values, (1 - core) * half_width, half_width, 1)
        other = swap(give)
        both = jnp.concatenate([jnp.where(core == 0, own, other), jnp.where(core == 0, other, own)], axis=0)
        spread = outer_sum(place, both).astype(bf16).reshape(peers, slot_cap, half_width)
        back = lax.all_to_all(spread, DP, 0, 0, tiled=True)
        return join_features(back, swap(back))[None]

    doc_rows = gather_near(doc_ids)
    doc_own = lax.dynamic_slice_in_dim(doc_rows, core * toks, toks, 1)
    doc_oth = lax.dynamic_slice_in_dim(doc_rows, (1 - core) * toks, toks, 1)
    pos = jnp.arange(toks)
    visible_own = (doc_own[:, :, None] == doc_own[:, None, :]) & (pos[None, :] <= pos[:, None])[None]
    visible_oth = (doc_own[:, :, None] == doc_oth[:, None, :]) & (core == 1)
    visible = jnp.concatenate([visible_own, visible_oth], axis=-1)

    x = collect(received).astype(f32)
    root_attn = inverse_root(x)
    norm_attn = x * root_attn
    norm_a = gather_near(norm_attn.astype(bf16))

    n3 = 3 * heads_part
    qkv_own = mm(norm_a, attn_own[:, :n3]).astype(bf16)
    qkv_oth = mm(norm_a, attn_oth[:, :n3]).astype(bf16)
    kv_own = qkv_own[:, heads_part:]
    kv_oth = qkv_oth[:, heads_part:]
    kv_own_far = swap(kv_oth)
    kv_oth_far = swap(kv_own)

    def heads(own, oth):
        both = jnp.concatenate([own, oth], axis=-1)
        return both.reshape(4, toks, -1, DH)

    hp = heads_part
    q = heads(qkv_own[:, :hp], qkv_oth[:, :hp])
    k = jnp.concatenate([heads(kv_own[:, :hp], kv_oth[:, :hp]), heads(kv_own_far[:, :hp], kv_oth_far[:, :hp])], axis=1)
    v = jnp.concatenate([heads(kv_own[:, hp:], kv_oth[:, hp:]), heads(kv_own_far[:, hp:], kv_oth_far[:, hp:])], axis=1)
    scores = jnp.einsum("rthd,rshd->rhts", q, k, preferred_element_type=f32) * score_scale
    scores = jnp.where(visible[:, None], scores, masked_score)
    lifted = jnp.exp(scores - jnp.max(scores, axis=-1, keepdims=True))
    probs = lifted / jnp.sum(lifted, axis=-1, keepdims=True)
    probs_low = probs.astype(bf16)
    attended = jnp.einsum("rhts,rshd->rthd", probs_low, v, preferred_element_type=f32).astype(bf16)
    attended = attended.reshape(4 * toks, -1)
    att_own, att_oth = attended[:, :hp], attended[:, hp:]
    out_own, out_oth = attn_own[:, n3:], attn_oth[:, n3:]
    branch = mm_t(att_own, out_own) + mm_t(att_oth, out_oth)
    hidden = x + scatter_near(branch.reshape(4, toks, width))

    root_ffn = inverse_root(hidden)
    norm_ffn = hidden * root_ffn
    norm_f = gather_near(norm_ffn.astype(bf16))
    grad_low = collect(arrived)
    grad_y = gather_near(grad_low)

    def ffn_half(weights):
        gate_w, up_w, down_w = (weights[:, i * ff_pad : (i + 1) * ff_pad] for i in range(3))
        gate = mm(norm_f, gate_w)
        up = mm(norm_f, up_w)
        sig = jax.nn.sigmoid(gate)
        silu = gate * sig
        product = (silu * up).astype(bf16)
        grad_product = mm(grad_y, down_w)
        grad_gate = (grad_product * up * sig * (1.0 + gate * (1.0 - sig))).astype(bf16)
        grad_up = (grad_product * silu).astype(bf16)
        branch = mm_t(product, down_w)
        grad_norm = mm_t(grad_gate, gate_w) + mm_t(grad_up, up_w)
        grads = jnp.concatenate(
            [outer_sum(norm_f, grad_gate), outer_sum(norm_f, grad_up), outer_sum(grad_y, product)], axis=-1
        ).astype(bf16)
        return branch, grad_norm, grads

    branch_own, grad_norm_own, ffn_grads_own = ffn_half(ffn_own)
    branch_oth, grad_norm_oth, ffn_grads_oth = ffn_half(ffn_oth)
    scaled_two = scatter_near((grad_norm_own + grad_norm_oth).reshape(4, toks, width))
    grad_hidden = grad_low.astype(f32) + root_ffn * (
        scaled_two - norm_ffn * jnp.mean(scaled_two * norm_ffn, axis=-1, keepdims=True)
    )
    grad_branch = gather_near(grad_hidden.astype(bf16))

    final = hidden + scatter_near((branch_own + branch_oth).reshape(4, toks, width))
    outputs = deliver(final.astype(bf16))

    def reduce_far(own, other):
        total = (own.astype(f32) + swap(other).astype(f32)).astype(bf16)
        part = lax.psum_scatter(far_rows(total, far_sizes, rows), FAR, scatter_dimension=0, tiled=True)
        cols = part.shape[-1]
        return lax.all_to_all(part.reshape(4, rows, cols), NEAR, 0, 0, tiled=True)

    ffn_grads = reduce_far(ffn_grads_own, ffn_grads_oth)

    grad_att_own = mm(grad_branch, out_own).astype(bf16)
    grad_att_oth = mm(grad_branch, out_oth).astype(bf16)
    grad_heads = heads(grad_att_own, grad_att_oth)
    grad_probs = jnp.einsum("rthd,rshd->rhts", grad_heads, v, preferred_element_type=f32)
    grad_v = jnp.einsum("rhts,rthd->rshd", probs_low, grad_heads, preferred_element_type=f32)
    grad_scores = probs * (grad_probs - jnp.sum(grad_probs * probs, axis=-1, keepdims=True))
    scores_low = grad_scores.astype(bf16)
    grad_q = (jnp.einsum("rhts,rshd->rthd", scores_low, k, preferred_element_type=f32) * score_scale).astype(bf16)
    grad_k = jnp.einsum("rhts,rthd->rshd", scores_low, q, preferred_element_type=f32) * score_scale
    grad_q = grad_q.reshape(4 * toks, -1)

    def halves(grad):
        near_part = grad[:, :toks].reshape(4 * toks, -1)
        far_part = grad[:, toks:].reshape(4 * toks, -1)
        return near_part[:, :hp], near_part[:, hp:], far_part[:, :hp], far_part[:, hp:]

    k_own, k_oth, k_own_far, k_oth_far = halves(grad_k)
    v_own, v_oth, v_own_far, v_oth_far = halves(grad_v)
    far_grads = jnp.concatenate([k_oth_far, v_oth_far, k_own_far, v_own_far], axis=-1).astype(bf16)
    back = swap(far_grads).astype(f32)
    gqkv_own = jnp.concatenate(
        [grad_q[:, :hp], (k_own + back[:, :hp]).astype(bf16), (v_own + back[:, hp : 2 * hp]).astype(bf16)], axis=-1
    )
    gqkv_oth = jnp.concatenate(
        [grad_q[:, hp:], (k_oth + back[:, 2 * hp : 3 * hp]).astype(bf16), (v_oth + back[:, 3 * hp :]).astype(bf16)], axis=-1
    )
    grad_norm_a = mm_t(gqkv_own, attn_own[:, :n3]) + mm_t(gqkv_oth, attn_oth[:, :n3])
    scaled_one = scatter_near(grad_norm_a.reshape(4, toks, width))
    grad_input = grad_hidden + root_attn * (
        scaled_one - norm_attn * jnp.mean(scaled_one * norm_attn, axis=-1, keepdims=True)
    )
    input_grad = deliver(grad_input.astype(bf16))

    attn_grads = reduce_far(
        jnp.concatenate([outer_sum(norm_a, gqkv_own), outer_sum(grad_branch, att_own)], axis=-1).astype(bf16),
        jnp.concatenate([outer_sum(norm_a, gqkv_oth), outer_sum(grad_branch, att_oth)], axis=-1).astype(bf16),
    )

    def unpack(blocks, start, size, total):
        piece = blocks[:, :, start : start + size].astype(f32)
        return piece.transpose(1, 0, 2).reshape(rows, total)

    raw_q, raw_k, raw_v, raw_o = (unpack(attn_grads, i * hp, hp, 4 * hp) for i in range(4))
    raw_g, raw_u, raw_d = (unpack(ffn_grads, i * ff_pad, ff_part, 4 * ff_part) for i in range(3))

    def gain_sum(raws, weights):
        return sum(jnp.sum(r * w.astype(f32), axis=1) for r, w in zip(raws, weights))

    gains = jnp.stack([gain_sum([raw_q, raw_k, raw_v], [w_query, w_key, w_value]), gain_sum([raw_g, raw_u], [w_gate, w_up])])
    gains = gains + swap(gains)
    return (
        outputs,
        input_grad,
        raw_q * gain_a,
        raw_k * gain_a,
        raw_v * gain_a,
        raw_o.T,
        raw_g * gain_f,
        raw_u * gain_f,
        raw_d.T,
        gains[0],
        gains[1],
    )


def solution(mesh):
    dp_size = mesh.shape["dp"]
    side = round((dp_size / 2) ** (1 / 3))
    grid = (2 * side, side // 2, 2, side // 2, 2, 2)
    inner = Mesh(np.asarray(mesh.devices).reshape(grid), ("z", "yh", "yl", "xh", "xl", "c"))
    rows_first = P(DP, "c")
    cols_first = P("c", DP)
    blocks = P(DP, None, None, None)
    weights = (rows_first, rows_first, rows_first, cols_first, rows_first, rows_first, cols_first, P(DP), P(DP))
    in_specs = (blocks, P(), P(DP, None)) + weights + (blocks,)
    out_specs = (blocks, blocks) + weights
    return jax.shard_map(body, mesh=inner, in_specs=in_specs, out_specs=out_specs, check_vma=False)
```

```python
import functools

import jax
import jax.numpy as jnp
import numpy as np
from jax import lax
from jax.experimental import pallas as pl
from jax.experimental.pallas import tpu as pltpu
from jax.sharding import Mesh, PartitionSpec as P

DH = 64
eps = 1e-05
masked_score = -1e30
bf16 = jnp.bfloat16
f32 = jnp.float32

DP = ("z", "yh", "yl", "xh", "xl")
FAR = ("z", "yh", "xh")
NEAR = ("yl", "xl")
CORE = "c"


def mm(left, right):
    return lax.dot_general(left, right, (((1,), (0,)), ((), ())), preferred_element_type=f32)


def mm_t(left, right):
    return lax.dot_general(left, right, (((1,), (1,)), ((), ())), preferred_element_type=f32)


def outer_sum(left, right):
    return lax.dot_general(left, right, (((0,), (0,)), ((), ())), preferred_element_type=f32)


def swap(value):
    return lax.ppermute(value, CORE, [(0, 1), (1, 0)])


def near(value, k):
    return lax.ppermute(value, NEAR, [(i, i ^ k) for i in range(4)])


def gather_near(value):
    return [value] + [near(value, k) for k in (1, 2, 3)]


def scatter_near(low):
    return [near(low[k - 1], k) for k in (1, 2, 3)]


def after(value, *tokens):
    return lax.optimization_barrier((value, tokens))[0]


def inverse_root(values):
    return lax.rsqrt(jnp.mean(values * values, axis=-1, keepdims=True) + eps)


def call(kernel, outs, args, scratch=(), limit=4, us=1.0):
    in_specs = [pl.BlockSpec(memory_space=pltpu.SMEM if a.ndim == 1 else pltpu.VMEM) for a in args]
    out_specs = [pl.BlockSpec(memory_space=pltpu.VMEM) for _ in outs]
    return pl.pallas_call(
        kernel,
        out_shape=[jax.ShapeDtypeStruct(shape, kind) for shape, kind in outs],
        in_specs=in_specs,
        out_specs=out_specs,
        scratch_shapes=list(scratch),
        compiler_params=pltpu.CompilerParams(vmem_limit_bytes=limit << 20),
        cost_estimate=pl.CostEstimate(flops=int(us * 1e9), bytes_accessed=int(us * 1e6), transcendentals=0),
    )(*args)


def lane_half(value, half):
    lanes = lax.broadcasted_iota(jnp.int32, value.shape, 1)
    keep = (lanes < DH) if half == 0 else (lanes >= DH)
    return jnp.where(keep, value, jnp.zeros_like(value))


def flipped(value):
    n = value.shape[1]
    eye = (
        lax.broadcasted_iota(jnp.int32, (n, n), 0) == lax.broadcasted_iota(jnp.int32, (n, n), 1)
    ).astype(bf16)
    return mm_t(eye, value).astype(bf16)


def pack_kernel(part, me, gain, *refs):
    n = len(refs) - 5
    weights, outs, blocks = refs[:n], refs[n : n + 4], refs[n + 4]
    size = blocks.shape[2] // n
    if size != part:
        blocks[...] = jnp.zeros(blocks.shape, blocks.dtype)
    for m, ref in enumerate(weights):
        w = ref[...].astype(f32)
        if m < n - 1:
            w = w * gain[...]
        w = w.astype(bf16)
        for i in range(4):
            blocks[i, :, m * size : m * size + part] = w[:, i * part : (i + 1) * part]
    for k, out in enumerate(outs):
        out[...] = blocks[me[0] ^ k]


def place_kernel(me, b0, b1, b2, b3, out):
    for k, ref in enumerate((b0, b1, b2, b3)):
        out[me[0] ^ k] = ref[...]


def place_far_kernel(me, far, b0, b1, b2, b3, out):
    for k, ref in enumerate((b0, b1, b2, b3)):
        plane = lax.rem(far[0] + (4 - k), 4)
        for i in range(4):
            out[plane * 4 + (me[0] ^ i)] = ref[i]


def collect_kernel(core, slot_row, slots, own, give):
    toks = own.shape[0]
    token = lax.broadcasted_iota(jnp.int32, (toks, slots.shape[0]), 0)
    for ref, half in ((own, core[0]), (give, 1 - core[0])):
        place = ((token + half * toks) == slot_row[...]).astype(bf16)
        ref[...] = mm(place, slots[...]).astype(bf16)


def normed(x):
    return x * inverse_root(x)


def enter_kernel(core, own, other, x_ref, y_ref, norm_ref):
    half = own.shape[1] // 2
    first = core[0] == 0
    for ref, at in ((x_ref, slice(0, half)), (y_ref, slice(half, 2 * half))):
        ref[:, :half] = jnp.where(first, own[:, at], other[:, at])
        ref[:, half:] = jnp.where(first, other[:, at], own[:, at])
    norm_ref[...] = normed(x_ref[...].astype(f32)).astype(bf16)


def project_kernel(n0, n1, n2, n3, w, q_ref, kv_ref, all_n):
    toks = n0.shape[0]
    hp = w.shape[2] // 4
    for r, ref in enumerate((n0, n1, n2, n3)):
        all_n[r * toks : (r + 1) * toks, :] = ref[...]
    for j in range(2):
        q_ref[:, j * hp : (j + 1) * hp] = mm(all_n[...], w[j, :, :hp]).astype(bf16)
        kv = mm(all_n[...], w[j, :, hp : 3 * hp]).astype(bf16)
        kv_ref[:, 2 * j * hp : 2 * (j + 1) * hp] = kv


def attend_kernel(scale, core, q_ref, kv, kvf, doc_q, doc_kn, doc_kf, w, p_ref, att_ref, own_ref, b1, b2, b3):
    hp = q_ref.shape[1] // 2
    rows = doc_q.shape[0]
    toks = q_ref.shape[0] // rows
    key_pos = lax.broadcasted_iota(jnp.int32, (toks, toks), 0)
    query_pos = lax.broadcasted_iota(jnp.int32, (toks, toks), 1)
    causal = key_pos <= query_pos
    later = core[0] == 1
    for r in range(rows):
        at = slice(r * toks, (r + 1) * toks)
        dq = doc_q[r : r + 1, :]
        near_ok = causal & (doc_kn[:, r : r + 1] == dq)
        far_ok = (doc_kf[:, r : r + 1] == dq) & later
        for j in range(2):
            base = 2 * j * hp
            q2 = q_ref[at, j * hp : (j + 1) * hp]
            kn, kf = kv[at, base : base + hp], kvf[at, base : base + hp]
            v_t = jnp.concatenate(
                [flipped(kv[at, base + hp : base + 2 * hp]), flipped(kvf[at, base + hp : base + 2 * hp])], axis=1
            )
            pieces = []
            for h in range(2):
                qh = lane_half(q2, h)
                sn = jnp.where(near_ok, mm_t(kn, qh) * scale, masked_score)
                sf = jnp.where(far_ok, mm_t(kf, qh) * scale, masked_score)
                top = jnp.maximum(jnp.max(sn, axis=0, keepdims=True), jnp.max(sf, axis=0, keepdims=True))
                en, ef = jnp.exp(sn - top), jnp.exp(sf - top)
                total = jnp.sum(en, axis=0, keepdims=True) + jnp.sum(ef, axis=0, keepdims=True)
                inv = 1.0 / total
                p = (jnp.concatenate([en, ef], axis=0) * inv).astype(bf16)
                p_ref[(r * 2 + j) * 2 + h] = p
                pieces.append(mm(v_t[h * DH : (h + 1) * DH, :], p))
            att_ref[at, j * hp : (j + 1) * hp] = flipped(jnp.concatenate(pieces, axis=0).astype(bf16)).astype(bf16)
        out = mm_t(att_ref[at, :hp], w[0, :, 3 * hp :]) + mm_t(att_ref[at, hp:], w[1, :, 3 * hp :])
        if r == 0:
            own_ref[...] = out
        else:
            (b1, b2, b3)[r - 1][...] = out.astype(bf16)


def attend_back_kernel(scale, g0, g1, g2, g3, w, q_ref, kv, kvf, p_ref, dq_ref, near_ref, far_ref, all_g, ga_ref):
    hp = q_ref.shape[1] // 2
    toks = g0.shape[0]
    for r, g_ref in enumerate((g0, g1, g2, g3)):
        at = slice(r * toks, (r + 1) * toks)
        all_g[at, :] = g_ref[...]
        for j in range(2):
            ga_ref[...] = mm(g_ref[...], w[j, :, 3 * hp :]).astype(bf16)
            g = ga_ref[...]
            base = 2 * j * hp
            q2 = q_ref[at, j * hp : (j + 1) * hp]
            v = jnp.concatenate([kv[at, base + hp : base + 2 * hp], kvf[at, base + hp : base + 2 * hp]], axis=0)
            k_t = jnp.concatenate([flipped(kv[at, base : base + hp]), flipped(kvf[at, base : base + hp])], axis=1)
            dqs, ps, dss, gs, qs = [], [], [], [], []
            for h in range(2):
                gh = lane_half(g, h)
                dp = mm_t(v, gh)
                p_low = p_ref[(r * 2 + j) * 2 + h]
                p = p_low.astype(f32)
                ds = p * (dp - jnp.sum(dp * p, axis=0, keepdims=True))
                ds = ds.astype(bf16)
                dqs.append(mm(k_t[h * DH : (h + 1) * DH, :], ds))
                ps.append(p_low)
                dss.append(ds)
                gs.append(gh)
                qs.append(lane_half(q2, h))
            dq = (jnp.concatenate(dqs, axis=0) * scale).astype(bf16)
            dq_ref[at, j * hp : (j + 1) * hp] = flipped(dq)
            dv = mm(jnp.concatenate(ps, axis=1), jnp.concatenate(gs, axis=0))
            dk = mm(jnp.concatenate(dss, axis=1), jnp.concatenate(qs, axis=0)) * scale
            near_ref[at, base : base + hp] = dk[:toks]
            near_ref[at, base + hp : base + 2 * hp] = dv[:toks]
            far_ref[at, base : base + hp] = dk[toks:].astype(bf16)
            far_ref[at, base + hp : base + 2 * hp] = dv[toks:].astype(bf16)


def project_back_kernel(dq, near_g, back, w, gown, goth, own_ref, b1, b2, b3, acc):
    hp = dq.shape[1] // 2
    toks = own_ref.shape[0]
    for j, g in enumerate((gown, goth)):
        g[:, :hp] = dq[:, j * hp : (j + 1) * hp]
        both = slice(2 * j * hp, 2 * (j + 1) * hp)
        g[:, hp:] = (near_g[:, both] + back[:, both].astype(f32)).astype(bf16)
    acc[...] = mm_t(gown[...], w[0, :, : 3 * hp]) + mm_t(goth[...], w[1, :, : 3 * hp])
    own_ref[...] = acc[:toks]
    for r, ref in enumerate((b1, b2, b3)):
        ref[...] = acc[(r + 1) * toks : (r + 2) * toks].astype(bf16)


def total_of(refs):
    total = refs[0][...]
    for ref in refs[1:]:
        total = total + ref[...].astype(f32)
    return total


def middle_kernel(x, b0, b1, b2, b3, hidden, norm_ref):
    value = x[...].astype(f32) + total_of((b0, b1, b2, b3))
    hidden[...] = value
    norm_ref[...] = normed(value).astype(bf16)


def ffn_kernel(n0, n1, n2, n3, y0, y1, y2, y3, w, mid, own_ref, b1, b2, b3, all_n, all_y, acc):
    toks = n0.shape[0]
    ff = w.shape[2] // 3
    for r in range(4):
        all_n[r * toks : (r + 1) * toks, :] = (n0, n1, n2, n3)[r][...]
        all_y[r * toks : (r + 1) * toks, :] = (y0, y1, y2, y3)[r][...]
    for j in range(2):
        gate = mm(all_n[...], w[j, :, :ff])
        up = mm(all_n[...], w[j, :, ff : 2 * ff])
        sig = jax.nn.sigmoid(gate)
        silu = gate * sig
        mid[j, :, 2 * ff :] = (silu * up).astype(bf16)
        grad_product = mm(all_y[...], w[j, :, 2 * ff :])
        mid[j, :, :ff] = (grad_product * up * sig * (1.0 + gate * (1.0 - sig))).astype(bf16)
        mid[j, :, ff : 2 * ff] = (grad_product * silu).astype(bf16)
        part = mm_t(mid[j, :, : 2 * ff], w[j, :, : 2 * ff])
        if j == 0:
            acc[...] = part
        else:
            acc[...] += part
    own_ref[...] = acc[:toks]
    for r, ref in enumerate((b1, b2, b3)):
        ref[...] = acc[(r + 1) * toks : (r + 2) * toks].astype(bf16)


def ffn_out_kernel(mid, w, own_ref, b1, b2, b3, acc):
    toks = own_ref.shape[0]
    ff = w.shape[2] // 3
    acc[...] = mm_t(mid[0, :, 2 * ff :], w[0, :, 2 * ff :]) + mm_t(mid[1, :, 2 * ff :], w[1, :, 2 * ff :])
    own_ref[...] = acc[:toks]
    for r, ref in enumerate((b1, b2, b3)):
        ref[...] = acc[(r + 1) * toks : (r + 2) * toks].astype(bf16)


def ffn_grads_kernel(all_n, all_y, mid, out):
    rows = out.shape[2]
    ff = out.shape[3] // 3
    for i in range(4):
        at = slice(i * rows, (i + 1) * rows)
        for j in range(2):
            out[i, j, :, : 2 * ff] = outer_sum(all_n[:, at], mid[j, :, : 2 * ff]).astype(bf16)
            out[i, j, :, 2 * ff :] = outer_sum(all_y[:, at], mid[j, :, 2 * ff :]).astype(bf16)


def split_halves(core, value, own, give):
    half = own.shape[1]
    first = core[0] == 0
    own[...] = jnp.where(first, value[:, :half], value[:, half:])
    give[...] = jnp.where(first, value[:, half:], value[:, :half])


def final_kernel(core, hidden, b0, b1, b2, b3, own, give):
    split_halves(core, (hidden[...] + total_of((b0, b1, b2, b3))).astype(bf16), own, give)


def norm_back(x, grad):
    root = inverse_root(x)
    norm = x * root
    return root * (grad - norm * jnp.mean(grad * norm, axis=-1, keepdims=True))


def middle_back_kernel(hidden, grad_low, b0, b1, b2, b3, out, low):
    grad = grad_low[...].astype(f32) + norm_back(hidden[...], total_of((b0, b1, b2, b3)))
    out[...] = grad
    low[...] = grad.astype(bf16)


def leave_kernel(core, x, grad_hidden, b0, b1, b2, b3, out_own, out_give, own, give):
    half = out_own.shape[1]
    own[:, :half] = out_own[...]
    give[:, :half] = out_give[...]
    grad = grad_hidden[...] + norm_back(x[...].astype(f32), total_of((b0, b1, b2, b3)))
    split_halves(core, grad.astype(bf16), own.at[:, half:], give.at[:, half:])


def spread_kernel(core, slot_col, own, other, out):
    toks = own.shape[0]
    first = core[0] == 0
    token = lax.broadcasted_iota(jnp.int32, (slot_col.shape[0], toks), 1)
    low = (token == slot_col[...]).astype(bf16)
    high = ((token + toks) == slot_col[...]).astype(bf16)
    own, other = own[...], other[...]
    out[...] = (mm(low, jnp.where(first, own, other)) + mm(high, jnp.where(first, other, own))).astype(bf16)


def join_kernel(core, own, other, out, grad):
    half = own.shape[1] // 2
    first = core[0] == 0
    for ref, at in ((out, slice(0, half)), (grad, slice(half, 2 * half))):
        ref[:, :half] = jnp.where(first, own[:, at], other[:, at])
        ref[:, half:] = jnp.where(first, other[:, at], own[:, at])


def attn_grads_kernel(core, all_n, all_g, g0, g1, att, own, oth):
    hp = att.shape[1] // 2
    first = core[0] == 0
    for j, out in enumerate((own, oth)):
        mine = first if j == 0 else core[0] == 1
        out[:, : 3 * hp] = outer_sum(all_n[...], jnp.where(mine, g0[...], g1[...])).astype(bf16)
        out[:, 3 * hp :] = outer_sum(all_g[...], jnp.where(mine, att[:, :hp], att[:, hp:])).astype(bf16)


def core_sum_kernel(far, own, other, t0, t1, t2, t3):
    rows = t0.shape[0]
    for k, ref in enumerate((t0, t1, t2, t3)):
        at = pl.ds(pl.multiple_of(lax.rem(far[0] + k, 4) * rows, rows), rows)
        ref[...] = (own[at, :].astype(f32) + other[at, :].astype(f32)).astype(bf16)


def far_sum_kernel(me, t0, t1, t2, t3, s0, s1, s2, s3):
    rows = s0.shape[0]
    for k, ref in enumerate((s0, s1, s2, s3)):
        at = pl.ds(pl.multiple_of((me[0] ^ k) * rows, rows), rows)
        total = t0[at, :].astype(f32)
        for other in (t1, t2, t3):
            total = total + other[at, :].astype(f32)
        ref[...] = total.astype(bf16)


def pick_kernel(me, part, s0, s1, s2, s3):
    rows = s0.shape[0]
    for k, ref in enumerate((s0, s1, s2, s3)):
        ref[...] = part[pl.ds(pl.multiple_of((me[0] ^ k) * rows, rows), rows), :]


def unpack_kernel(part, me, gain, s0, s1, s2, s3, *refs):
    n = (len(refs) - 1) // 2
    weights, outs, gain_sum, blocks = refs[: n - 1], refs[n - 1 : 2 * n - 1], refs[2 * n - 1], refs[2 * n]
    for k, ref in enumerate((s0, s1, s2, s3)):
        blocks[me[0] ^ k] = ref[...]
    size = blocks.shape[2] // n
    total = jnp.zeros(gain_sum.shape, f32)
    for m, out in enumerate(outs):
        for i in range(4):
            raw = blocks[i, :, m * size : m * size + part].astype(f32)
            at = slice(i * part, (i + 1) * part)
            if m < n - 1:
                total = total + jnp.sum(raw * weights[m][:, at].astype(f32), axis=1, keepdims=True)
                raw = raw * gain[...]
            out[:, at] = raw
    gain_sum[...] = total


def natural_rows(weight, far_sizes, rows):
    nz, nyh, nxh = far_sizes
    if nyh * nxh == 1:
        return weight
    cols = weight.shape[-1]
    split = weight.reshape(nz, nyh, nxh, 2, 2, rows, cols)
    return split.transpose(0, 1, 3, 2, 4, 5, 6).reshape(-1, cols)


def far_rows(weight, far_sizes, rows):
    nz, nyh, nxh = far_sizes
    if nyh * nxh == 1:
        return weight
    cols = weight.shape[-1]
    split = weight.reshape(nz, nyh, 2, nxh, 2, rows, cols)
    return split.transpose(0, 1, 3, 2, 4, 5, 6).reshape(-1, cols)


def spread_pack(pieces):
    rows = pieces[0].shape[0]
    blocks = [p.reshape(rows, 4, -1) for p in pieces]
    return jnp.concatenate(blocks, axis=-1).transpose(1, 0, 2)


def near_exchange(blocks, my_near):
    got = jnp.zeros(blocks.shape, blocks.dtype)
    for k in range(4):
        give = lax.dynamic_index_in_dim(blocks, my_near ^ k, 0, keepdims=True)
        got = lax.dynamic_update_slice_in_dim(got, near(give, k) if k else give, my_near ^ k, 0)
    return got


def body(patches, counts, doc_ids, w_query, w_key, w_value, w_output, w_gate, w_up, w_down, gain_attn, gain_ffn, cotangent):
    core = lax.axis_index(CORE)
    my_row = lax.axis_index(DP)
    my_near = lax.axis_index(NEAR)
    my_far = lax.axis_index(FAR)
    core_ref, near_ref, far_ref = core.reshape(1), my_near.reshape(1), my_far.reshape(1)
    peers, slot_cap, width = patches.shape[1:]
    half_width = width // 2
    slot_count = peers * slot_cap
    tok_count = doc_ids.shape[1]
    toks = tok_count // 2
    group = 4 * toks
    rows = w_query.shape[0]
    far_sizes = tuple(lax.axis_size(a) for a in FAR)
    far = far_sizes[0] * far_sizes[1] * far_sizes[2]
    direct = far == 4 and rows % 16 == 0
    score_scale = DH ** (-0.5)
    hp = w_query.shape[1] // 4
    ff_part = w_gate.shape[1] // 4
    ff_pad = -(-ff_part // 128) * 128
    gain_a = gain_attn.astype(f32)[:, None]
    gain_f = gain_ffn.astype(f32)[:, None]

    def far_shift(value, k):
        return lax.ppermute(value, FAR, [(i, (i + k) % far) for i in range(far)])

    def half_features(blocks):
        return lax.dynamic_slice_in_dim(blocks[0], core * half_width, half_width, 2)

    both = jnp.concatenate([half_features(patches), half_features(cotangent)], axis=-1)
    received = lax.all_to_all(both, DP, 0, 0, tiled=True).reshape(slot_count, width)

    def packed(weights, gain, part, size, token):
        weights = after(weights, token)
        if direct:
            return call(
                functools.partial(pack_kernel, part),
                [((rows, size * len(weights)), bf16)] * 4,
                [near_ref, gain, *weights],
                [pltpu.VMEM((4, rows, size * len(weights)), bf16)],
            )
        scaled = [(w.astype(f32) * gain).astype(bf16) for w in weights[:-1]] + [weights[-1]]
        return [jnp.pad(w.reshape(rows, 4, part), ((0, 0), (0, 0), (0, size - part))).reshape(rows, -1) for w in scaled]

    attn_weights = [w_query, w_key, w_value, w_output.T]
    ffn_weights = [w_gate, w_up, w_down.T]
    def gathered(pack, *tokens):
        if direct:
            got = scatter_near(pack[1:])
            (flat,) = call(place_kernel, [((4,) + pack[0].shape, bf16)], [near_ref, pack[0], *got])
        else:
            flat = near_exchange(spread_pack(pack), my_near)
        cols = flat.shape[-1]
        flat = flat.reshape(4 * rows, cols)
        return flat, lambda operand: lax.all_gather(operand, (CORE,) + FAR, axis=0, tiled=True).reshape(2, width, cols)

    attn_flat, gather_attn = gathered(packed(attn_weights, gain_a, hp, hp, both))
    attn_w = gather_attn(attn_flat)
    ffn_flat, gather_ffn = gathered(packed(ffn_weights, gain_f, ff_part, ff_pad, attn_flat))
    doc_rows = jnp.concatenate(gather_near(after(doc_ids, attn_flat)), axis=0)
    my_counts = lax.dynamic_index_in_dim(counts, my_row, 0, keepdims=False)
    offsets = jnp.cumsum(my_counts) - my_counts
    slots = jnp.arange(slot_cap, dtype=jnp.int32)
    slot_token = jnp.where(slots[None, :] < my_counts[:, None], offsets[:, None] + slots[None, :], -1).reshape(-1)
    slot_row, slot_col = slot_token[None, :], slot_token[:, None]
    received, slot_row, slot_col, doc_rows, ffn_flat = lax.optimization_barrier(
        (received, slot_row, slot_col, doc_rows, ffn_flat)
    )
    ffn_w = gather_ffn(ffn_flat)
    if not direct:
        attn_w, ffn_w = (jnp.stack([natural_rows(w[i], far_sizes, rows) for i in range(2)]) for w in (attn_w, ffn_w))
    doc_own = lax.dynamic_slice_in_dim(doc_rows, core * toks, toks, 1)
    doc_oth = lax.dynamic_slice_in_dim(doc_rows, (1 - core) * toks, toks, 1)

    docs = (doc_own, doc_own.T, doc_oth.T)
    slab = ((toks, width), f32), ((toks, width), bf16), ((toks, width), bf16), ((toks, width), bf16)
    token_low = ((toks, width), bf16)
    half_low = ((toks, half_width), bf16)
    whole = ((group, width), bf16)
    acc = pltpu.VMEM((group, width), f32)

    own, give = call(collect_kernel, [token_low, token_low], [core_ref, slot_row, received])
    x, grad_low, norm = call(enter_kernel, [token_low] * 3, [core_ref, own, swap(give)])
    norm_a = gather_near(norm)
    grad_y = gather_near(grad_low)
    q, kv, norm_a_all = call(
        project_kernel,
        [((group, 2 * hp), bf16), ((group, 4 * hp), bf16), whole],
        [after(norm, docs, ffn_flat), *norm_a[1:], attn_w],
        us=2,
    )
    kv_far = swap(kv)
    probs, attended, *branch = call(
        functools.partial(attend_kernel, score_scale),
        [((4 * 2 * hp // DH, 2 * toks, toks), bf16), ((group, 2 * hp), bf16), *slab],
        [core_ref, q, kv, kv_far, *docs, attn_w],
        us=6,
    )
    branch = after(branch, grad_y)
    hidden, norm = call(middle_kernel, [slab[0], token_low], [x, branch[0], *scatter_near(branch[1:])])
    norm_f = gather_near(norm)
    mid, grad_norm, *grad_norm_low, norm_f_all, grad_y_all = call(
        ffn_kernel, [((2, group, 3 * ff_pad), bf16), *slab, whole, whole], [*norm_f, *grad_y, ffn_w], [acc], 12, 7
    )
    branch = call(ffn_out_kernel, slab, [mid, ffn_w], [acc], us=2)
    (ffn_grads,) = call(
        ffn_grads_kernel, [((4, 2, width // 4, 3 * ff_pad), bf16)], [norm_f_all, grad_y_all, mid], (), 12, 4
    )
    grad_hidden, grad_hidden_low = call(
        middle_back_kernel, [slab[0], token_low], [hidden, grad_low, grad_norm, *scatter_near(grad_norm_low)]
    )
    grad_branch = gather_near(grad_hidden_low)
    final_parts = scatter_near(after(branch[1:], grad_hidden_low))

    if direct:
        ffn_part = lax.psum_scatter(ffn_grads.reshape(-1, 3 * ff_pad), FAR + (CORE,), scatter_dimension=0, tiled=True)
    else:
        ordered = jnp.moveaxis(ffn_grads, 1, 0).reshape(2, width, 3 * ff_pad)
        ordered = jnp.stack([far_rows(ordered[i], far_sizes, rows).reshape(far, -1, 3 * ff_pad) for i in range(2)], axis=1)
        ffn_part = lax.psum_scatter(ordered.reshape(-1, 3 * ff_pad), FAR + (CORE,), scatter_dimension=0, tiled=True)

    grad_q, grad_kv, far_give, grad_branch_all = call(
        functools.partial(attend_back_kernel, score_scale),
        [((group, 2 * hp), bf16), ((group, 4 * hp), f32), ((group, 4 * hp), bf16), whole],
        [*grad_branch, attn_w, q, kv, kv_far, probs],
        [pltpu.VMEM((toks, hp), bf16)],
        us=7,
    )
    out_own, out_give = call(final_kernel, [half_low, half_low], [core_ref, hidden, branch[0], *final_parts])
    gqkv_own, gqkv_oth, *grad_norm = call(
        project_back_kernel,
        [((group, 3 * hp), bf16), ((group, 3 * hp), bf16), *slab],
        [grad_q, grad_kv, swap(after(far_give, out_own)), attn_w],
        [acc],
        us=2,
    )
    arriving = scatter_near(grad_norm[1:])
    grads_own, grads_oth = call(
        attn_grads_kernel,
        [((width, 4 * hp), bf16)] * 2,
        [core_ref, norm_a_all, grad_branch_all, gqkv_own, gqkv_oth, attended],
        us=3,
    )
    other = swap(grads_oth)
    own, give = call(
        leave_kernel, [token_low, token_low], [core_ref, x, grad_hidden, grad_norm[0], *arriving, out_own, out_give]
    )

    def finished(pieces, weights, gain, part, size):
        n = len(weights)
        return call(
            functools.partial(unpack_kernel, part),
            [((rows, 4 * part), f32)] * n + [((rows, 1), f32)],
            [near_ref, gain, *pieces, *weights[:-1]],
            [pltpu.VMEM((4, rows, n * size), bf16)],
        )

    def finished_plain(blocks, weights, gain, part, size):
        blocks = near_exchange(blocks.reshape(4, rows, -1), my_near)
        raws = []
        for m in range(len(weights)):
            piece = blocks[:, :, m * size : m * size + part].astype(f32)
            raws.append(piece.transpose(1, 0, 2).reshape(rows, 4 * part))
        total = sum(jnp.sum(r * w.astype(f32), axis=1, keepdims=True) for r, w in zip(raws[:-1], weights[:-1]))
        return [r * gain for r in raws[:-1]] + [raws[-1], total]

    def returned(own, *tokens):
        (spread,) = call(spread_kernel, [((slot_count, width), bf16)], [core_ref, slot_col, after(own, tokens), swap(give)])
        back = lax.all_to_all(spread.reshape(peers, slot_cap, width), DP, 0, 0, tiled=True)
        return back.reshape(slot_count, width)

    if direct:
        planes = call(core_sum_kernel, [((4 * rows, 4 * hp), bf16)] * 4, [far_ref, grads_own, other])
        back = returned(own, planes)
        planes = [planes[0]] + [far_shift(planes[k], k) for k in range(1, 4)]
        pieces = call(far_sum_kernel, [((rows, 4 * hp), bf16)] * 4, [near_ref, *planes])
        pieces = [pieces[0]] + scatter_near(pieces[1:])
        *attn_grads, sum_a = finished(pieces, attn_weights, gain_a, hp, hp)
        pieces = call(pick_kernel, [((rows, 3 * ff_pad), bf16)] * 4, [near_ref, ffn_part])
        pieces = [pieces[0]] + scatter_near(pieces[1:])
        *ffn_grads, sum_f = finished(pieces, ffn_weights, gain_f, ff_part, ff_pad)
        back = after(back, ffn_grads, attn_grads)
    else:
        back = returned(own)
        total = far_rows((grads_own.astype(f32) + other.astype(f32)).astype(bf16), far_sizes, rows)
        attn_part = lax.psum_scatter(total, FAR, scatter_dimension=0, tiled=True)
        *attn_grads, sum_a = finished_plain(attn_part, attn_weights, gain_a, hp, hp)
        *ffn_grads, sum_f = finished_plain(ffn_part, ffn_weights, gain_f, ff_part, ff_pad)
    gains = jnp.concatenate([sum_a, sum_f], axis=1).T
    gains = gains + swap(gains)
    outputs, input_grad = call(join_kernel, [((slot_count, width), bf16)] * 2, [core_ref, back, swap(back)])
    grad_q, grad_k, grad_v, grad_o = attn_grads
    grad_g, grad_u, grad_d = ffn_grads
    return (
        outputs.reshape(patches.shape),
        input_grad.reshape(patches.shape),
        grad_q,
        grad_k,
        grad_v,
        grad_o.T,
        grad_g,
        grad_u,
        grad_d.T,
        gains[0],
        gains[1],
    )


def solution(mesh):
    dp_size = mesh.shape["dp"]
    side = round((dp_size / 2) ** (1 / 3))
    grid = (2 * side, side // 2, 2, side // 2, 2, 2)
    inner = Mesh(np.asarray(mesh.devices).reshape(grid), ("z", "yh", "yl", "xh", "xl", "c"))
    rows_first = P(DP, "c")
    cols_first = P("c", DP)
    blocks = P(DP, None, None, None)
    weights = (rows_first, rows_first, rows_first, cols_first, rows_first, rows_first, cols_first, P(DP), P(DP))
    in_specs = (blocks, P(), P(DP, None)) + weights + (blocks,)
    out_specs = (blocks, blocks) + weights
    return jax.shard_map(body, mesh=inner, in_specs=in_specs, out_specs=out_specs, check_vma=False)
```

```python
import functools

import jax
import jax.numpy as jnp
import numpy as np
from jax import lax
from jax.experimental import pallas as pl
from jax.experimental.pallas import tpu as pltpu
from jax.sharding import Mesh, PartitionSpec as P

DH = 64
eps = 1e-05
masked_score = -1e30
bf16 = jnp.bfloat16
f32 = jnp.float32

DP = ("z", "yh", "yl", "xh", "xl")
FAR = ("z", "yh", "xh")
NEAR = ("yl", "xl")
CORE = "c"


def mm(left, right):
    return lax.dot_general(left, right, (((1,), (0,)), ((), ())), preferred_element_type=f32)


def mm_t(left, right):
    return lax.dot_general(left, right, (((1,), (1,)), ((), ())), preferred_element_type=f32)


def outer_sum(left, right):
    return lax.dot_general(left, right, (((0,), (0,)), ((), ())), preferred_element_type=f32)


def swap(value):
    return lax.ppermute(value, CORE, [(0, 1), (1, 0)])


def near(value, k):
    return lax.ppermute(value, NEAR, [(i, i ^ k) for i in range(4)])


def gather_near(value):
    return [value] + [near(value, k) for k in (1, 2, 3)]


def scatter_near(low):
    return [near(low[k - 1], k) for k in (1, 2, 3)]


def after(value, *tokens):
    return lax.optimization_barrier((value, tokens))[0]


def inverse_root(values):
    return lax.rsqrt(jnp.mean(values * values, axis=-1, keepdims=True) + eps)


def call(kernel, outs, args, scratch=(), limit=4, us=1.0, far_args=(), far_outs=()):
    def space(i, ndim, left):
        if i in left:
            return pl.BlockSpec(memory_space=pltpu.HBM)
        return pl.BlockSpec(memory_space=pltpu.SMEM if ndim == 1 else pltpu.VMEM)

    args = [pltpu.with_memory_space_constraint(a, pltpu.HBM) if i in far_args else a for i, a in enumerate(args)]
    return pl.pallas_call(
        kernel,
        out_shape=[
            pltpu.HBM(shape, kind) if i in far_outs else jax.ShapeDtypeStruct(shape, kind)
            for i, (shape, kind) in enumerate(outs)
        ],
        in_specs=[space(i, a.ndim, far_args) for i, a in enumerate(args)],
        out_specs=[space(i, 2, far_outs) for i in range(len(outs))],
        scratch_shapes=list(scratch),
        compiler_params=pltpu.CompilerParams(vmem_limit_bytes=limit << 20),
        cost_estimate=pl.CostEstimate(flops=int(us * 1e9), bytes_accessed=int(us * 1e6), transcendentals=0),
    )(*args)


def bring(pairs, sems, first=0):
    copies = [pltpu.make_async_copy(a, b, sems.at[first + i]) for i, (a, b) in enumerate(pairs)]
    for copy in copies:
        copy.start()
    return copies


def wait(copies):
    for copy in copies:
        copy.wait()


def stacked(refs, whole, first=0):
    rows = refs[0].shape[0]
    return [(ref, whole.at[pl.ds((first + r) * rows, rows)]) for r, ref in enumerate(refs)]


def lane_half(value, half):
    lanes = lax.broadcasted_iota(jnp.int32, value.shape, 1)
    keep = (lanes < DH) if half == 0 else (lanes >= DH)
    return jnp.where(keep, value, jnp.zeros_like(value))


def flipped(value):
    n = value.shape[1]
    eye = (
        lax.broadcasted_iota(jnp.int32, (n, n), 0) == lax.broadcasted_iota(jnp.int32, (n, n), 1)
    ).astype(bf16)
    return mm_t(eye, value).astype(bf16)


def fetch_kernel(*refs):
    n = (len(refs) - 1) // 2
    wait(bring(list(zip(refs[:n], refs[n : 2 * n])), refs[2 * n]))


def fetch(arrays, us=1.0):
    outs = [(a.shape, a.dtype) for a in arrays]
    return call(fetch_kernel, outs, arrays, [pltpu.SemaphoreType.DMA((len(arrays),))], 2, us, range(len(arrays)))


def pack_kernel(part, me, gain, *refs):
    n = len(refs) - 5
    weights, outs, blocks = refs[:n], refs[n : n + 4], refs[n + 4]
    size = blocks.shape[2] // n
    if size != part:
        blocks[...] = jnp.zeros(blocks.shape, blocks.dtype)
    for m, ref in enumerate(weights):
        w = ref[...].astype(f32)
        if m < n - 1:
            w = w * gain[...]
        w = w.astype(bf16)
        for i in range(4):
            blocks[i, :, m * size : m * size + part] = w[:, i * part : (i + 1) * part]
    for k, out in enumerate(outs):
        out[...] = blocks[me[0] ^ k]


def place_kernel(me, b0, b1, b2, b3, out):
    for k, ref in enumerate((b0, b1, b2, b3)):
        out[me[0] ^ k] = ref[...]


def place_far_kernel(me, far, b0, b1, b2, b3, out):
    for k, ref in enumerate((b0, b1, b2, b3)):
        plane = lax.rem(far[0] + (4 - k), 4)
        for i in range(4):
            out[plane * 4 + (me[0] ^ i)] = ref[i]


def collect_kernel(core, slot_row, slots, own, give):
    toks = own.shape[0]
    token = lax.broadcasted_iota(jnp.int32, (toks, slots.shape[0]), 0)
    for ref, half in ((own, core[0]), (give, 1 - core[0])):
        place = ((token + half * toks) == slot_row[...]).astype(bf16)
        ref[...] = mm(place, slots[...]).astype(bf16)


def normed(x):
    return x * inverse_root(x)


def enter_kernel(core, own, other, x_ref, y_ref, norm_ref, x_far, sems):
    half = own.shape[1] // 2
    first = core[0] == 0
    for ref, at in ((x_ref, slice(0, half)), (y_ref, slice(half, 2 * half))):
        ref[:, :half] = jnp.where(first, own[:, at], other[:, at])
        ref[:, half:] = jnp.where(first, other[:, at], own[:, at])
    kept = bring([(x_ref, x_far)], sems)
    norm_ref[...] = normed(x_ref[...].astype(f32)).astype(bf16)
    wait(kept)


def project_kernel(n0, n1, n2, n3, w, q_ref, kv_ref, n_far, all_n, sems):
    hp = w.shape[2] // 4
    toks = n0.shape[0]
    blocks = bring(stacked((n1, n2, n3), all_n, 1), sems)
    all_n[:toks, :] = n0[...]
    wait(blocks)
    kept = bring([(all_n, n_far)], sems, 3)
    for j in range(2):
        out = mm(all_n[...], w[j, :, : 3 * hp])
        q_ref[:, j * hp : (j + 1) * hp] = out[:, :hp].astype(bf16)
        kv_ref[:, 2 * j * hp : 2 * (j + 1) * hp] = out[:, hp:].astype(bf16)
    wait(kept)


def attend_kernel(scale, core, q_ref, kv, kvf, doc_q, doc_kn, doc_kf, w_far, p_far, q_far, kv_far, kvf_far, att_far, own_ref, b1, b2, b3, p_ref, att_ref, w, sems, p_sems):
    hp = q_ref.shape[1] // 2
    weights = bring([(w_far.at[j, :, pl.ds(3 * hp, hp)], w.at[j]) for j in range(2)], sems)
    kept = bring([(q_ref, q_far), (kv, kv_far), (kvf, kvf_far)], sems, 2)
    rows = doc_q.shape[0]
    toks = q_ref.shape[0] // rows
    key_pos = lax.broadcasted_iota(jnp.int32, (toks, toks), 0)
    query_pos = lax.broadcasted_iota(jnp.int32, (toks, toks), 1)
    causal = key_pos <= query_pos
    later = core[0] == 1
    for r in range(rows):
        at = slice(r * toks, (r + 1) * toks)
        dq = doc_q[r : r + 1, :]
        near_ok = causal & (doc_kn[:, r : r + 1] == dq)
        far_ok = (doc_kf[:, r : r + 1] == dq) & later
        for j in range(2):
            base = 2 * j * hp
            q2 = q_ref[at, j * hp : (j + 1) * hp]
            kn, kf = kv[at, base : base + hp], kvf[at, base : base + hp]
            v_t = jnp.concatenate(
                [flipped(kv[at, base + hp : base + 2 * hp]), flipped(kvf[at, base + hp : base + 2 * hp])], axis=1
            )
            pieces = []
            for h in range(2):
                qh = lane_half(q2, h)
                sn = jnp.where(near_ok, mm_t(kn, qh) * scale, masked_score)
                sf = jnp.where(far_ok, mm_t(kf, qh) * scale, masked_score)
                top = jnp.maximum(jnp.max(sn, axis=0, keepdims=True), jnp.max(sf, axis=0, keepdims=True))
                en, ef = jnp.exp(sn - top), jnp.exp(sf - top)
                total = jnp.sum(en, axis=0, keepdims=True) + jnp.sum(ef, axis=0, keepdims=True)
                inv = 1.0 / total
                p = (jnp.concatenate([en, ef], axis=0) * inv).astype(bf16)
                at_head = (r * 2 + j) * 2 + h
                p_ref[at_head] = p
                kept += bring([(p_ref.at[at_head], p_far.at[at_head])], p_sems, at_head)
                pieces.append(mm(v_t[h * DH : (h + 1) * DH, :], p))
            att_ref[at, j * hp : (j + 1) * hp] = flipped(jnp.concatenate(pieces, axis=0).astype(bf16)).astype(bf16)
        if r == 0:
            wait(weights)
        out = mm_t(att_ref[at, :hp], w[0]) + mm_t(att_ref[at, hp:], w[1])
        if r == 0:
            own_ref[...] = out
        else:
            (b1, b2, b3)[r - 1][...] = out.astype(bf16)
    wait(kept + bring([(att_ref, att_far)], sems, 5))


def attend_back_kernel(scale, g0, g1, g2, g3, w_out, q_ref, kv, kvf, p_ref, hidden_ref, w_far, dq_ref, near_ref, far_ref, w, g_far, hidden_far, all_g, ga_ref, sems):
    hp = q_ref.shape[1] // 2
    toks = g0.shape[0]
    out = bring([(w_far.at[j, :, pl.ds(0, 3 * hp)], w.at[j]) for j in range(2)] + [(hidden_ref, hidden_far)], sems)
    for r, ref in enumerate((g0, g1, g2, g3)):
        all_g[r * toks : (r + 1) * toks, :] = ref[...]
    out += bring([(all_g, g_far)], sems, 3)
    for j in range(2):
        ga_ref[:, j * hp : (j + 1) * hp] = mm(all_g[...], w_out[j]).astype(bf16)
    for r in range(4):
        at = slice(r * toks, (r + 1) * toks)
        for j in range(2):
            g = ga_ref[at, j * hp : (j + 1) * hp]
            base = 2 * j * hp
            q2 = q_ref[at, j * hp : (j + 1) * hp]
            v = jnp.concatenate([kv[at, base + hp : base + 2 * hp], kvf[at, base + hp : base + 2 * hp]], axis=0)
            k_t = jnp.concatenate([flipped(kv[at, base : base + hp]), flipped(kvf[at, base : base + hp])], axis=1)
            dqs, ps, dss, gs, qs = [], [], [], [], []
            for h in range(2):
                gh = lane_half(g, h)
                dp = mm_t(v, gh)
                p_low = p_ref[(r * 2 + j) * 2 + h]
                p = p_low.astype(f32)
                ds = p * (dp - jnp.sum(dp * p, axis=0, keepdims=True))
                ds = ds.astype(bf16)
                dqs.append(mm(k_t[h * DH : (h + 1) * DH, :], ds))
                ps.append(p_low)
                dss.append(ds)
                gs.append(gh)
                qs.append(lane_half(q2, h))
            dq = (jnp.concatenate(dqs, axis=0) * scale).astype(bf16)
            dq_ref[at, j * hp : (j + 1) * hp] = flipped(dq)
            dv = mm(jnp.concatenate(ps, axis=1), jnp.concatenate(gs, axis=0))
            dk = mm(jnp.concatenate(dss, axis=1), jnp.concatenate(qs, axis=0)) * scale
            near_ref[at, base : base + hp] = dk[:toks]
            near_ref[at, base + hp : base + 2 * hp] = dv[:toks]
            far_ref[at, base : base + hp] = dk[toks:].astype(bf16)
            far_ref[at, base + hp : base + 2 * hp] = dv[toks:].astype(bf16)
    wait(out)


def project_back_kernel(dq, near_g, back, w, n_far, g_far, att_far, gown, goth, own_ref, b1, b2, b3, n_ref, g_ref, att_ref, acc, sems):
    hp = dq.shape[1] // 2
    toks = own_ref.shape[0]
    got = bring([(n_far, n_ref), (g_far, g_ref), (att_far, att_ref)], sems)
    for j, g in enumerate((gown, goth)):
        g[:, :hp] = dq[:, j * hp : (j + 1) * hp]
        both = slice(2 * j * hp, 2 * (j + 1) * hp)
        g[:, hp:] = (near_g[:, both] + back[:, both].astype(f32)).astype(bf16)
    acc[...] = mm_t(gown[...], w[0])
    acc[...] += mm_t(goth[...], w[1])
    own_ref[...] = acc[:toks]
    for r, ref in enumerate((b1, b2, b3)):
        ref[...] = acc[(r + 1) * toks : (r + 2) * toks].astype(bf16)
    wait(got)


def total_of(refs):
    total = refs[0][...]
    for ref in refs[1:]:
        total = total + ref[...].astype(f32)
    return total


def middle_kernel(x, b0, b1, b2, b3, hidden, norm_ref):
    value = x[...].astype(f32) + total_of((b0, b1, b2, b3))
    hidden[...] = value
    norm_ref[...] = normed(value).astype(bf16)


def ffn_kernel(n0, n1, n2, n3, all_y, w, hidden, mid, all_n, hidden_far, own_far, b1, b2, b3, acc, sems):
    toks = n0.shape[0]
    ff = w.shape[2] // 3
    blocks_n = bring(stacked((n1, n2, n3), all_n, 1), sems)
    kept = bring([(hidden, hidden_far)], sems, 3)
    all_n[:toks, :] = n0[...]
    wait(blocks_n)
    for j in range(2):
        gate = mm(all_n[...], w[j, :, :ff])
        up = mm(all_n[...], w[j, :, ff : 2 * ff])
        sig = jax.nn.sigmoid(gate)
        silu = gate * sig
        mid[j, :, 2 * ff :] = (silu * up).astype(bf16)
        grad_product = mm(all_y[...], w[j, :, 2 * ff :])
        mid[j, :, :ff] = (grad_product * up * sig * (1.0 + gate * (1.0 - sig))).astype(bf16)
        mid[j, :, ff : 2 * ff] = (grad_product * silu).astype(bf16)
        part = mm_t(mid[j, :, : 2 * ff], w[j, :, : 2 * ff])
        if j == 0:
            acc[...] = part
        else:
            acc[...] += part
    kept += bring([(acc.at[pl.ds(0, toks)], own_far)], sems, 4)
    for r, ref in enumerate((b1, b2, b3)):
        ref[...] = acc[(r + 1) * toks : (r + 2) * toks].astype(bf16)
    wait(kept)


def fetch_ffn_kernel(y0, y1, y2, y3, w_far, all_y, w, sems):
    wait(bring(stacked((y0, y1, y2, y3), all_y) + [(w_far, w)], sems))


def fetch_back_kernel(w_far, w, sems):
    hp = w.shape[2]
    wait(bring([(w_far.at[j, :, pl.ds(3 * hp, hp)], w.at[j]) for j in range(2)], sems))


def ffn_out_kernel(mid, w_far, own_far, b1, b2, b3, w, acc, sems):
    toks = b1.shape[0]
    ff = w.shape[2]
    weights = bring([(w_far.at[j, :, pl.ds(2 * ff, ff)], w.at[j]) for j in range(2)], sems)
    weights[0].wait()
    acc[...] = mm_t(mid[0, :, 2 * ff :], w[0])
    weights[1].wait()
    acc[...] += mm_t(mid[1, :, 2 * ff :], w[1])
    kept = bring([(acc.at[pl.ds(0, toks)], own_far)], sems, 2)
    for r, ref in enumerate((b1, b2, b3)):
        ref[...] = acc[(r + 1) * toks : (r + 2) * toks].astype(bf16)
    wait(kept)


def ffn_grads_kernel(all_n, y0, y1, y2, y3, mid, out_far, all_y, out, sems, out_sems):
    rows = out.shape[2]
    ff = out.shape[3] // 3
    copies = bring(stacked((y0, y1, y2, y3), all_y), sems)
    kept = []
    for i in range(4):
        for j in range(2):
            out[i, j, :, : 2 * ff] = outer_sum(all_n[:, i * rows : (i + 1) * rows], mid[j, :, : 2 * ff]).astype(bf16)
    wait(copies)
    for i in range(4):
        for j in range(2):
            out[i, j, :, 2 * ff :] = outer_sum(all_y[:, i * rows : (i + 1) * rows], mid[j, :, 2 * ff :]).astype(bf16)
            kept += bring([(out.at[i, j], out_far.at[i, j])], out_sems, 2 * i + j)
    wait(kept)


def split_halves(core, value, own, give):
    half = own.shape[1]
    first = core[0] == 0
    own[...] = jnp.where(first, value[:, :half], value[:, half:])
    give[...] = jnp.where(first, value[:, half:], value[:, :half])


def final_kernel(core, hidden_far, own_far, b1, b2, b3, own, give, hidden, part, sems):
    wait(bring([(hidden_far, hidden), (own_far, part)], sems))
    split_halves(core, (hidden[...] + total_of((part, b1, b2, b3))).astype(bf16), own, give)


def norm_back(x, grad):
    root = inverse_root(x)
    norm = x * root
    return root * (grad - norm * jnp.mean(grad * norm, axis=-1, keepdims=True))


def middle_back_kernel(hidden, grad_low, b0, b1, b2, b3, out, low):
    grad = grad_low[...].astype(f32) + norm_back(hidden[...], total_of((b0, b1, b2, b3)))
    out[...] = grad
    low[...] = grad.astype(bf16)


def leave_kernel(core, x, grad_hidden, b0, b1, b2, b3, out_own, out_give, own, give):
    half = out_own.shape[1]
    own[:, :half] = out_own[...]
    give[:, :half] = out_give[...]
    grad = grad_hidden[...] + norm_back(x[...].astype(f32), total_of((b0, b1, b2, b3)))
    split_halves(core, grad.astype(bf16), own.at[:, half:], give.at[:, half:])


def spread_kernel(core, slot_col, own, other, out):
    toks = own.shape[0]
    first = core[0] == 0
    token = lax.broadcasted_iota(jnp.int32, (slot_col.shape[0], toks), 1)
    low = (token == slot_col[...]).astype(bf16)
    high = ((token + toks) == slot_col[...]).astype(bf16)
    own, other = own[...], other[...]
    out[...] = (mm(low, jnp.where(first, own, other)) + mm(high, jnp.where(first, other, own))).astype(bf16)


def join_kernel(core, own, other, out, grad):
    half = own.shape[1] // 2
    first = core[0] == 0
    for ref, at in ((out, slice(0, half)), (grad, slice(half, 2 * half))):
        ref[:, :half] = jnp.where(first, own[:, at], other[:, at])
        ref[:, half:] = jnp.where(first, other[:, at], own[:, at])


def attn_grads_kernel(all_n, all_g, g0, g1, att, out_far, out, sems):
    rows = out.shape[2]
    hp = out.shape[3] // 4
    kept = []
    for i in range(4):
        at = slice(i * rows, (i + 1) * rows)
        for j, g in enumerate((g0, g1)):
            out[i, j, :, : 3 * hp] = outer_sum(all_n[:, at], g[...]).astype(bf16)
            out[i, j, :, 3 * hp :] = outer_sum(all_g[:, at], att[:, j * hp : (j + 1) * hp]).astype(bf16)
            kept += bring([(out.at[i, j], out_far.at[i, j])], sems, 2 * i + j)
    wait(kept)


def pick_kernel(me, part, s0, s1, s2, s3):
    rows = s0.shape[0]
    for k, ref in enumerate((s0, s1, s2, s3)):
        ref[...] = part[pl.ds(pl.multiple_of((me[0] ^ k) * rows, rows), rows), :]


def unpack_kernel(part, me, gain, s0, s1, s2, s3, *refs):
    n = (len(refs) - 1) // 2
    weights, outs, gain_sum, blocks = refs[: n - 1], refs[n - 1 : 2 * n - 1], refs[2 * n - 1], refs[2 * n]
    for k, ref in enumerate((s0, s1, s2, s3)):
        blocks[me[0] ^ k] = ref[...]
    size = blocks.shape[2] // n
    total = jnp.zeros(gain_sum.shape, f32)
    for m, out in enumerate(outs):
        for i in range(4):
            raw = blocks[i, :, m * size : m * size + part].astype(f32)
            at = slice(i * part, (i + 1) * part)
            if m < n - 1:
                total = total + jnp.sum(raw * weights[m][:, at].astype(f32), axis=1, keepdims=True)
                raw = raw * gain[...]
            out[:, at] = raw
    gain_sum[...] = total


def natural_rows(weight, far_sizes, rows):
    nz, nyh, nxh = far_sizes
    if nyh * nxh == 1:
        return weight
    cols = weight.shape[-1]
    split = weight.reshape(nz, nyh, nxh, 2, 2, rows, cols)
    return split.transpose(0, 1, 3, 2, 4, 5, 6).reshape(-1, cols)


def far_rows(weight, far_sizes, rows):
    nz, nyh, nxh = far_sizes
    if nyh * nxh == 1:
        return weight
    cols = weight.shape[-1]
    split = weight.reshape(nz, nyh, 2, nxh, 2, rows, cols)
    return split.transpose(0, 1, 3, 2, 4, 5, 6).reshape(-1, cols)


def spread_pack(pieces):
    rows = pieces[0].shape[0]
    blocks = [p.reshape(rows, 4, -1) for p in pieces]
    return jnp.concatenate(blocks, axis=-1).transpose(1, 0, 2)


def near_exchange(blocks, my_near):
    got = jnp.zeros(blocks.shape, blocks.dtype)
    for k in range(4):
        give = lax.dynamic_index_in_dim(blocks, my_near ^ k, 0, keepdims=True)
        got = lax.dynamic_update_slice_in_dim(got, near(give, k) if k else give, my_near ^ k, 0)
    return got


def body(patches, counts, doc_ids, w_query, w_key, w_value, w_output, w_gate, w_up, w_down, gain_attn, gain_ffn, cotangent):
    core = lax.axis_index(CORE)
    my_row = lax.axis_index(DP)
    my_near = lax.axis_index(NEAR)
    my_far = lax.axis_index(FAR)
    core_ref, near_ref, far_ref = core.reshape(1), my_near.reshape(1), my_far.reshape(1)
    peers, slot_cap, width = patches.shape[1:]
    half_width = width // 2
    slot_count = peers * slot_cap
    tok_count = doc_ids.shape[1]
    toks = tok_count // 2
    group = 4 * toks
    rows = w_query.shape[0]
    far_sizes = tuple(lax.axis_size(a) for a in FAR)
    far = far_sizes[0] * far_sizes[1] * far_sizes[2]
    direct = far == 4 and rows % 16 == 0
    score_scale = DH ** (-0.5)
    hp = w_query.shape[1] // 4
    ff_part = w_gate.shape[1] // 4
    ff_pad = -(-ff_part // 128) * 128
    gain_a = gain_attn.astype(f32)[:, None]
    gain_f = gain_ffn.astype(f32)[:, None]

    def far_shift(value, k):
        return lax.ppermute(value, FAR, [(i, (i + k) % far) for i in range(far)])

    def half_features(blocks):
        return lax.dynamic_slice_in_dim(blocks[0], core * half_width, half_width, 2)

    both = jnp.concatenate([half_features(patches), half_features(cotangent)], axis=-1)
    received = lax.all_to_all(both, DP, 0, 0, tiled=True).reshape(slot_count, width)

    def packed(weights, gain, part, size, token):
        weights = after(weights, token)
        if direct:
            return call(
                functools.partial(pack_kernel, part),
                [((rows, size * len(weights)), bf16)] * 4,
                [near_ref, gain, *weights],
                [pltpu.VMEM((4, rows, size * len(weights)), bf16)],
            )
        scaled = [(w.astype(f32) * gain).astype(bf16) for w in weights[:-1]] + [weights[-1]]
        return [jnp.pad(w.reshape(rows, 4, part), ((0, 0), (0, 0), (0, size - part))).reshape(rows, -1) for w in scaled]

    attn_weights = [w_query, w_key, w_value, w_output.T]
    ffn_weights = [w_gate, w_up, w_down.T]
    def gathered(pack, *tokens):
        if direct:
            got = scatter_near(pack[1:])
            (flat,) = call(place_kernel, [((4,) + pack[0].shape, bf16)], [near_ref, pack[0], *got])
        else:
            flat = near_exchange(spread_pack(pack), my_near)
        cols = flat.shape[-1]
        flat = flat.reshape(4 * rows, cols)
        return flat, lambda operand: lax.all_gather(operand, (CORE,) + FAR, axis=0, tiled=True).reshape(2, width, cols)

    attn_flat, gather_attn = gathered(packed(attn_weights, gain_a, hp, hp, both))
    attn_w = gather_attn(attn_flat)
    ffn_flat, gather_ffn = gathered(packed(ffn_weights, gain_f, ff_part, ff_pad, attn_flat))
    doc_rows = jnp.concatenate(gather_near(after(doc_ids, attn_flat)), axis=0)
    my_counts = lax.dynamic_index_in_dim(counts, my_row, 0, keepdims=False)
    offsets = jnp.cumsum(my_counts) - my_counts
    slots = jnp.arange(slot_cap, dtype=jnp.int32)
    slot_token = jnp.where(slots[None, :] < my_counts[:, None], offsets[:, None] + slots[None, :], -1).reshape(-1)
    slot_row, slot_col = slot_token[None, :], slot_token[:, None]
    received, slot_row, slot_col, doc_rows, ffn_flat = lax.optimization_barrier(
        (received, slot_row, slot_col, doc_rows, ffn_flat)
    )
    ffn_w = gather_ffn(ffn_flat)
    if not direct:
        attn_w, ffn_w = (jnp.stack([natural_rows(w[i], far_sizes, rows) for i in range(2)]) for w in (attn_w, ffn_w))
    doc_own = lax.dynamic_slice_in_dim(doc_rows, core * toks, toks, 1)
    doc_oth = lax.dynamic_slice_in_dim(doc_rows, (1 - core) * toks, toks, 1)

    docs = (doc_own, doc_own.T, doc_oth.T)
    slab = ((toks, width), f32), ((toks, width), bf16), ((toks, width), bf16), ((toks, width), bf16)
    token_low = ((toks, width), bf16)
    half_low = ((toks, half_width), bf16)
    whole = ((group, width), bf16)
    sems = pltpu.SemaphoreType.DMA
    slab_low, slab_full, all_low = pltpu.VMEM((toks, width), bf16), pltpu.VMEM((toks, width), f32), pltpu.VMEM(*whole)
    acc = pltpu.VMEM((group, width), f32)
    attn_cols = pltpu.VMEM((2, width, 3 * hp), bf16)
    out_cols = pltpu.VMEM((2, width, hp), bf16)
    q_shape, kv_shape = ((group, 2 * hp), bf16), ((group, 4 * hp), bf16)
    head_count = 4 * 2 * hp // DH
    probs_shape = ((head_count, 2 * toks, toks), bf16)
    ffn_w_shape = ((2, width, 3 * ff_pad), bf16)

    own, give = call(collect_kernel, [token_low, token_low], [core_ref, slot_row, received])
    x, grad_low, norm, x_far = call(
        enter_kernel, [token_low] * 4, [core_ref, own, swap(give)], [sems((1,))], far_outs=(3,)
    )
    norm_a = gather_near(norm)
    grad_y = gather_near(grad_low)
    (attn_near,) = fetch([attn_w])
    q, kv, norm_a_all = call(
        project_kernel,
        [q_shape, kv_shape, whole],
        [after(norm, docs, ffn_flat), *norm_a[1:], attn_near],
        [all_low, sems((4,))],
        us=0,
        far_args=range(1, 4),
        far_outs=(2,),
    )
    probs, q_far, kv_far, kvf_far, attended, *branch = call(
        functools.partial(attend_kernel, score_scale),
        [probs_shape, q_shape, kv_shape, kv_shape, q_shape, *slab],
        [core_ref, q, kv, swap(kv), *docs, attn_w],
        [pltpu.VMEM(*probs_shape), pltpu.VMEM(*q_shape), out_cols, sems((6,)), sems((head_count,))],
        us=0,
        far_args=(7,),
        far_outs=range(5),
    )
    branch = after(branch, grad_y)
    hidden, norm = call(middle_kernel, [slab[0], token_low], [x, branch[0], *scatter_near(branch[1:])])
    norm_f = gather_near(norm)
    y_all, ffn_near = call(
        fetch_ffn_kernel, [whole, ffn_w_shape], [*grad_y, ffn_w], [sems((5,))], us=2, far_args=range(5)
    )
    mid, norm_f_all, hidden, grad_norm, *grad_norm_low = call(
        ffn_kernel,
        [((2, group, 3 * ff_pad), bf16), whole, slab[0], *slab],
        [*norm_f, y_all, ffn_near, hidden],
        [acc, sems((5,))],
        12,
        7,
        range(1, 4),
        (2, 3),
    )
    branch = call(
        ffn_out_kernel,
        slab,
        [mid, ffn_w],
        [pltpu.VMEM((2, width, ff_pad), bf16), acc, sems((3,))],
        6,
        2,
        (1,),
        (0,),
    )
    ffn_grads_shape = ((4, 2, width // 4, 3 * ff_pad), bf16)
    (ffn_grads,) = call(
        ffn_grads_kernel,
        [ffn_grads_shape],
        [norm_f_all, *grad_y, mid],
        [all_low, pltpu.VMEM(*ffn_grads_shape), sems((4,)), sems((8,))],
        12,
        4,
        range(1, 5),
        (0,),
    )
    grad_hidden, grad_hidden_low = call(
        middle_back_kernel,
        [slab[0], token_low],
        [*fetch([hidden, grad_low]), *fetch([grad_norm]), *scatter_near(grad_norm_low)],
    )
    grad_branch = gather_near(grad_hidden_low)
    final_parts = scatter_near(after(branch[1:], grad_hidden_low))

    def reduced(grads):
        cols = grads.shape[-1]
        if not direct:
            halves = jnp.moveaxis(grads, 1, 0).reshape(2, width, cols)
            grads = jnp.stack([far_rows(half, far_sizes, rows).reshape(far, -1, cols) for half in halves], axis=1)
        return lax.psum_scatter(grads.reshape(-1, cols), FAR + (CORE,), scatter_dimension=0, tiled=True)

    ffn_part = reduced(ffn_grads)

    grad_q, grad_kv, far_give, attn_near, grad_branch_all, grad_hidden = call(
        functools.partial(attend_back_kernel, score_scale),
        [q_shape, ((group, 4 * hp), f32), kv_shape, ((2, width, 3 * hp), bf16), whole, slab[0]],
        [*grad_branch, *call(fetch_back_kernel, [((2, width, hp), bf16)], [attn_w], [sems((2,))], far_args=(0,)),
         *fetch([q_far, kv_far, kvf_far, probs]), grad_hidden, attn_w],
        [all_low, pltpu.VMEM(*q_shape), sems((4,))],
        us=7,
        far_args=(10,),
        far_outs=(4, 5),
    )
    out_own, out_give = call(
        final_kernel,
        [half_low, half_low],
        [core_ref, hidden, branch[0], *after(final_parts, grad_q)],
        [slab_full, slab_full, sems((2,))],
        far_args=(1, 2),
    )
    gqkv_own, gqkv_oth, own_norm, *grad_norm, n_all, g_all, att = call(
        project_back_kernel,
        [((group, 3 * hp), bf16), ((group, 3 * hp), bf16), *slab, whole, whole, q_shape],
        [grad_q, grad_kv, swap(after(far_give, out_own)), attn_near, norm_a_all, grad_branch_all, attended],
        [acc, sems((3,))],
        us=2,
        far_args=(4, 5, 6),
    )
    arriving = scatter_near(grad_norm)
    attn_grads_shape = ((4, 2, width // 4, 4 * hp), bf16)
    (attn_grads,) = call(
        attn_grads_kernel,
        [attn_grads_shape],
        [n_all, g_all, gqkv_own, gqkv_oth, att],
        [pltpu.VMEM(*attn_grads_shape), sems((8,))],
        8,
        3,
        far_outs=(0,),
    )
    attn_part = reduced(after(attn_grads, ffn_part, arriving))
    own, give = call(
        leave_kernel,
        [token_low, token_low],
        [core_ref, *fetch([x_far, grad_hidden]), own_norm, *arriving, out_own, out_give],
    )

    def finished(pieces, weights, gain, part, size):
        n = len(weights)
        return call(
            functools.partial(unpack_kernel, part),
            [((rows, 4 * part), f32)] * n + [((rows, 1), f32)],
            [near_ref, gain, *pieces, *weights[:-1]],
            [pltpu.VMEM((4, rows, n * size), bf16)],
        )

    def finished_plain(blocks, weights, gain, part, size):
        blocks = near_exchange(blocks.reshape(4, rows, -1), my_near)
        raws = []
        for m in range(len(weights)):
            piece = blocks[:, :, m * size : m * size + part].astype(f32)
            raws.append(piece.transpose(1, 0, 2).reshape(rows, 4 * part))
        total = sum(jnp.sum(r * w.astype(f32), axis=1, keepdims=True) for r, w in zip(raws[:-1], weights[:-1]))
        return [r * gain for r in raws[:-1]] + [raws[-1], total]

    def returned(own, *tokens):
        (spread,) = call(spread_kernel, [((slot_count, width), bf16)], [core_ref, slot_col, after(own, tokens), swap(give)])
        back = lax.all_to_all(spread.reshape(peers, slot_cap, width), DP, 0, 0, tiled=True)
        return back.reshape(slot_count, width)

    if direct:
        back = returned(own)

        def pieces_of(part):
            pieces = call(pick_kernel, [((rows, part.shape[1]), bf16)] * 4, [near_ref, part])
            return [pieces[0]] + scatter_near(pieces[1:])

        *ffn_grads, sum_f = finished(pieces_of(ffn_part), ffn_weights, gain_f, ff_part, ff_pad)
        *attn_grads, sum_a = finished(pieces_of(attn_part), attn_weights, gain_a, hp, hp)
        back = after(back, ffn_grads, attn_grads)
    else:
        back = returned(own)
        *attn_grads, sum_a = finished_plain(attn_part, attn_weights, gain_a, hp, hp)
        *ffn_grads, sum_f = finished_plain(ffn_part, ffn_weights, gain_f, ff_part, ff_pad)
    gains = jnp.concatenate([sum_a, sum_f], axis=1).T
    gains = gains + swap(gains)
    outputs, input_grad = call(join_kernel, [((slot_count, width), bf16)] * 2, [core_ref, back, swap(back)])
    grad_q, grad_k, grad_v, grad_o = attn_grads
    grad_g, grad_u, grad_d = ffn_grads
    return (
        outputs.reshape(patches.shape),
        input_grad.reshape(patches.shape),
        grad_q,
        grad_k,
        grad_v,
        grad_o.T,
        grad_g,
        grad_u,
        grad_d.T,
        gains[0],
        gains[1],
    )


def solution(mesh):
    dp_size = mesh.shape["dp"]
    side = round((dp_size / 2) ** (1 / 3))
    grid = (2 * side, side // 2, 2, side // 2, 2, 2)
    inner = Mesh(np.asarray(mesh.devices).reshape(grid), ("z", "yh", "yl", "xh", "xl", "c"))
    rows_first = P(DP, "c")
    cols_first = P("c", DP)
    blocks = P(DP, None, None, None)
    weights = (rows_first, rows_first, rows_first, cols_first, rows_first, rows_first, cols_first, P(DP), P(DP))
    in_specs = (blocks, P(), P(DP, None)) + weights + (blocks,)
    out_specs = (blocks, blocks) + weights
    return jax.shard_map(body, mesh=inner, in_specs=in_specs, out_specs=out_specs, check_vma=False)
```

```python
import functools

import jax
import jax.numpy as jnp
import numpy as np
from jax import lax
from jax.experimental import pallas as pl
from jax.experimental.pallas import tpu as pltpu
from jax.sharding import Mesh, PartitionSpec as P

DH = 64
eps = 1e-05
masked_score = -1e30
bf16 = jnp.bfloat16
f32 = jnp.float32

DP = ("z", "yh", "yl", "xh", "xl")
FAR = ("z", "yh", "xh")
NEAR = ("yl", "xl")
CORE = "c"


def mm(left, right):
    return lax.dot_general(left, right, (((1,), (0,)), ((), ())), preferred_element_type=f32)


def mm_t(left, right):
    return lax.dot_general(left, right, (((1,), (1,)), ((), ())), preferred_element_type=f32)


def outer_sum(left, right):
    return lax.dot_general(left, right, (((0,), (0,)), ((), ())), preferred_element_type=f32)


def swap(value):
    return lax.ppermute(value, CORE, [(0, 1), (1, 0)])


def near(value, k):
    return lax.ppermute(value, NEAR, [(i, i ^ k) for i in range(4)])


def gather_near(value):
    return [value] + [near(value, k) for k in (1, 2, 3)]


def scatter_near(low):
    return [near(low[k - 1], k) for k in (1, 2, 3)]


def after(value, *tokens):
    return lax.optimization_barrier((value, tokens))[0]


def inverse_root(values):
    return lax.rsqrt(jnp.mean(values * values, axis=-1, keepdims=True) + eps)


def call(kernel, outs, args, scratch=(), limit=4, us=1.0, far_args=(), far_outs=(), aliases=None):
    def space(i, ndim, left):
        if i in left:
            return pl.BlockSpec(memory_space=pltpu.HBM)
        return pl.BlockSpec(memory_space=pltpu.SMEM if ndim == 1 else pltpu.VMEM)

    args = [pltpu.with_memory_space_constraint(a, pltpu.HBM) if i in far_args else a for i, a in enumerate(args)]
    return pl.pallas_call(
        kernel,
        out_shape=[
            pltpu.HBM(shape, kind) if i in far_outs else jax.ShapeDtypeStruct(shape, kind)
            for i, (shape, kind) in enumerate(outs)
        ],
        in_specs=[space(i, a.ndim, far_args) for i, a in enumerate(args)],
        out_specs=[space(i, 2, far_outs) for i in range(len(outs))],
        scratch_shapes=list(scratch),
        input_output_aliases=aliases or {},
        compiler_params=pltpu.CompilerParams(vmem_limit_bytes=limit << 20),
        cost_estimate=pl.CostEstimate(flops=int(us * 1e9), bytes_accessed=int(us * 1e6), transcendentals=0),
    )(*args)


def bring(pairs, sems, first=0):
    copies = [pltpu.make_async_copy(a, b, sems.at[first + i]) for i, (a, b) in enumerate(pairs)]
    for copy in copies:
        copy.start()
    return copies


def wait(copies):
    for copy in copies:
        copy.wait()


def stacked(refs, whole, first=0):
    rows = refs[0].shape[0]
    return [(ref, whole.at[pl.ds((first + r) * rows, rows)]) for r, ref in enumerate(refs)]


def lane_half(value, half):
    lanes = lax.broadcasted_iota(jnp.int32, value.shape, 1)
    keep = (lanes < DH) if half == 0 else (lanes >= DH)
    return jnp.where(keep, value, jnp.zeros_like(value))


def flipped(value):
    n = value.shape[1]
    eye = (
        lax.broadcasted_iota(jnp.int32, (n, n), 0) == lax.broadcasted_iota(jnp.int32, (n, n), 1)
    ).astype(bf16)
    return mm_t(eye, value).astype(bf16)


def fetch_kernel(*refs):
    n = (len(refs) - 1) // 2
    wait(bring(list(zip(refs[:n], refs[n : 2 * n])), refs[2 * n]))


def fetch(arrays, us=1.0):
    outs = [(a.shape, a.dtype) for a in arrays]
    return call(fetch_kernel, outs, arrays, [pltpu.SemaphoreType.DMA((len(arrays),))], 2, us, range(len(arrays)))


def pack_kernel(part, me, gain, *refs):
    n = len(refs) - 5
    weights, outs, blocks = refs[:n], refs[n : n + 4], refs[n + 4]
    size = blocks.shape[2] // n
    if size != part:
        blocks[...] = jnp.zeros(blocks.shape, blocks.dtype)
    for m, ref in enumerate(weights):
        w = ref[...].astype(f32)
        if m < n - 1:
            w = w * gain[...]
        w = w.astype(bf16)
        for i in range(4):
            blocks[i, :, m * size : m * size + part] = w[:, i * part : (i + 1) * part]
    for k, out in enumerate(outs):
        out[...] = blocks[me[0] ^ k]


def place_kernel(me, b0, b1, b2, b3, out):
    for k, ref in enumerate((b0, b1, b2, b3)):
        out[me[0] ^ k] = ref[...]


def place_far_kernel(me, far, b0, b1, b2, b3, out):
    for k, ref in enumerate((b0, b1, b2, b3)):
        plane = lax.rem(far[0] + (4 - k), 4)
        for i in range(4):
            out[plane * 4 + (me[0] ^ i)] = ref[i]


def collect_kernel(core, slot_row, slots, own, give):
    toks = own.shape[0]
    token = lax.broadcasted_iota(jnp.int32, (toks, slots.shape[0]), 0)
    for ref, half in ((own, core[0]), (give, 1 - core[0])):
        place = ((token + half * toks) == slot_row[...]).astype(bf16)
        ref[...] = mm(place, slots[...]).astype(bf16)


def normed(x):
    return x * inverse_root(x)


def enter_kernel(core, own, other, x_ref, y_ref, norm_ref, x_far, sems):
    half = own.shape[1] // 2
    first = core[0] == 0
    for ref, at in ((x_ref, slice(0, half)), (y_ref, slice(half, 2 * half))):
        ref[:, :half] = jnp.where(first, own[:, at], other[:, at])
        ref[:, half:] = jnp.where(first, other[:, at], own[:, at])
    kept = bring([(x_ref, x_far)], sems)
    norm_ref[...] = normed(x_ref[...].astype(f32)).astype(bf16)
    wait(kept)


def project_kernel(n0, n1, n2, n3, w, q_ref, kv_ref, n_far, all_n, sems):
    hp = w.shape[2] // 4
    toks = n0.shape[0]
    blocks = bring(stacked((n1, n2, n3), all_n, 1), sems)
    all_n[:toks, :] = n0[...]
    wait(blocks)
    kept = bring([(all_n, n_far)], sems, 3)
    for j in range(2):
        out = mm(all_n[...], w[j, :, : 3 * hp])
        q_ref[:, j * hp : (j + 1) * hp] = out[:, :hp].astype(bf16)
        kv_ref[:, 2 * j * hp : 2 * (j + 1) * hp] = out[:, hp:].astype(bf16)
    wait(kept)


def attend_kernel(scale, core, q_ref, kv, kvf, doc_q, doc_kn, doc_kf, w_far, p_far, q_far, kv_far, kvf_far, att_far, own_ref, b1, b2, b3, p_ref, att_ref, w, sems, p_sems):
    hp = q_ref.shape[1] // 2
    weights = bring([(w_far.at[j, :, pl.ds(3 * hp, hp)], w.at[j]) for j in range(2)], sems)
    kept = bring([(q_ref, q_far), (kv, kv_far), (kvf, kvf_far)], sems, 2)
    rows = doc_q.shape[0]
    toks = q_ref.shape[0] // rows
    key_pos = lax.broadcasted_iota(jnp.int32, (toks, toks), 0)
    query_pos = lax.broadcasted_iota(jnp.int32, (toks, toks), 1)
    causal = key_pos <= query_pos
    later = core[0] == 1
    for r in range(rows):
        at = slice(r * toks, (r + 1) * toks)
        dq = doc_q[r : r + 1, :]
        near_ok = causal & (doc_kn[:, r : r + 1] == dq)
        far_ok = (doc_kf[:, r : r + 1] == dq) & later
        for j in range(2):
            base = 2 * j * hp
            q2 = q_ref[at, j * hp : (j + 1) * hp]
            kn, kf = kv[at, base : base + hp], kvf[at, base : base + hp]
            v_t = jnp.concatenate(
                [flipped(kv[at, base + hp : base + 2 * hp]), flipped(kvf[at, base + hp : base + 2 * hp])], axis=1
            )
            pieces = []
            for h in range(2):
                qh = lane_half(q2, h)
                sn = jnp.where(near_ok, mm_t(kn, qh) * scale, masked_score)
                sf = jnp.where(far_ok, mm_t(kf, qh) * scale, masked_score)
                top = jnp.maximum(jnp.max(sn, axis=0, keepdims=True), jnp.max(sf, axis=0, keepdims=True))
                en, ef = jnp.exp(sn - top), jnp.exp(sf - top)
                total = jnp.sum(en, axis=0, keepdims=True) + jnp.sum(ef, axis=0, keepdims=True)
                inv = 1.0 / total
                p = (jnp.concatenate([en, ef], axis=0) * inv).astype(bf16)
                at_head = (r * 2 + j) * 2 + h
                p_ref[at_head] = p
                kept += bring([(p_ref.at[at_head], p_far.at[at_head])], p_sems, at_head)
                pieces.append(mm(v_t[h * DH : (h + 1) * DH, :], p))
            att_ref[at, j * hp : (j + 1) * hp] = flipped(jnp.concatenate(pieces, axis=0).astype(bf16)).astype(bf16)
        kept += bring([(att_ref.at[pl.ds(r * toks, toks)], att_far.at[pl.ds(r * toks, toks)])], sems, 5 + r)
        if r == 0:
            wait(weights)
        out = mm_t(att_ref[at, :hp], w[0]) + mm_t(att_ref[at, hp:], w[1])
        if r == 0:
            own_ref[...] = out
        else:
            (b1, b2, b3)[r - 1][...] = out.astype(bf16)
    wait(kept)


def attend_back_kernel(scale, g0, g1, g2, g3, w_out, q_ref, kv, kvf, p_ref, hidden_ref, w_far, dq_ref, near_ref, far_ref, w, g_far, hidden_far, all_g, ga_ref, sems):
    hp = q_ref.shape[1] // 2
    toks = g0.shape[0]
    out = bring([(w_far.at[j, :, pl.ds(0, 3 * hp)], w.at[j]) for j in range(2)] + [(hidden_ref, hidden_far)], sems)
    for r, ref in enumerate((g0, g1, g2, g3)):
        all_g[r * toks : (r + 1) * toks, :] = ref[...]
    out += bring([(all_g, g_far)], sems, 3)
    for j in range(2):
        ga_ref[:, j * hp : (j + 1) * hp] = mm(all_g[...], w_out[j]).astype(bf16)
    for r in range(4):
        at = slice(r * toks, (r + 1) * toks)
        for j in range(2):
            g = ga_ref[at, j * hp : (j + 1) * hp]
            base = 2 * j * hp
            q2 = q_ref[at, j * hp : (j + 1) * hp]
            v = jnp.concatenate([kv[at, base + hp : base + 2 * hp], kvf[at, base + hp : base + 2 * hp]], axis=0)
            k_t = jnp.concatenate([flipped(kv[at, base : base + hp]), flipped(kvf[at, base : base + hp])], axis=1)
            dqs, ps, dss, gs, qs = [], [], [], [], []
            for h in range(2):
                gh = lane_half(g, h)
                dp = mm_t(v, gh)
                p_low = p_ref[(r * 2 + j) * 2 + h]
                p = p_low.astype(f32)
                ds = p * (dp - jnp.sum(dp * p, axis=0, keepdims=True))
                ds = ds.astype(bf16)
                dqs.append(mm(k_t[h * DH : (h + 1) * DH, :], ds))
                ps.append(p_low)
                dss.append(ds)
                gs.append(gh)
                qs.append(lane_half(q2, h))
            dq = (jnp.concatenate(dqs, axis=0) * scale).astype(bf16)
            dq_ref[at, j * hp : (j + 1) * hp] = flipped(dq)
            dv = mm(jnp.concatenate(ps, axis=1), jnp.concatenate(gs, axis=0))
            dk = mm(jnp.concatenate(dss, axis=1), jnp.concatenate(qs, axis=0)) * scale
            near_ref[at, base : base + hp] = dk[:toks]
            near_ref[at, base + hp : base + 2 * hp] = dv[:toks]
            far_ref[at, base : base + hp] = dk[toks:].astype(bf16)
            far_ref[at, base + hp : base + 2 * hp] = dv[toks:].astype(bf16)
    wait(out)


def project_back_kernel(dq, near_g, back, w, n_far, g_far, att_far, gown, goth, own_ref, b1, b2, b3, n_ref, g_ref, att_ref, acc, sems):
    hp = dq.shape[1] // 2
    toks = own_ref.shape[0]
    got = bring([(n_far, n_ref), (g_far, g_ref), (att_far, att_ref)], sems)
    for j, g in enumerate((gown, goth)):
        g[:, :hp] = dq[:, j * hp : (j + 1) * hp]
        both = slice(2 * j * hp, 2 * (j + 1) * hp)
        g[:, hp:] = (near_g[:, both] + back[:, both].astype(f32)).astype(bf16)
    acc[...] = mm_t(gown[...], w[0])
    acc[...] += mm_t(goth[...], w[1])
    own_ref[...] = acc[:toks]
    for r, ref in enumerate((b1, b2, b3)):
        ref[...] = acc[(r + 1) * toks : (r + 2) * toks].astype(bf16)
    wait(got)


def total_of(refs):
    total = refs[0][...]
    for ref in refs[1:]:
        total = total + ref[...].astype(f32)
    return total


def middle_kernel(x, b0, b1, b2, b3, hidden, norm_ref):
    value = x[...].astype(f32) + total_of((b0, b1, b2, b3))
    hidden[...] = value
    norm_ref[...] = normed(value).astype(bf16)


def ffn_kernel(second, n0, n1, y, w, *refs):
    if second:
        mid, all_n, b0, b1, acc = refs[2:]
    else:
        hidden, mid, all_n, hidden_far, b0, b1, acc, sems = refs
        kept = bring([(hidden, hidden_far)], sems)
    toks = n0.shape[0]
    ff = w.shape[2] // 3
    rows = pl.ds(2 * toks if second else 0, 2 * toks)
    for r, ref in enumerate((n0, n1)):
        all_n[pl.ds((2 * second + r) * toks, toks), :] = ref[...]
    for j in range(2):
        gate = mm(all_n[rows, :], w[j, :, :ff])
        up = mm(all_n[rows, :], w[j, :, ff : 2 * ff])
        sig = jax.nn.sigmoid(gate)
        silu = gate * sig
        mid[rows, (4 + j) * ff : (5 + j) * ff] = (silu * up).astype(bf16)
        grad_product = mm(y[...], w[j, :, 2 * ff :])
        at = 2 * j * ff
        mid[rows, at : at + ff] = (grad_product * up * sig * (1.0 + gate * (1.0 - sig))).astype(bf16)
        mid[rows, at + ff : at + 2 * ff] = (grad_product * silu).astype(bf16)
        part = mm_t(mid[rows, at : at + 2 * ff], w[j, :, : 2 * ff])
        if j == 0:
            acc[...] = part
        else:
            acc[...] += part
    b0[...] = acc[:toks].astype(b0.dtype)
    b1[...] = acc[toks:].astype(bf16)
    if not second:
        wait(kept)


def fetch_ffn_kernel(y0, y1, y2, y3, w_far, y_first, y_second, w, sems):
    wait(bring(stacked((y0, y1), y_first) + stacked((y2, y3), y_second) + [(w_far, w)], sems))


def fetch_back_kernel(w_far, w, sems):
    hp = w.shape[2]
    wait(bring([(w_far.at[j, :, pl.ds(3 * hp, hp)], w.at[j]) for j in range(2)], sems))


def ffn_out_kernel(mid, w_far, own_far, b1, b2, b3, w, acc, sems):
    toks = b1.shape[0]
    ff = w.shape[2]
    weights = bring([(w_far.at[j, :, pl.ds(2 * ff, ff)], w.at[j]) for j in range(2)], sems)
    weights[0].wait()
    acc[...] = mm_t(mid[:, 4 * ff : 5 * ff], w[0])
    weights[1].wait()
    acc[...] += mm_t(mid[:, 5 * ff :], w[1])
    kept = bring([(acc.at[pl.ds(0, toks)], own_far)], sems, 2)
    for r, ref in enumerate((b1, b2, b3)):
        ref[...] = acc[(r + 1) * toks : (r + 2) * toks].astype(bf16)
    wait(kept)


def ffn_grads_kernel(all_n, y0, y1, y2, y3, mid, own_ref, out_far, own_far, all_y, out, sems, out_sems):
    rows = out.shape[2]
    ff = out.shape[3] // 3
    copies = bring(stacked((y0, y1, y2, y3), all_y), sems)
    kept = bring([(own_ref, own_far)], sems, 4)
    for i in range(4):
        grads = outer_sum(all_n[:, i * rows : (i + 1) * rows], mid[:, : 4 * ff]).astype(bf16)
        for j in range(2):
            out[i, j, :, : 2 * ff] = grads[:, 2 * j * ff : 2 * (j + 1) * ff]
        if i == 0:
            wait(copies)
        grads = outer_sum(all_y[:, i * rows : (i + 1) * rows], mid[:, 4 * ff :]).astype(bf16)
        for j in range(2):
            out[i, j, :, 2 * ff :] = grads[:, j * ff : (j + 1) * ff]
        kept += bring([(out.at[i], out_far.at[i])], out_sems, i)
    wait(kept)


def split_halves(core, value, own, give):
    half = own.shape[1]
    first = core[0] == 0
    own[...] = jnp.where(first, value[:, :half], value[:, half:])
    give[...] = jnp.where(first, value[:, half:], value[:, :half])


def final_kernel(core, hidden_far, own_far, b1, b2, b3, own, give, hidden, part, sems):
    wait(bring([(hidden_far, hidden), (own_far, part)], sems))
    split_halves(core, (hidden[...] + total_of((part, b1, b2, b3))).astype(bf16), own, give)


def norm_back(x, grad):
    root = inverse_root(x)
    norm = x * root
    return root * (grad - norm * jnp.mean(grad * norm, axis=-1, keepdims=True))


def middle_back_kernel(hidden, grad_low, b0, b1, b2, b3, out, low):
    grad = grad_low[...].astype(f32) + norm_back(hidden[...], total_of((b0, b1, b2, b3)))
    out[...] = grad
    low[...] = grad.astype(bf16)


def leave_kernel(core, x, grad_hidden, b0, b1, b2, b3, out_own, out_give, own, give):
    half = out_own.shape[1]
    own[:, :half] = out_own[...]
    give[:, :half] = out_give[...]
    grad = grad_hidden[...] + norm_back(x[...].astype(f32), total_of((b0, b1, b2, b3)))
    split_halves(core, grad.astype(bf16), own.at[:, half:], give.at[:, half:])


def spread_kernel(core, slot_col, own, other, out):
    toks = own.shape[0]
    first = core[0] == 0
    token = lax.broadcasted_iota(jnp.int32, (slot_col.shape[0], toks), 1)
    low = (token == slot_col[...]).astype(bf16)
    high = ((token + toks) == slot_col[...]).astype(bf16)
    own, other = own[...], other[...]
    out[...] = (mm(low, jnp.where(first, own, other)) + mm(high, jnp.where(first, other, own))).astype(bf16)


def join_kernel(core, own, other, out, grad):
    half = own.shape[1] // 2
    first = core[0] == 0
    for ref, at in ((out, slice(0, half)), (grad, slice(half, 2 * half))):
        ref[:, :half] = jnp.where(first, own[:, at], other[:, at])
        ref[:, half:] = jnp.where(first, other[:, at], own[:, at])


def attn_grads_kernel(core, all_n, all_g, g0, g1, att, own, oth):
    hp = att.shape[1] // 2
    for j, out in enumerate((own, oth)):
        mine = core[0] == j
        out[:, : 3 * hp] = outer_sum(all_n[...], jnp.where(mine, g0[...], g1[...])).astype(bf16)
        out[:, 3 * hp :] = outer_sum(all_g[...], jnp.where(mine, att[:, :hp], att[:, hp:])).astype(bf16)


def core_sum_kernel(far, own, other, t0, t1, t2, t3):
    rows = t0.shape[0]
    for k, ref in enumerate((t0, t1, t2, t3)):
        at = pl.ds(pl.multiple_of(lax.rem(far[0] + k, 4) * rows, rows), rows)
        ref[...] = (own[at, :].astype(f32) + other[at, :].astype(f32)).astype(bf16)


def far_sum_kernel(me, t0, t1, t2, t3, s0, s1, s2, s3):
    rows = s0.shape[0]
    for k, ref in enumerate((s0, s1, s2, s3)):
        at = pl.ds(pl.multiple_of((me[0] ^ k) * rows, rows), rows)
        total = t0[at, :].astype(f32)
        for other in (t1, t2, t3):
            total = total + other[at, :].astype(f32)
        ref[...] = total.astype(bf16)


def pick_kernel(me, part, s0, s1, s2, s3, sems):
    rows = s0.shape[0]
    pairs = [(part.at[pl.ds(pl.multiple_of((me[0] ^ k) * rows, rows), rows)], ref) for k, ref in enumerate((s0, s1, s2, s3))]
    wait(bring(pairs, sems))


def unpack_kernel(part, me, gain, s0, s1, s2, s3, *refs):
    n = (len(refs) - 1) // 2
    weights, outs, gain_sum, blocks = refs[: n - 1], refs[n - 1 : 2 * n - 1], refs[2 * n - 1], refs[2 * n]
    for k, ref in enumerate((s0, s1, s2, s3)):
        blocks[me[0] ^ k] = ref[...]
    size = blocks.shape[2] // n
    total = jnp.zeros(gain_sum.shape, f32)
    for m, out in enumerate(outs):
        for i in range(4):
            raw = blocks[i, :, m * size : m * size + part].astype(f32)
            at = slice(i * part, (i + 1) * part)
            if m < n - 1:
                total = total + jnp.sum(raw * weights[m][:, at].astype(f32), axis=1, keepdims=True)
                raw = raw * gain[...]
            out[:, at] = raw
    gain_sum[...] = total


def natural_rows(weight, far_sizes, rows):
    nz, nyh, nxh = far_sizes
    if nyh * nxh == 1:
        return weight
    cols = weight.shape[-1]
    split = weight.reshape(nz, nyh, nxh, 2, 2, rows, cols)
    return split.transpose(0, 1, 3, 2, 4, 5, 6).reshape(-1, cols)


def far_rows(weight, far_sizes, rows):
    nz, nyh, nxh = far_sizes
    if nyh * nxh == 1:
        return weight
    cols = weight.shape[-1]
    split = weight.reshape(nz, nyh, 2, nxh, 2, rows, cols)
    return split.transpose(0, 1, 3, 2, 4, 5, 6).reshape(-1, cols)


def spread_pack(pieces):
    rows = pieces[0].shape[0]
    blocks = [p.reshape(rows, 4, -1) for p in pieces]
    return jnp.concatenate(blocks, axis=-1).transpose(1, 0, 2)


def near_exchange(blocks, my_near):
    got = jnp.zeros(blocks.shape, blocks.dtype)
    for k in range(4):
        give = lax.dynamic_index_in_dim(blocks, my_near ^ k, 0, keepdims=True)
        got = lax.dynamic_update_slice_in_dim(got, near(give, k) if k else give, my_near ^ k, 0)
    return got


def body(patches, counts, doc_ids, w_query, w_key, w_value, w_output, w_gate, w_up, w_down, gain_attn, gain_ffn, cotangent):
    core = lax.axis_index(CORE)
    my_row = lax.axis_index(DP)
    my_near = lax.axis_index(NEAR)
    my_far = lax.axis_index(FAR)
    core_ref, near_ref, far_ref = core.reshape(1), my_near.reshape(1), my_far.reshape(1)
    peers, slot_cap, width = patches.shape[1:]
    half_width = width // 2
    slot_count = peers * slot_cap
    tok_count = doc_ids.shape[1]
    toks = tok_count // 2
    group = 4 * toks
    rows = w_query.shape[0]
    far_sizes = tuple(lax.axis_size(a) for a in FAR)
    far = far_sizes[0] * far_sizes[1] * far_sizes[2]
    direct = far == 4 and rows % 16 == 0
    score_scale = DH ** (-0.5)
    hp = w_query.shape[1] // 4
    ff_part = w_gate.shape[1] // 4
    ff_pad = -(-ff_part // 128) * 128
    gain_a = gain_attn.astype(f32)[:, None]
    gain_f = gain_ffn.astype(f32)[:, None]

    def far_shift(value, k):
        return lax.ppermute(value, FAR, [(i, (i + k) % far) for i in range(far)])

    def half_features(blocks):
        return lax.dynamic_slice_in_dim(blocks[0], core * half_width, half_width, 2)

    both = jnp.concatenate([half_features(patches), half_features(cotangent)], axis=-1)
    received = lax.all_to_all(both, DP, 0, 0, tiled=True).reshape(slot_count, width)

    def packed(weights, gain, part, size, token):
        weights = after(weights, token)
        if direct:
            return call(
                functools.partial(pack_kernel, part),
                [((rows, size * len(weights)), bf16)] * 4,
                [near_ref, gain, *weights],
                [pltpu.VMEM((4, rows, size * len(weights)), bf16)],
            )
        scaled = [(w.astype(f32) * gain).astype(bf16) for w in weights[:-1]] + [weights[-1]]
        return [jnp.pad(w.reshape(rows, 4, part), ((0, 0), (0, 0), (0, size - part))).reshape(rows, -1) for w in scaled]

    attn_weights = [w_query, w_key, w_value, w_output.T]
    ffn_weights = [w_gate, w_up, w_down.T]
    def gathered(pack, *tokens):
        if direct:
            got = scatter_near(pack[1:])
            (flat,) = call(place_kernel, [((4,) + pack[0].shape, bf16)], [near_ref, pack[0], *got])
        else:
            flat = near_exchange(spread_pack(pack), my_near)
        cols = flat.shape[-1]
        flat = flat.reshape(4 * rows, cols)
        return flat, lambda operand: lax.all_gather(operand, (CORE,) + FAR, axis=0, tiled=True).reshape(2, width, cols)

    attn_flat, gather_attn = gathered(packed(attn_weights, gain_a, hp, hp, both))
    attn_w = gather_attn(attn_flat)
    ffn_flat, gather_ffn = gathered(packed(ffn_weights, gain_f, ff_part, ff_pad, attn_flat))
    doc_rows = jnp.concatenate(gather_near(after(doc_ids, attn_flat)), axis=0)
    my_counts = lax.dynamic_index_in_dim(counts, my_row, 0, keepdims=False)
    offsets = jnp.cumsum(my_counts) - my_counts
    slots = jnp.arange(slot_cap, dtype=jnp.int32)
    slot_token = jnp.where(slots[None, :] < my_counts[:, None], offsets[:, None] + slots[None, :], -1).reshape(-1)
    slot_row, slot_col = slot_token[None, :], slot_token[:, None]
    received, slot_row, slot_col, doc_rows, ffn_flat = lax.optimization_barrier(
        (received, slot_row, slot_col, doc_rows, ffn_flat)
    )
    ffn_w = gather_ffn(ffn_flat)
    if not direct:
        attn_w, ffn_w = (jnp.stack([natural_rows(w[i], far_sizes, rows) for i in range(2)]) for w in (attn_w, ffn_w))
    doc_own = lax.dynamic_slice_in_dim(doc_rows, core * toks, toks, 1)
    doc_oth = lax.dynamic_slice_in_dim(doc_rows, (1 - core) * toks, toks, 1)

    docs = (doc_own, doc_own.T, doc_oth.T)
    slab = ((toks, width), f32), ((toks, width), bf16), ((toks, width), bf16), ((toks, width), bf16)
    token_low = ((toks, width), bf16)
    half_low = ((toks, half_width), bf16)
    whole = ((group, width), bf16)
    sems = pltpu.SemaphoreType.DMA
    slab_low, slab_full, all_low = pltpu.VMEM((toks, width), bf16), pltpu.VMEM((toks, width), f32), pltpu.VMEM(*whole)
    acc = pltpu.VMEM((group, width), f32)
    attn_cols = pltpu.VMEM((2, width, 3 * hp), bf16)
    out_cols = pltpu.VMEM((2, width, hp), bf16)
    q_shape, kv_shape = ((group, 2 * hp), bf16), ((group, 4 * hp), bf16)
    head_count = 4 * 2 * hp // DH
    probs_shape = ((head_count, 2 * toks, toks), bf16)
    ffn_w_shape = ((2, width, 3 * ff_pad), bf16)

    own, give = call(collect_kernel, [token_low, token_low], [core_ref, slot_row, received])
    x, grad_low, norm, x_far = call(
        enter_kernel, [token_low] * 4, [core_ref, own, swap(give)], [sems((1,))], far_outs=(3,)
    )
    norm_a = gather_near(norm)
    grad_y = gather_near(grad_low)
    (attn_near,) = fetch([attn_w])
    q, kv, norm_a_all = call(
        project_kernel,
        [q_shape, kv_shape, whole],
        [after(norm, docs, ffn_flat), *norm_a[1:], attn_near],
        [all_low, sems((4,))],
        us=0,
        far_args=range(1, 4),
        far_outs=(2,),
    )
    probs, q_far, kv_far, kvf_far, attended, *branch = call(
        functools.partial(attend_kernel, score_scale),
        [probs_shape, q_shape, kv_shape, kv_shape, q_shape, *slab],
        [core_ref, q, kv, swap(kv), *docs, attn_w],
        [pltpu.VMEM(*probs_shape), pltpu.VMEM(*q_shape), out_cols, sems((9,)), sems((head_count,))],
        us=0,
        far_args=(7,),
        far_outs=range(5),
    )
    branch = after(branch, grad_y)
    hidden, norm = call(middle_kernel, [slab[0], token_low], [x, branch[0], *scatter_near(branch[1:])])
    norm_f = gather_near(norm)
    half_group = group // 2
    half_whole = ((half_group, width), bf16)
    y_first, y_second, ffn_near = call(
        fetch_ffn_kernel,
        [half_whole, half_whole, ffn_w_shape],
        [*grad_y, ffn_w],
        [sems((5,))],
        us=2,
        far_args=range(5),
    )
    mid_shape = ((group, 6 * ff_pad), bf16)
    half_acc = pltpu.VMEM((half_group, width), f32)
    mid, norm_f_all, hidden, grad_norm, *grad_norm_low = call(
        functools.partial(ffn_kernel, False),
        [mid_shape, whole, slab[0], slab[0], slab[1]],
        [*norm_f[:2], y_first, ffn_near, hidden],
        [half_acc, sems((1,))],
        8,
        3,
        (),
        (2,),
    )
    mid, norm_f_all, *more = call(
        functools.partial(ffn_kernel, True),
        [mid_shape, whole, slab[1], slab[1]],
        [*norm_f[2:], y_second, ffn_near, mid, norm_f_all],
        [half_acc],
        8,
        3,
        aliases={4: 0, 5: 1},
    )
    grad_norm_low += more
    branch = call(
        ffn_out_kernel,
        slab,
        [mid, ffn_w],
        [pltpu.VMEM((2, width, ff_pad), bf16), acc, sems((3,))],
        6,
        2,
        (1,),
        (0,),
    )
    ffn_grads_shape = ((4, 2, width // 4, 3 * ff_pad), bf16)
    ffn_grads, grad_norm = call(
        ffn_grads_kernel,
        [ffn_grads_shape, slab[0]],
        [norm_f_all, *grad_y, mid, grad_norm],
        [all_low, pltpu.VMEM(*ffn_grads_shape), sems((5,)), sems((4,))],
        12,
        4,
        range(1, 5),
        (0, 1),
    )
    grad_hidden, grad_hidden_low = call(
        middle_back_kernel,
        [slab[0], token_low],
        [*fetch([hidden, grad_low]), *fetch([after(grad_norm, branch[1:])]), *scatter_near(grad_norm_low)],
    )
    grad_branch = gather_near(grad_hidden_low)
    final_parts = scatter_near(after(branch[1:], grad_hidden_low))

    def reduced(grads):
        cols = grads.shape[-1]
        if not direct:
            halves = jnp.moveaxis(grads, 1, 0).reshape(2, width, cols)
            grads = jnp.stack([far_rows(half, far_sizes, rows).reshape(far, -1, cols) for half in halves], axis=1)
        return lax.psum_scatter(grads.reshape(-1, cols), FAR + (CORE,), scatter_dimension=0, tiled=True)

    ffn_part = reduced(ffn_grads)

    grad_q, grad_kv, far_give, attn_near, grad_branch_all, grad_hidden = call(
        functools.partial(attend_back_kernel, score_scale),
        [q_shape, ((group, 4 * hp), f32), kv_shape, ((2, width, 3 * hp), bf16), whole, slab[0]],
        [*grad_branch, *call(fetch_back_kernel, [((2, width, hp), bf16)], [attn_w], [sems((2,))], far_args=(0,)),
         *fetch([q_far, kv_far, kvf_far, probs]), grad_hidden, attn_w],
        [all_low, pltpu.VMEM(*q_shape), sems((4,))],
        us=7,
        far_args=(10,),
        far_outs=(4, 5),
    )
    out_own, out_give = call(
        final_kernel,
        [half_low, half_low],
        [core_ref, hidden, branch[0], *after(final_parts, grad_q)],
        [slab_full, slab_full, sems((2,))],
        far_args=(1, 2),
    )
    gqkv_own, gqkv_oth, own_norm, *grad_norm, n_all, g_all, att = call(
        project_back_kernel,
        [((group, 3 * hp), bf16), ((group, 3 * hp), bf16), *slab, whole, whole, q_shape],
        [grad_q, grad_kv, swap(after(far_give, final_parts)), attn_near, norm_a_all, grad_branch_all, attended],
        [acc, sems((3,))],
        us=2,
        far_args=(4, 5, 6),
    )
    arriving = scatter_near(grad_norm)
    grads_own, grads_oth = call(
        attn_grads_kernel,
        [((width, 4 * hp), bf16)] * 2,
        [core_ref, n_all, g_all, gqkv_own, gqkv_oth, att],
        us=3,
    )
    other = swap(grads_oth)
    planes = ()
    if direct:
        planes = call(core_sum_kernel, [((4 * rows, 4 * hp), bf16)] * 4, [far_ref, grads_own, other])
    own, give = call(
        leave_kernel,
        [token_low, token_low],
        [core_ref, *fetch([x_far, grad_hidden]), after(own_norm, planes), *arriving, out_own, out_give],
    )

    def finished(pieces, weights, gain, part, size):
        n = len(weights)
        return call(
            functools.partial(unpack_kernel, part),
            [((rows, 4 * part), f32)] * n + [((rows, 1), f32)],
            [near_ref, gain, *pieces, *weights[:-1]],
            [pltpu.VMEM((4, rows, n * size), bf16)],
        )

    def finished_plain(blocks, weights, gain, part, size):
        blocks = near_exchange(blocks.reshape(4, rows, -1), my_near)
        raws = []
        for m in range(len(weights)):
            piece = blocks[:, :, m * size : m * size + part].astype(f32)
            raws.append(piece.transpose(1, 0, 2).reshape(rows, 4 * part))
        total = sum(jnp.sum(r * w.astype(f32), axis=1, keepdims=True) for r, w in zip(raws[:-1], weights[:-1]))
        return [r * gain for r in raws[:-1]] + [raws[-1], total]

    def returned(own, *tokens):
        (spread,) = call(spread_kernel, [((slot_count, width), bf16)], [core_ref, slot_col, after(own, tokens), swap(give)])
        back = lax.all_to_all(spread.reshape(peers, slot_cap, width), DP, 0, 0, tiled=True)
        return back.reshape(slot_count, width)

    if direct:
        back = returned(own)
        planes = [planes[0]] + [far_shift(planes[k], k) for k in range(1, 4)]

        def pieces_of(part):
            pieces = call(pick_kernel, [((rows, part.shape[1]), bf16)] * 4, [near_ref, part], [sems((4,))], far_args=(1,))
            return [pieces[0]] + scatter_near(pieces[1:])

        *ffn_grads, sum_f = finished(pieces_of(after(ffn_part, planes[1])), ffn_weights, gain_f, ff_part, ff_pad)
        planes[0] = after(planes[0], ffn_grads)
        pieces = call(far_sum_kernel, [((rows, 4 * hp), bf16)] * 4, [near_ref, *planes], us=23)
        pieces = [pieces[0]] + scatter_near(pieces[1:])
        *attn_grads, sum_a = finished(pieces, attn_weights, gain_a, hp, hp)
        back = after(back, ffn_grads, attn_grads)
    else:
        back = returned(own)
        total = far_rows((grads_own.astype(f32) + other.astype(f32)).astype(bf16), far_sizes, rows)
        attn_part = lax.psum_scatter(total, FAR, scatter_dimension=0, tiled=True)
        *attn_grads, sum_a = finished_plain(attn_part, attn_weights, gain_a, hp, hp)
        *ffn_grads, sum_f = finished_plain(ffn_part, ffn_weights, gain_f, ff_part, ff_pad)
    gains = jnp.concatenate([sum_a, sum_f], axis=1).T
    gains = gains + swap(gains)
    outputs, input_grad = call(join_kernel, [((slot_count, width), bf16)] * 2, [core_ref, back, swap(back)])
    grad_q, grad_k, grad_v, grad_o = attn_grads
    grad_g, grad_u, grad_d = ffn_grads
    return (
        outputs.reshape(patches.shape),
        input_grad.reshape(patches.shape),
        grad_q,
        grad_k,
        grad_v,
        grad_o.T,
        grad_g,
        grad_u,
        grad_d.T,
        gains[0],
        gains[1],
    )


def solution(mesh):
    dp_size = mesh.shape["dp"]
    side = round((dp_size / 2) ** (1 / 3))
    grid = (2 * side, side // 2, 2, side // 2, 2, 2)
    inner = Mesh(np.asarray(mesh.devices).reshape(grid), ("z", "yh", "yl", "xh", "xl", "c"))
    rows_first = P(DP, "c")
    cols_first = P("c", DP)
    blocks = P(DP, None, None, None)
    weights = (rows_first, rows_first, rows_first, cols_first, rows_first, rows_first, cols_first, P(DP), P(DP))
    in_specs = (blocks, P(), P(DP, None)) + weights + (blocks,)
    out_specs = (blocks, blocks) + weights
    return jax.shard_map(body, mesh=inner, in_specs=in_specs, out_specs=out_specs, check_vma=False)
```

```python
import functools

import jax
import jax.numpy as jnp
import numpy as np
from jax import lax
from jax.experimental import pallas as pl
from jax.experimental.pallas import tpu as pltpu
from jax.sharding import Mesh, PartitionSpec as P

DH = 64
eps = 1e-05
masked_score = -1e30
bf16 = jnp.bfloat16
f32 = jnp.float32

DP = ("z", "yh", "yl", "xh", "xl")
FAR = ("z", "yh", "xh")
NEAR = ("yl", "xl")
CORE = "c"


def mm(left, right):
    return lax.dot_general(left, right, (((1,), (0,)), ((), ())), preferred_element_type=f32)


def mm_t(left, right):
    return lax.dot_general(left, right, (((1,), (1,)), ((), ())), preferred_element_type=f32)


def outer_sum(left, right):
    return lax.dot_general(left, right, (((0,), (0,)), ((), ())), preferred_element_type=f32)


def swap(value):
    return lax.ppermute(value, CORE, [(0, 1), (1, 0)])


def near(value, k):
    return lax.ppermute(value, NEAR, [(i, i ^ k) for i in range(4)])


def gather_near(value):
    return [value] + [near(value, k) for k in (1, 2, 3)]


def scatter_near(low):
    return [near(low[k - 1], k) for k in (1, 2, 3)]


def after(value, *tokens):
    return lax.optimization_barrier((value, tokens))[0]


def inverse_root(values):
    return lax.rsqrt(jnp.mean(values * values, axis=-1, keepdims=True) + eps)


def call(kernel, outs, args, scratch=(), limit=4, us=1.0, far_args=(), far_outs=(), aliases=None):
    def space(i, ndim, left):
        if i in left:
            return pl.BlockSpec(memory_space=pltpu.HBM)
        return pl.BlockSpec(memory_space=pltpu.SMEM if ndim == 1 else pltpu.VMEM)

    args = [pltpu.with_memory_space_constraint(a, pltpu.HBM) if i in far_args else a for i, a in enumerate(args)]
    return pl.pallas_call(
        kernel,
        out_shape=[
            pltpu.HBM(shape, kind) if i in far_outs else jax.ShapeDtypeStruct(shape, kind)
            for i, (shape, kind) in enumerate(outs)
        ],
        in_specs=[space(i, a.ndim, far_args) for i, a in enumerate(args)],
        out_specs=[space(i, 2, far_outs) for i in range(len(outs))],
        scratch_shapes=list(scratch),
        input_output_aliases=aliases or {},
        compiler_params=pltpu.CompilerParams(vmem_limit_bytes=limit << 20),
        cost_estimate=pl.CostEstimate(flops=int(us * 1e9), bytes_accessed=int(us * 1e6), transcendentals=0),
    )(*args)


def bring(pairs, sems, first=0):
    copies = [pltpu.make_async_copy(a, b, sems.at[first + i]) for i, (a, b) in enumerate(pairs)]
    for copy in copies:
        copy.start()
    return copies


def wait(copies):
    for copy in copies:
        copy.wait()


def stacked(refs, whole, first=0):
    rows = refs[0].shape[0]
    return [(ref, whole.at[pl.ds((first + r) * rows, rows)]) for r, ref in enumerate(refs)]


def lane_half(value, half):
    lanes = lax.broadcasted_iota(jnp.int32, value.shape, 1)
    keep = (lanes < DH) if half == 0 else (lanes >= DH)
    return jnp.where(keep, value, jnp.zeros_like(value))


def flipped(value):
    n = value.shape[1]
    eye = (
        lax.broadcasted_iota(jnp.int32, (n, n), 0) == lax.broadcasted_iota(jnp.int32, (n, n), 1)
    ).astype(bf16)
    return mm_t(eye, value).astype(bf16)


def fetch_kernel(*refs):
    n = (len(refs) - 1) // 2
    wait(bring(list(zip(refs[:n], refs[n : 2 * n])), refs[2 * n]))


def fetch(arrays, us=1.0):
    outs = [(a.shape, a.dtype) for a in arrays]
    return call(fetch_kernel, outs, arrays, [pltpu.SemaphoreType.DMA((len(arrays),))], 2, us, range(len(arrays)))


def pack_kernel(part, me, gain, *refs):
    n = len(refs) - 5
    weights, outs, blocks = refs[:n], refs[n : n + 4], refs[n + 4]
    size = blocks.shape[2] // n
    if size != part:
        blocks[...] = jnp.zeros(blocks.shape, blocks.dtype)
    for m, ref in enumerate(weights):
        w = ref[...].astype(f32)
        if m < n - 1:
            w = w * gain[...]
        w = w.astype(bf16)
        for i in range(4):
            blocks[i, :, m * size : m * size + part] = w[:, i * part : (i + 1) * part]
    for k, out in enumerate(outs):
        out[...] = blocks[me[0] ^ k]


def place_kernel(me, b0, b1, b2, b3, out):
    for k, ref in enumerate((b0, b1, b2, b3)):
        out[me[0] ^ k] = ref[...]


def place_far_kernel(me, far, b0, b1, b2, b3, out):
    for k, ref in enumerate((b0, b1, b2, b3)):
        plane = lax.rem(far[0] + (4 - k), 4)
        for i in range(4):
            out[plane * 4 + (me[0] ^ i)] = ref[i]


def join_attn_kernel(core, own, other, both, far, sems):
    both[core[0]] = own[...]
    both[1 - core[0]] = other[...]
    wait(bring([(both, far)], sems))


def collect_kernel(core, slot_row, slots, own, give):
    toks = own.shape[0]
    token = lax.broadcasted_iota(jnp.int32, (toks, slots.shape[0]), 0)
    for ref, half in ((own, core[0]), (give, 1 - core[0])):
        place = ((token + half * toks) == slot_row[...]).astype(bf16)
        ref[...] = mm(place, slots[...]).astype(bf16)


def normed(x):
    return x * inverse_root(x)


def enter_kernel(core, own, other, x_ref, y_ref, norm_ref, x_far, sems):
    half = own.shape[1] // 2
    first = core[0] == 0
    for ref, at in ((x_ref, slice(0, half)), (y_ref, slice(half, 2 * half))):
        ref[:, :half] = jnp.where(first, own[:, at], other[:, at])
        ref[:, half:] = jnp.where(first, other[:, at], own[:, at])
    kept = bring([(x_ref, x_far)], sems)
    norm_ref[...] = normed(x_ref[...].astype(f32)).astype(bf16)
    wait(kept)


def project_kernel(n0, n1, n2, n3, w, q_ref, kv_ref, n_far, all_n, sems):
    hp = w.shape[2] // 4
    toks = n0.shape[0]
    blocks = bring(stacked((n1, n2, n3), all_n, 1), sems)
    all_n[:toks, :] = n0[...]
    wait(blocks)
    kept = bring([(all_n, n_far)], sems, 3)
    for j in range(2):
        out = mm(all_n[...], w[j, :, : 3 * hp])
        q_ref[:, j * hp : (j + 1) * hp] = out[:, :hp].astype(bf16)
        kv_ref[:, 2 * j * hp : 2 * (j + 1) * hp] = out[:, hp:].astype(bf16)
    wait(kept)


def attend_kernel(scale, core, q_ref, kv, kvf, doc_q, doc_kn, doc_kf, w_far, p_far, q_far, kv_far, kvf_far, att_far, own_ref, b1, b2, b3, p_ref, att_ref, w, sems, p_sems):
    hp = q_ref.shape[1] // 2
    weights = bring([(w_far.at[j, :, pl.ds(3 * hp, hp)], w.at[j]) for j in range(2)], sems)
    kept = bring([(q_ref, q_far), (kv, kv_far), (kvf, kvf_far)], sems, 2)
    rows = doc_q.shape[0]
    toks = q_ref.shape[0] // rows
    key_pos = lax.broadcasted_iota(jnp.int32, (toks, toks), 0)
    query_pos = lax.broadcasted_iota(jnp.int32, (toks, toks), 1)
    causal = key_pos <= query_pos
    later = core[0] == 1
    for r in range(rows):
        at = slice(r * toks, (r + 1) * toks)
        dq = doc_q[r : r + 1, :]
        near_ok = causal & (doc_kn[:, r : r + 1] == dq)
        far_ok = (doc_kf[:, r : r + 1] == dq) & later
        for j in range(2):
            base = 2 * j * hp
            q2 = q_ref[at, j * hp : (j + 1) * hp]
            kn, kf = kv[at, base : base + hp], kvf[at, base : base + hp]
            v_t = jnp.concatenate(
                [flipped(kv[at, base + hp : base + 2 * hp]), flipped(kvf[at, base + hp : base + 2 * hp])], axis=1
            )
            pieces = []
            for h in range(2):
                qh = lane_half(q2, h)
                sn = jnp.where(near_ok, mm_t(kn, qh) * scale, masked_score)
                sf = jnp.where(far_ok, mm_t(kf, qh) * scale, masked_score)
                top = jnp.maximum(jnp.max(sn, axis=0, keepdims=True), jnp.max(sf, axis=0, keepdims=True))
                en, ef = jnp.exp(sn - top), jnp.exp(sf - top)
                total = jnp.sum(en, axis=0, keepdims=True) + jnp.sum(ef, axis=0, keepdims=True)
                inv = 1.0 / total
                p = (jnp.concatenate([en, ef], axis=0) * inv).astype(bf16)
                at_head = (r * 2 + j) * 2 + h
                p_ref[at_head] = p
                kept += bring([(p_ref.at[at_head], p_far.at[at_head])], p_sems, at_head)
                pieces.append(mm(v_t[h * DH : (h + 1) * DH, :], p))
            att_ref[at, j * hp : (j + 1) * hp] = flipped(jnp.concatenate(pieces, axis=0).astype(bf16)).astype(bf16)
        kept += bring([(att_ref.at[pl.ds(r * toks, toks)], att_far.at[pl.ds(r * toks, toks)])], sems, 5 + r)
        if r == 0:
            wait(weights)
        out = mm_t(att_ref[at, :hp], w[0]) + mm_t(att_ref[at, hp:], w[1])
        if r == 0:
            own_ref[...] = out
        else:
            (b1, b2, b3)[r - 1][...] = out.astype(bf16)
    wait(kept)


def attend_back_kernel(scale, g0, g1, g2, g3, w_out, q_ref, kv, kvf, p_ref, hidden_ref, w_far, dq_ref, near_ref, far_ref, w, g_far, hidden_far, all_g, ga_ref, sems):
    hp = q_ref.shape[1] // 2
    toks = g0.shape[0]
    out = bring([(w_far.at[j, :, pl.ds(0, 3 * hp)], w.at[j]) for j in range(2)] + [(hidden_ref, hidden_far)], sems)
    for r, ref in enumerate((g0, g1, g2, g3)):
        all_g[r * toks : (r + 1) * toks, :] = ref[...]
    out += bring([(all_g, g_far)], sems, 3)
    for j in range(2):
        ga_ref[:, j * hp : (j + 1) * hp] = mm(all_g[...], w_out[j]).astype(bf16)
    for r in range(4):
        at = slice(r * toks, (r + 1) * toks)
        for j in range(2):
            g = ga_ref[at, j * hp : (j + 1) * hp]
            base = 2 * j * hp
            q2 = q_ref[at, j * hp : (j + 1) * hp]
            v = jnp.concatenate([kv[at, base + hp : base + 2 * hp], kvf[at, base + hp : base + 2 * hp]], axis=0)
            k_t = jnp.concatenate([flipped(kv[at, base : base + hp]), flipped(kvf[at, base : base + hp])], axis=1)
            dqs, ps, dss, gs, qs = [], [], [], [], []
            for h in range(2):
                gh = lane_half(g, h)
                dp = mm_t(v, gh)
                p_low = p_ref[(r * 2 + j) * 2 + h]
                p = p_low.astype(f32)
                ds = p * (dp - jnp.sum(dp * p, axis=0, keepdims=True))
                ds = ds.astype(bf16)
                dqs.append(mm(k_t[h * DH : (h + 1) * DH, :], ds))
                ps.append(p_low)
                dss.append(ds)
                gs.append(gh)
                qs.append(lane_half(q2, h))
            dq = (jnp.concatenate(dqs, axis=0) * scale).astype(bf16)
            dq_ref[at, j * hp : (j + 1) * hp] = flipped(dq)
            dv = mm(jnp.concatenate(ps, axis=1), jnp.concatenate(gs, axis=0))
            dk = mm(jnp.concatenate(dss, axis=1), jnp.concatenate(qs, axis=0)) * scale
            near_ref[at, base : base + hp] = dk[:toks]
            near_ref[at, base + hp : base + 2 * hp] = dv[:toks]
            far_ref[at, base : base + hp] = dk[toks:].astype(bf16)
            far_ref[at, base + hp : base + 2 * hp] = dv[toks:].astype(bf16)
    wait(out)


def project_back_kernel(dq, near_g, back, w, n_far, g_far, att_far, gown, goth, own_ref, b1, b2, b3, n_ref, g_ref, att_ref, acc, sems):
    hp = dq.shape[1] // 2
    toks = own_ref.shape[0]
    got = bring([(n_far, n_ref), (g_far, g_ref), (att_far, att_ref)], sems)
    for j, g in enumerate((gown, goth)):
        g[:, :hp] = dq[:, j * hp : (j + 1) * hp]
        both = slice(2 * j * hp, 2 * (j + 1) * hp)
        g[:, hp:] = (near_g[:, both] + back[:, both].astype(f32)).astype(bf16)
    acc[...] = mm_t(gown[...], w[0])
    acc[...] += mm_t(goth[...], w[1])
    own_ref[...] = acc[:toks]
    for r, ref in enumerate((b1, b2, b3)):
        ref[...] = acc[(r + 1) * toks : (r + 2) * toks].astype(bf16)
    wait(got)


def total_of(refs):
    total = refs[0][...]
    for ref in refs[1:]:
        total = total + ref[...].astype(f32)
    return total


def middle_kernel(x, b0, b1, b2, b3, hidden, norm_ref):
    value = x[...].astype(f32) + total_of((b0, b1, b2, b3))
    hidden[...] = value
    norm_ref[...] = normed(value).astype(bf16)


def ffn_kernel(second, n0, n1, y, w, *refs):
    if second:
        mid, all_n, b0, b1, acc = refs[2:]
    else:
        hidden, mid, all_n, hidden_far, b0, b1, acc, sems = refs
        kept = bring([(hidden, hidden_far)], sems)
    toks = n0.shape[0]
    ff = w.shape[2] // 3
    rows = pl.ds(2 * toks if second else 0, 2 * toks)
    for r, ref in enumerate((n0, n1)):
        all_n[pl.ds((2 * second + r) * toks, toks), :] = ref[...]
    for j in range(2):
        gate = mm(all_n[rows, :], w[j, :, :ff])
        up = mm(all_n[rows, :], w[j, :, ff : 2 * ff])
        sig = jax.nn.sigmoid(gate)
        silu = gate * sig
        mid[rows, (4 + j) * ff : (5 + j) * ff] = (silu * up).astype(bf16)
        grad_product = mm(y[...], w[j, :, 2 * ff :])
        at = 2 * j * ff
        mid[rows, at : at + ff] = (grad_product * up * sig * (1.0 + gate * (1.0 - sig))).astype(bf16)
        mid[rows, at + ff : at + 2 * ff] = (grad_product * silu).astype(bf16)
        part = mm_t(mid[rows, at : at + 2 * ff], w[j, :, : 2 * ff])
        if j == 0:
            acc[...] = part
        else:
            acc[...] += part
    b0[...] = acc[:toks].astype(b0.dtype)
    b1[...] = acc[toks:].astype(bf16)
    if not second:
        wait(kept)


def fetch_ffn_kernel(y0, y1, y2, y3, w_far, y_first, y_second, w, sems):
    wait(bring(stacked((y0, y1), y_first) + stacked((y2, y3), y_second) + [(w_far, w)], sems))


def fetch_back_kernel(w_far, w, sems):
    hp = w.shape[2]
    wait(bring([(w_far.at[j, :, pl.ds(3 * hp, hp)], w.at[j]) for j in range(2)], sems))


def ffn_out_kernel(mid, w_far, own_far, b1, b2, b3, w, acc, sems):
    toks = b1.shape[0]
    ff = w.shape[2]
    weights = bring([(w_far.at[j, :, pl.ds(2 * ff, ff)], w.at[j]) for j in range(2)], sems)
    weights[0].wait()
    acc[...] = mm_t(mid[:, 4 * ff : 5 * ff], w[0])
    weights[1].wait()
    acc[...] += mm_t(mid[:, 5 * ff :], w[1])
    kept = bring([(acc.at[pl.ds(0, toks)], own_far)], sems, 2)
    for r, ref in enumerate((b1, b2, b3)):
        ref[...] = acc[(r + 1) * toks : (r + 2) * toks].astype(bf16)
    wait(kept)


def ffn_grads_kernel(all_n, y0, y1, y2, y3, mid, own_ref, out_far, own_far, all_y, out, sems, out_sems):
    rows = out.shape[2]
    ff = out.shape[3] // 3
    copies = bring(stacked((y0, y1, y2, y3), all_y), sems)
    kept = bring([(own_ref, own_far)], sems, 4)
    for i in range(4):
        grads = outer_sum(all_n[:, i * rows : (i + 1) * rows], mid[:, : 4 * ff]).astype(bf16)
        for j in range(2):
            out[i, j, :, : 2 * ff] = grads[:, 2 * j * ff : 2 * (j + 1) * ff]
        if i == 0:
            wait(copies)
        grads = outer_sum(all_y[:, i * rows : (i + 1) * rows], mid[:, 4 * ff :]).astype(bf16)
        for j in range(2):
            out[i, j, :, 2 * ff :] = grads[:, j * ff : (j + 1) * ff]
        kept += bring([(out.at[i], out_far.at[i])], out_sems, i)
    wait(kept)


def split_halves(core, value, own, give):
    half = own.shape[1]
    first = core[0] == 0
    own[...] = jnp.where(first, value[:, :half], value[:, half:])
    give[...] = jnp.where(first, value[:, half:], value[:, :half])


def final_kernel(core, hidden_far, own_far, b1, b2, b3, own, give, hidden, part, sems):
    wait(bring([(hidden_far, hidden), (own_far, part)], sems))
    split_halves(core, (hidden[...] + total_of((part, b1, b2, b3))).astype(bf16), own, give)


def norm_back(x, grad):
    root = inverse_root(x)
    norm = x * root
    return root * (grad - norm * jnp.mean(grad * norm, axis=-1, keepdims=True))


def middle_back_kernel(hidden, grad_low, b0, b1, b2, b3, out, low):
    grad = grad_low[...].astype(f32) + norm_back(hidden[...], total_of((b0, b1, b2, b3)))
    out[...] = grad
    low[...] = grad.astype(bf16)


def leave_kernel(core, x, grad_hidden, b0, b1, b2, b3, out_own, out_give, own, give):
    half = out_own.shape[1]
    own[:, :half] = out_own[...]
    give[:, :half] = out_give[...]
    grad = grad_hidden[...] + norm_back(x[...].astype(f32), total_of((b0, b1, b2, b3)))
    split_halves(core, grad.astype(bf16), own.at[:, half:], give.at[:, half:])


def spread_kernel(core, slot_col, own, other, out):
    toks = own.shape[0]
    first = core[0] == 0
    token = lax.broadcasted_iota(jnp.int32, (slot_col.shape[0], toks), 1)
    low = (token == slot_col[...]).astype(bf16)
    high = ((token + toks) == slot_col[...]).astype(bf16)
    own, other = own[...], other[...]
    out[...] = (mm(low, jnp.where(first, own, other)) + mm(high, jnp.where(first, other, own))).astype(bf16)


def join_kernel(core, own, other, out, grad):
    half = own.shape[1] // 2
    first = core[0] == 0
    for ref, at in ((out, slice(0, half)), (grad, slice(half, 2 * half))):
        ref[:, :half] = jnp.where(first, own[:, at], other[:, at])
        ref[:, half:] = jnp.where(first, other[:, at], own[:, at])


def attn_grads_kernel(core, all_n, all_g, g0, g1, att, own, oth):
    hp = att.shape[1] // 2
    for j, out in enumerate((own, oth)):
        mine = core[0] == j
        out[:, : 3 * hp] = outer_sum(all_n[...], jnp.where(mine, g0[...], g1[...])).astype(bf16)
        out[:, 3 * hp :] = outer_sum(all_g[...], jnp.where(mine, att[:, :hp], att[:, hp:])).astype(bf16)


def core_sum_kernel(far, own, other, t0, t1, t2, t3):
    rows = t0.shape[0]
    for k, ref in enumerate((t0, t1, t2, t3)):
        at = pl.ds(pl.multiple_of(lax.rem(far[0] + k, 4) * rows, rows), rows)
        ref[...] = (own[at, :].astype(f32) + other[at, :].astype(f32)).astype(bf16)


def far_sum_kernel(me, t0, t1, t2, t3, s0, s1, s2, s3):
    rows = s0.shape[0]
    for k, ref in enumerate((s0, s1, s2, s3)):
        at = pl.ds(pl.multiple_of((me[0] ^ k) * rows, rows), rows)
        total = t0[at, :].astype(f32)
        for other in (t1, t2, t3):
            total = total + other[at, :].astype(f32)
        ref[...] = total.astype(bf16)


def pick_kernel(me, part, s0, s1, s2, s3, sems):
    rows = s0.shape[0]
    pairs = [(part.at[pl.ds(pl.multiple_of((me[0] ^ k) * rows, rows), rows)], ref) for k, ref in enumerate((s0, s1, s2, s3))]
    wait(bring(pairs, sems))


def unpack_kernel(part, me, gain, s0, s1, s2, s3, *refs):
    n = (len(refs) - 1) // 2
    weights, outs, gain_sum, blocks = refs[: n - 1], refs[n - 1 : 2 * n - 1], refs[2 * n - 1], refs[2 * n]
    for k, ref in enumerate((s0, s1, s2, s3)):
        blocks[me[0] ^ k] = ref[...]
    size = blocks.shape[2] // n
    total = jnp.zeros(gain_sum.shape, f32)
    for m, out in enumerate(outs):
        for i in range(4):
            raw = blocks[i, :, m * size : m * size + part].astype(f32)
            at = slice(i * part, (i + 1) * part)
            if m < n - 1:
                total = total + jnp.sum(raw * weights[m][:, at].astype(f32), axis=1, keepdims=True)
                raw = raw * gain[...]
            out[:, at] = raw
    gain_sum[...] = total


def natural_rows(weight, far_sizes, rows):
    nz, nyh, nxh = far_sizes
    if nyh * nxh == 1:
        return weight
    cols = weight.shape[-1]
    split = weight.reshape(nz, nyh, nxh, 2, 2, rows, cols)
    return split.transpose(0, 1, 3, 2, 4, 5, 6).reshape(-1, cols)


def far_rows(weight, far_sizes, rows):
    nz, nyh, nxh = far_sizes
    if nyh * nxh == 1:
        return weight
    cols = weight.shape[-1]
    split = weight.reshape(nz, nyh, 2, nxh, 2, rows, cols)
    return split.transpose(0, 1, 3, 2, 4, 5, 6).reshape(-1, cols)


def spread_pack(pieces):
    rows = pieces[0].shape[0]
    blocks = [p.reshape(rows, 4, -1) for p in pieces]
    return jnp.concatenate(blocks, axis=-1).transpose(1, 0, 2)


def near_exchange(blocks, my_near):
    got = jnp.zeros(blocks.shape, blocks.dtype)
    for k in range(4):
        give = lax.dynamic_index_in_dim(blocks, my_near ^ k, 0, keepdims=True)
        got = lax.dynamic_update_slice_in_dim(got, near(give, k) if k else give, my_near ^ k, 0)
    return got


def body(patches, counts, doc_ids, w_query, w_key, w_value, w_output, w_gate, w_up, w_down, gain_attn, gain_ffn, cotangent):
    core = lax.axis_index(CORE)
    my_row = lax.axis_index(DP)
    my_near = lax.axis_index(NEAR)
    my_far = lax.axis_index(FAR)
    core_ref, near_ref, far_ref = core.reshape(1), my_near.reshape(1), my_far.reshape(1)
    peers, slot_cap, width = patches.shape[1:]
    half_width = width // 2
    slot_count = peers * slot_cap
    tok_count = doc_ids.shape[1]
    toks = tok_count // 2
    group = 4 * toks
    rows = w_query.shape[0]
    far_sizes = tuple(lax.axis_size(a) for a in FAR)
    far = far_sizes[0] * far_sizes[1] * far_sizes[2]
    direct = far == 4 and rows % 16 == 0
    score_scale = DH ** (-0.5)
    hp = w_query.shape[1] // 4
    ff_part = w_gate.shape[1] // 4
    ff_pad = -(-ff_part // 128) * 128
    gain_a = gain_attn.astype(f32)[:, None]
    gain_f = gain_ffn.astype(f32)[:, None]

    def far_shift(value, k):
        return lax.ppermute(value, FAR, [(i, (i + k) % far) for i in range(far)])

    def half_features(blocks):
        return lax.dynamic_slice_in_dim(blocks[0], core * half_width, half_width, 2)

    both = jnp.concatenate([half_features(patches), half_features(cotangent)], axis=-1)
    received = lax.all_to_all(both, DP, 0, 0, tiled=True).reshape(slot_count, width)

    def packed(weights, gain, part, size, token):
        weights = after(weights, token)
        if direct:
            return call(
                functools.partial(pack_kernel, part),
                [((rows, size * len(weights)), bf16)] * 4,
                [near_ref, gain, *weights],
                [pltpu.VMEM((4, rows, size * len(weights)), bf16)],
            )
        scaled = [(w.astype(f32) * gain).astype(bf16) for w in weights[:-1]] + [weights[-1]]
        return [jnp.pad(w.reshape(rows, 4, part), ((0, 0), (0, 0), (0, size - part))).reshape(rows, -1) for w in scaled]

    attn_weights = [w_query, w_key, w_value, w_output.T]
    ffn_weights = [w_gate, w_up, w_down.T]
    def gathered(pack, *tokens):
        if direct:
            got = scatter_near(pack[1:])
            (flat,) = call(place_kernel, [((4,) + pack[0].shape, bf16)], [near_ref, pack[0], *got])
        else:
            flat = near_exchange(spread_pack(pack), my_near)
        cols = flat.shape[-1]
        flat = flat.reshape(4 * rows, cols)
        return flat, lambda operand: lax.all_gather(operand, (CORE,) + FAR, axis=0, tiled=True).reshape(2, width, cols)

    attn_pack = packed(attn_weights, gain_a, hp, hp, both)
    if direct:
        attn_flat = jnp.stack([attn_pack[0]] + scatter_near(attn_pack[1:]))
        shifted = [attn_flat] + [far_shift(attn_flat, k) for k in range(1, far)]
    else:
        attn_flat, gather_attn = gathered(attn_pack)
        attn_w = gather_attn(attn_flat)
        shifted = attn_w
    ffn_flat, gather_ffn = gathered(packed(ffn_weights, gain_f, ff_part, ff_pad, attn_flat))
    doc_rows = jnp.concatenate(gather_near(after(doc_ids, attn_flat)), axis=0)
    my_counts = lax.dynamic_index_in_dim(counts, my_row, 0, keepdims=False)
    offsets = jnp.cumsum(my_counts) - my_counts
    slots = jnp.arange(slot_cap, dtype=jnp.int32)
    slot_token = jnp.where(slots[None, :] < my_counts[:, None], offsets[:, None] + slots[None, :], -1).reshape(-1)
    slot_row, slot_col = slot_token[None, :], slot_token[:, None]
    received, slot_row, slot_col, doc_rows, ffn_flat, shifted = lax.optimization_barrier(
        (received, slot_row, slot_col, doc_rows, ffn_flat, shifted)
    )
    ffn_w = gather_ffn(after(ffn_flat, shifted))
    if direct:
        (attn_own,) = call(place_far_kernel, [((16, rows, 4 * hp), bf16)], [near_ref, far_ref, *shifted])
        attn_own = attn_own.reshape(width, 4 * hp)
        attn_near, attn_w = call(
            join_attn_kernel,
            [((2, width, 4 * hp), bf16)] * 2,
            [core_ref, attn_own, swap(attn_own)],
            [pltpu.SemaphoreType.DMA((3,))],
            far_outs=(1,),
        )
    else:
        attn_w, ffn_w = (jnp.stack([natural_rows(w[i], far_sizes, rows) for i in range(2)]) for w in (attn_w, ffn_w))
    doc_own = lax.dynamic_slice_in_dim(doc_rows, core * toks, toks, 1)
    doc_oth = lax.dynamic_slice_in_dim(doc_rows, (1 - core) * toks, toks, 1)

    docs = (doc_own, doc_own.T, doc_oth.T)
    slab = ((toks, width), f32), ((toks, width), bf16), ((toks, width), bf16), ((toks, width), bf16)
    token_low = ((toks, width), bf16)
    half_low = ((toks, half_width), bf16)
    whole = ((group, width), bf16)
    sems = pltpu.SemaphoreType.DMA
    slab_low, slab_full, all_low = pltpu.VMEM((toks, width), bf16), pltpu.VMEM((toks, width), f32), pltpu.VMEM(*whole)
    acc = pltpu.VMEM((group, width), f32)
    attn_cols = pltpu.VMEM((2, width, 3 * hp), bf16)
    out_cols = pltpu.VMEM((2, width, hp), bf16)
    q_shape, kv_shape = ((group, 2 * hp), bf16), ((group, 4 * hp), bf16)
    head_count = 4 * 2 * hp // DH
    probs_shape = ((head_count, 2 * toks, toks), bf16)
    ffn_w_shape = ((2, width, 3 * ff_pad), bf16)

    own, give = call(collect_kernel, [token_low, token_low], [core_ref, slot_row, received], us=1)
    x, grad_low, norm, x_far = call(
        enter_kernel, [token_low] * 4, [core_ref, own, swap(give)], [sems((1,))], far_outs=(3,)
    )
    norm_a = gather_near(norm)
    grad_y = gather_near(grad_low)
    if not direct:
        (attn_near,) = fetch([attn_w])
    q, kv, norm_a_all = call(
        project_kernel,
        [q_shape, kv_shape, whole],
        [after(norm, docs, ffn_flat), *norm_a[1:], attn_near],
        [all_low, sems((4,))],
        us=0,
        far_args=range(1, 4),
        far_outs=(2,),
    )
    probs, q_far, kv_far, kvf_far, attended, *branch = call(
        functools.partial(attend_kernel, score_scale),
        [probs_shape, q_shape, kv_shape, kv_shape, q_shape, *slab],
        [core_ref, q, kv, swap(kv), *docs, attn_w],
        [pltpu.VMEM(*probs_shape), pltpu.VMEM(*q_shape), out_cols, sems((9,)), sems((head_count,))],
        us=0,
        far_args=(7,),
        far_outs=range(5),
    )
    branch = after(branch, grad_y)
    hidden, norm = call(middle_kernel, [slab[0], token_low], [x, branch[0], *scatter_near(branch[1:])])
    norm_f = gather_near(norm)
    half_group = group // 2
    half_whole = ((half_group, width), bf16)
    y_first, y_second, ffn_near = call(
        fetch_ffn_kernel,
        [half_whole, half_whole, ffn_w_shape],
        [*grad_y, ffn_w],
        [sems((5,))],
        us=2,
        far_args=range(5),
    )
    mid_shape = ((group, 6 * ff_pad), bf16)
    half_acc = pltpu.VMEM((half_group, width), f32)
    mid, norm_f_all, hidden, grad_norm, *grad_norm_low = call(
        functools.partial(ffn_kernel, False),
        [mid_shape, whole, slab[0], slab[0], slab[1]],
        [*norm_f[:2], y_first, ffn_near, hidden],
        [half_acc, sems((1,))],
        8,
        3,
        (),
        (2,),
    )
    mid, norm_f_all, *more = call(
        functools.partial(ffn_kernel, True),
        [mid_shape, whole, slab[1], slab[1]],
        [*norm_f[2:], y_second, ffn_near, mid, norm_f_all],
        [half_acc],
        8,
        3,
        aliases={4: 0, 5: 1},
    )
    grad_norm_low += more
    branch = call(
        ffn_out_kernel,
        slab,
        [mid, ffn_w],
        [pltpu.VMEM((2, width, ff_pad), bf16), acc, sems((3,))],
        6,
        2,
        (1,),
        (0,),
    )
    ffn_grads_shape = ((4, 2, width // 4, 3 * ff_pad), bf16)
    ffn_grads, grad_norm = call(
        ffn_grads_kernel,
        [ffn_grads_shape, slab[0]],
        [norm_f_all, *grad_y, mid, grad_norm],
        [all_low, pltpu.VMEM(*ffn_grads_shape), sems((5,)), sems((4,))],
        12,
        4,
        range(1, 5),
        (0, 1),
    )
    grad_hidden, grad_hidden_low = call(
        middle_back_kernel,
        [slab[0], token_low],
        [*fetch([hidden, grad_low]), *fetch([after(grad_norm, branch[1:])]), *scatter_near(grad_norm_low)],
    )
    grad_branch = gather_near(grad_hidden_low)
    final_parts = scatter_near(after(branch[1:], grad_hidden_low))

    def reduced(grads):
        cols = grads.shape[-1]
        if not direct:
            halves = jnp.moveaxis(grads, 1, 0).reshape(2, width, cols)
            grads = jnp.stack([far_rows(half, far_sizes, rows).reshape(far, -1, cols) for half in halves], axis=1)
        return lax.psum_scatter(grads.reshape(-1, cols), FAR + (CORE,), scatter_dimension=0, tiled=True)

    ffn_part = reduced(ffn_grads)

    grad_q, grad_kv, far_give, attn_near, grad_branch_all, grad_hidden = call(
        functools.partial(attend_back_kernel, score_scale),
        [q_shape, ((group, 4 * hp), f32), kv_shape, ((2, width, 3 * hp), bf16), whole, slab[0]],
        [*grad_branch, *call(fetch_back_kernel, [((2, width, hp), bf16)], [attn_w], [sems((2,))], far_args=(0,)),
         *fetch([q_far, kv_far, kvf_far, probs]), grad_hidden, attn_w],
        [all_low, pltpu.VMEM(*q_shape), sems((4,))],
        us=7,
        far_args=(10,),
        far_outs=(4, 5),
    )
    out_own, out_give = call(
        final_kernel,
        [half_low, half_low],
        [core_ref, hidden, branch[0], *after(final_parts, grad_q)],
        [slab_full, slab_full, sems((2,))],
        far_args=(1, 2),
    )
    gqkv_own, gqkv_oth, own_norm, *grad_norm, n_all, g_all, att = call(
        project_back_kernel,
        [((group, 3 * hp), bf16), ((group, 3 * hp), bf16), *slab, whole, whole, q_shape],
        [grad_q, grad_kv, swap(after(far_give, final_parts)), attn_near, norm_a_all, grad_branch_all, attended],
        [acc, sems((3,))],
        us=2,
        far_args=(4, 5, 6),
    )
    arriving = scatter_near(grad_norm)
    grads_own, grads_oth = call(
        attn_grads_kernel,
        [((width, 4 * hp), bf16)] * 2,
        [core_ref, n_all, g_all, gqkv_own, gqkv_oth, att],
        us=3,
    )
    other = swap(grads_oth)
    planes = ()
    if direct:
        planes = call(core_sum_kernel, [((4 * rows, 4 * hp), bf16)] * 4, [far_ref, grads_own, other])
    own, give = call(
        leave_kernel,
        [token_low, token_low],
        [core_ref, *fetch([x_far, grad_hidden]), after(own_norm, planes), *arriving, out_own, out_give],
    )

    def finished(pieces, weights, gain, part, size):
        n = len(weights)
        return call(
            functools.partial(unpack_kernel, part),
            [((rows, 4 * part), f32)] * n + [((rows, 1), f32)],
            [near_ref, gain, *pieces, *weights[:-1]],
            [pltpu.VMEM((4, rows, n * size), bf16)],
        )

    def finished_plain(blocks, weights, gain, part, size):
        blocks = near_exchange(blocks.reshape(4, rows, -1), my_near)
        raws = []
        for m in range(len(weights)):
            piece = blocks[:, :, m * size : m * size + part].astype(f32)
            raws.append(piece.transpose(1, 0, 2).reshape(rows, 4 * part))
        total = sum(jnp.sum(r * w.astype(f32), axis=1, keepdims=True) for r, w in zip(raws[:-1], weights[:-1]))
        return [r * gain for r in raws[:-1]] + [raws[-1], total]

    def returned(own, *tokens):
        (spread,) = call(spread_kernel, [((slot_count, width), bf16)], [core_ref, slot_col, after(own, tokens), swap(give)])
        back = lax.all_to_all(spread.reshape(peers, slot_cap, width), DP, 0, 0, tiled=True)
        return back.reshape(slot_count, width)

    if direct:
        back = returned(own)
        planes = [planes[0]] + [far_shift(planes[k], k) for k in range(1, 4)]

        def pieces_of(part):
            pieces = call(pick_kernel, [((rows, part.shape[1]), bf16)] * 4, [near_ref, part], [sems((4,))], far_args=(1,))
            return [pieces[0]] + scatter_near(pieces[1:])

        *ffn_grads, sum_f = finished(pieces_of(after(ffn_part, planes[1])), ffn_weights, gain_f, ff_part, ff_pad)
        planes[0] = after(planes[0], ffn_grads)
        pieces = call(far_sum_kernel, [((rows, 4 * hp), bf16)] * 4, [near_ref, *planes], us=23)
        pieces = [pieces[0]] + scatter_near(pieces[1:])
        *attn_grads, sum_a = finished(pieces, attn_weights, gain_a, hp, hp)
        back = after(back, ffn_grads, attn_grads)
    else:
        back = returned(own)
        total = far_rows((grads_own.astype(f32) + other.astype(f32)).astype(bf16), far_sizes, rows)
        attn_part = lax.psum_scatter(total, FAR, scatter_dimension=0, tiled=True)
        *attn_grads, sum_a = finished_plain(attn_part, attn_weights, gain_a, hp, hp)
        *ffn_grads, sum_f = finished_plain(ffn_part, ffn_weights, gain_f, ff_part, ff_pad)
    gains = jnp.concatenate([sum_a, sum_f], axis=1).T
    gains = gains + swap(gains)
    outputs, input_grad = call(join_kernel, [((slot_count, width), bf16)] * 2, [core_ref, back, swap(back)])
    grad_q, grad_k, grad_v, grad_o = attn_grads
    grad_g, grad_u, grad_d = ffn_grads
    return (
        outputs.reshape(patches.shape),
        input_grad.reshape(patches.shape),
        grad_q,
        grad_k,
        grad_v,
        grad_o.T,
        grad_g,
        grad_u,
        grad_d.T,
        gains[0],
        gains[1],
    )


def solution(mesh):
    dp_size = mesh.shape["dp"]
    side = round((dp_size / 2) ** (1 / 3))
    grid = (2 * side, side // 2, 2, side // 2, 2, 2)
    inner = Mesh(np.asarray(mesh.devices).reshape(grid), ("z", "yh", "yl", "xh", "xl", "c"))
    rows_first = P(DP, "c")
    cols_first = P("c", DP)
    blocks = P(DP, None, None, None)
    weights = (rows_first, rows_first, rows_first, cols_first, rows_first, rows_first, cols_first, P(DP), P(DP))
    in_specs = (blocks, P(), P(DP, None)) + weights + (blocks,)
    out_specs = (blocks, blocks) + weights
    return jax.shard_map(body, mesh=inner, in_specs=in_specs, out_specs=out_specs, check_vma=False)
```

```python
import functools

import jax
import jax.numpy as jnp
import numpy as np
from jax import lax
from jax.experimental import pallas as pl
from jax.experimental.pallas import tpu as pltpu
from jax.sharding import Mesh, PartitionSpec as P

DH = 64
eps = 1e-05
masked_score = -1e30
bf16 = jnp.bfloat16
f32 = jnp.float32

DP = ("z", "yh", "yl", "xh", "xl")
FAR = ("z", "yh", "xh")
NEAR = ("yl", "xl")
CORE = "c"


def mm(left, right):
    return lax.dot_general(left, right, (((1,), (0,)), ((), ())), preferred_element_type=f32)


def mm_t(left, right):
    return lax.dot_general(left, right, (((1,), (1,)), ((), ())), preferred_element_type=f32)


def outer_sum(left, right):
    return lax.dot_general(left, right, (((0,), (0,)), ((), ())), preferred_element_type=f32)


def swap(value):
    return lax.ppermute(value, CORE, [(0, 1), (1, 0)])


def near(value, k):
    return lax.ppermute(value, NEAR, [(i, i ^ k) for i in range(4)])


def gather_near(value):
    return [value] + [near(value, k) for k in (1, 2, 3)]


def scatter_near(low):
    return [near(low[k - 1], k) for k in (1, 2, 3)]


def after(value, *tokens):
    return lax.optimization_barrier((value, tokens))[0]


def inverse_root(values):
    return lax.rsqrt(jnp.mean(values * values, axis=-1, keepdims=True) + eps)


def call(kernel, outs, args, scratch=(), limit=4, us=1.0, far_args=(), far_outs=(), aliases=None):
    def space(i, ndim, left):
        if i in left:
            return pl.BlockSpec(memory_space=pltpu.HBM)
        return pl.BlockSpec(memory_space=pltpu.SMEM if ndim == 1 else pltpu.VMEM)

    args = [pltpu.with_memory_space_constraint(a, pltpu.HBM) if i in far_args else a for i, a in enumerate(args)]
    return pl.pallas_call(
        kernel,
        out_shape=[
            pltpu.HBM(shape, kind) if i in far_outs else jax.ShapeDtypeStruct(shape, kind)
            for i, (shape, kind) in enumerate(outs)
        ],
        in_specs=[space(i, a.ndim, far_args) for i, a in enumerate(args)],
        out_specs=[space(i, 2, far_outs) for i in range(len(outs))],
        scratch_shapes=list(scratch),
        input_output_aliases=aliases or {},
        compiler_params=pltpu.CompilerParams(vmem_limit_bytes=limit << 20),
        cost_estimate=pl.CostEstimate(flops=int(us * 1e9), bytes_accessed=int(us * 1e6), transcendentals=0),
    )(*args)


def bring(pairs, sems, first=0):
    copies = [pltpu.make_async_copy(a, b, sems.at[first + i]) for i, (a, b) in enumerate(pairs)]
    for copy in copies:
        copy.start()
    return copies


def wait(copies):
    for copy in copies:
        copy.wait()


def stacked(refs, whole, first=0):
    rows = refs[0].shape[0]
    return [(ref, whole.at[pl.ds((first + r) * rows, rows)]) for r, ref in enumerate(refs)]


def lane_half(value, half):
    lanes = lax.broadcasted_iota(jnp.int32, value.shape, 1)
    keep = (lanes < DH) if half == 0 else (lanes >= DH)
    return jnp.where(keep, value, jnp.zeros_like(value))


def flipped(value):
    n = value.shape[1]
    eye = (
        lax.broadcasted_iota(jnp.int32, (n, n), 0) == lax.broadcasted_iota(jnp.int32, (n, n), 1)
    ).astype(bf16)
    return mm_t(eye, value).astype(bf16)


def fetch_kernel(*refs):
    n = (len(refs) - 1) // 2
    wait(bring(list(zip(refs[:n], refs[n : 2 * n])), refs[2 * n]))


def fetch(arrays, us=1.0):
    outs = [(a.shape, a.dtype) for a in arrays]
    return call(fetch_kernel, outs, arrays, [pltpu.SemaphoreType.DMA((len(arrays),))], 2, us, range(len(arrays)))


def pack_kernel(part, me, gain, *refs):
    n = len(refs) - 5
    weights, outs, blocks = refs[:n], refs[n : n + 4], refs[n + 4]
    size = blocks.shape[2] // n
    if size != part:
        blocks[...] = jnp.zeros(blocks.shape, blocks.dtype)
    for m, ref in enumerate(weights):
        w = ref[...].astype(f32)
        if m < n - 1:
            w = w * gain[...]
        w = w.astype(bf16)
        for i in range(4):
            blocks[i, :, m * size : m * size + part] = w[:, i * part : (i + 1) * part]
    for k, out in enumerate(outs):
        out[...] = blocks[me[0] ^ k]


def place_kernel(me, b0, b1, b2, b3, out):
    for k, ref in enumerate((b0, b1, b2, b3)):
        out[me[0] ^ k] = ref[...]


def place_far_kernel(me, far, b0, b1, b2, b3, out):
    for k, ref in enumerate((b0, b1, b2, b3)):
        plane = lax.rem(far[0] + (4 - k), 4)
        for i in range(4):
            out[plane * 4 + (me[0] ^ i)] = ref[i]


def join_attn_kernel(core, own, other, both, far, sems):
    both[core[0]] = own[...]
    both[1 - core[0]] = other[...]
    wait(bring([(both, far)], sems))


def collect_kernel(core, slot_row, slots, own, give):
    toks = own.shape[0]
    token = lax.broadcasted_iota(jnp.int32, (toks, slots.shape[0]), 0)
    for ref, half in ((own, core[0]), (give, 1 - core[0])):
        place = ((token + half * toks) == slot_row[...]).astype(bf16)
        ref[...] = mm(place, slots[...]).astype(bf16)


def normed(x):
    return x * inverse_root(x)


def enter_kernel(core, own, other, x_ref, y_ref, norm_ref, x_far, sems):
    half = own.shape[1] // 2
    first = core[0] == 0
    for ref, at in ((x_ref, slice(0, half)), (y_ref, slice(half, 2 * half))):
        ref[:, :half] = jnp.where(first, own[:, at], other[:, at])
        ref[:, half:] = jnp.where(first, other[:, at], own[:, at])
    kept = bring([(x_ref, x_far)], sems)
    norm_ref[...] = normed(x_ref[...].astype(f32)).astype(bf16)
    wait(kept)


def project_kernel(n0, n1, n2, n3, w, q_ref, kv_ref, n_far, all_n, sems):
    hp = w.shape[2] // 4
    toks = n0.shape[0]
    blocks = bring(stacked((n1, n2, n3), all_n, 1), sems)
    all_n[:toks, :] = n0[...]
    wait(blocks)
    kept = bring([(all_n, n_far)], sems, 3)
    for j in range(2):
        out = mm(all_n[...], w[j, :, : 3 * hp])
        q_ref[:, j * hp : (j + 1) * hp] = out[:, :hp].astype(bf16)
        kv_ref[:, 2 * j * hp : 2 * (j + 1) * hp] = out[:, hp:].astype(bf16)
    wait(kept)


def attend_kernel(scale, core, q_ref, kv, kvf, doc_q, doc_kn, doc_kf, w_far, p_far, q_far, kv_far, kvf_far, att_far, own_ref, b1, b2, b3, p_ref, att_ref, w, sems, p_sems):
    hp = q_ref.shape[1] // 2
    weights = bring([(w_far.at[j, :, pl.ds(3 * hp, hp)], w.at[j]) for j in range(2)], sems)
    kept = bring([(q_ref, q_far), (kv, kv_far), (kvf, kvf_far)], sems, 2)
    rows = doc_q.shape[0]
    toks = q_ref.shape[0] // rows
    key_pos = lax.broadcasted_iota(jnp.int32, (toks, toks), 0)
    query_pos = lax.broadcasted_iota(jnp.int32, (toks, toks), 1)
    causal = key_pos <= query_pos
    later = core[0] == 1
    for r in range(rows):
        at = slice(r * toks, (r + 1) * toks)
        dq = doc_q[r : r + 1, :]
        near_ok = causal & (doc_kn[:, r : r + 1] == dq)
        far_ok = (doc_kf[:, r : r + 1] == dq) & later
        for j in range(2):
            base = 2 * j * hp
            q2 = q_ref[at, j * hp : (j + 1) * hp]
            kn, kf = kv[at, base : base + hp], kvf[at, base : base + hp]
            v_t = jnp.concatenate(
                [flipped(kv[at, base + hp : base + 2 * hp]), flipped(kvf[at, base + hp : base + 2 * hp])], axis=1
            )
            pieces = []
            for h in range(2):
                qh = lane_half(q2, h)
                sn = jnp.where(near_ok, mm_t(kn, qh) * scale, masked_score)
                sf = jnp.where(far_ok, mm_t(kf, qh) * scale, masked_score)
                top = jnp.maximum(jnp.max(sn, axis=0, keepdims=True), jnp.max(sf, axis=0, keepdims=True))
                en, ef = jnp.exp(sn - top), jnp.exp(sf - top)
                total = jnp.sum(en, axis=0, keepdims=True) + jnp.sum(ef, axis=0, keepdims=True)
                inv = 1.0 / total
                p = (jnp.concatenate([en, ef], axis=0) * inv).astype(bf16)
                at_head = (r * 2 + j) * 2 + h
                p_ref[at_head] = p
                kept += bring([(p_ref.at[at_head], p_far.at[at_head])], p_sems, at_head)
                pieces.append(mm(v_t[h * DH : (h + 1) * DH, :], p))
            att_ref[at, j * hp : (j + 1) * hp] = flipped(jnp.concatenate(pieces, axis=0).astype(bf16)).astype(bf16)
        kept += bring([(att_ref.at[pl.ds(r * toks, toks)], att_far.at[pl.ds(r * toks, toks)])], sems, 5 + r)
        if r == 0:
            wait(weights)
        out = mm_t(att_ref[at, :hp], w[0]) + mm_t(att_ref[at, hp:], w[1])
        if r == 0:
            own_ref[...] = out
        else:
            (b1, b2, b3)[r - 1][...] = out.astype(bf16)
    wait(kept)


def attend_back_kernel(scale, g0, g1, g2, g3, w_out, q_ref, kv, kvf, p_ref, hidden_ref, w_far, dq_ref, near_ref, far_ref, w, g_far, hidden_far, all_g, ga_ref, sems):
    hp = q_ref.shape[1] // 2
    toks = g0.shape[0]
    out = bring([(w_far.at[j, :, pl.ds(0, 3 * hp)], w.at[j]) for j in range(2)] + [(hidden_ref, hidden_far)], sems)
    for r, ref in enumerate((g0, g1, g2, g3)):
        all_g[r * toks : (r + 1) * toks, :] = ref[...]
    out += bring([(all_g, g_far)], sems, 3)
    for j in range(2):
        ga_ref[:, j * hp : (j + 1) * hp] = mm(all_g[...], w_out[j]).astype(bf16)
    for r in range(4):
        at = slice(r * toks, (r + 1) * toks)
        for j in range(2):
            g = ga_ref[at, j * hp : (j + 1) * hp]
            base = 2 * j * hp
            q2 = q_ref[at, j * hp : (j + 1) * hp]
            v = jnp.concatenate([kv[at, base + hp : base + 2 * hp], kvf[at, base + hp : base + 2 * hp]], axis=0)
            k_t = jnp.concatenate([flipped(kv[at, base : base + hp]), flipped(kvf[at, base : base + hp])], axis=1)
            dqs, ps, dss, gs, qs = [], [], [], [], []
            for h in range(2):
                gh = lane_half(g, h)
                dp = mm_t(v, gh)
                p_low = p_ref[(r * 2 + j) * 2 + h]
                p = p_low.astype(f32)
                ds = p * (dp - jnp.sum(dp * p, axis=0, keepdims=True))
                ds = ds.astype(bf16)
                dqs.append(mm(k_t[h * DH : (h + 1) * DH, :], ds))
                ps.append(p_low)
                dss.append(ds)
                gs.append(gh)
                qs.append(lane_half(q2, h))
            dq = (jnp.concatenate(dqs, axis=0) * scale).astype(bf16)
            dq_ref[at, j * hp : (j + 1) * hp] = flipped(dq)
            dv = mm(jnp.concatenate(ps, axis=1), jnp.concatenate(gs, axis=0))
            dk = mm(jnp.concatenate(dss, axis=1), jnp.concatenate(qs, axis=0)) * scale
            near_ref[at, base : base + hp] = dk[:toks]
            near_ref[at, base + hp : base + 2 * hp] = dv[:toks]
            far_ref[at, base : base + hp] = dk[toks:].astype(bf16)
            far_ref[at, base + hp : base + 2 * hp] = dv[toks:].astype(bf16)
    wait(out)


def project_back_kernel(dq, near_g, back, w, n_far, g_far, att_far, gown, goth, own_ref, b1, b2, b3, n_ref, g_ref, att_ref, acc, sems):
    hp = dq.shape[1] // 2
    toks = own_ref.shape[0]
    got = bring([(n_far, n_ref), (g_far, g_ref), (att_far, att_ref)], sems)
    for j, g in enumerate((gown, goth)):
        g[:, :hp] = dq[:, j * hp : (j + 1) * hp]
        both = slice(2 * j * hp, 2 * (j + 1) * hp)
        g[:, hp:] = (near_g[:, both] + back[:, both].astype(f32)).astype(bf16)
    acc[...] = mm_t(gown[...], w[0])
    acc[...] += mm_t(goth[...], w[1])
    own_ref[...] = acc[:toks]
    for r, ref in enumerate((b1, b2, b3)):
        ref[...] = acc[(r + 1) * toks : (r + 2) * toks].astype(bf16)
    wait(got)


def total_of(refs):
    total = refs[0][...]
    for ref in refs[1:]:
        total = total + ref[...].astype(f32)
    return total


def middle_kernel(x, b0, b1, b2, b3, hidden, norm_ref):
    value = x[...].astype(f32) + total_of((b0, b1, b2, b3))
    hidden[...] = value
    norm_ref[...] = normed(value).astype(bf16)


def ffn_kernel(second, n0, n1, y, w, *refs):
    if second:
        mid, all_n, b0, b1, acc = refs[2:]
    else:
        hidden, mid, all_n, hidden_far, b0, b1, acc, sems = refs
        kept = bring([(hidden, hidden_far)], sems)
    toks = n0.shape[0]
    ff = w.shape[2] // 3
    rows = pl.ds(2 * toks if second else 0, 2 * toks)
    for r, ref in enumerate((n0, n1)):
        all_n[pl.ds((2 * second + r) * toks, toks), :] = ref[...]
    for j in range(2):
        gate = mm(all_n[rows, :], w[j, :, :ff])
        up = mm(all_n[rows, :], w[j, :, ff : 2 * ff])
        sig = jax.nn.sigmoid(gate)
        silu = gate * sig
        mid[rows, (4 + j) * ff : (5 + j) * ff] = (silu * up).astype(bf16)
        grad_product = mm(y[...], w[j, :, 2 * ff :])
        at = 2 * j * ff
        mid[rows, at : at + ff] = (grad_product * up * sig * (1.0 + gate * (1.0 - sig))).astype(bf16)
        mid[rows, at + ff : at + 2 * ff] = (grad_product * silu).astype(bf16)
        part = mm_t(mid[rows, at : at + 2 * ff], w[j, :, : 2 * ff])
        if j == 0:
            acc[...] = part
        else:
            acc[...] += part
    b0[...] = acc[:toks].astype(b0.dtype)
    b1[...] = acc[toks:].astype(bf16)
    if not second:
        wait(kept)


def fetch_ffn_kernel(y0, y1, y2, y3, w_far, y_first, y_second, w, sems):
    wait(bring(stacked((y0, y1), y_first) + stacked((y2, y3), y_second) + [(w_far, w)], sems))


def fetch_back_kernel(w_far, w, sems):
    hp = w.shape[2]
    wait(bring([(w_far.at[j, :, pl.ds(3 * hp, hp)], w.at[j]) for j in range(2)], sems))


def ffn_out_kernel(mid, w_far, own_far, b1, b2, b3, w, acc, sems):
    toks = b1.shape[0]
    ff = w.shape[2]
    weights = bring([(w_far.at[j, :, pl.ds(2 * ff, ff)], w.at[j]) for j in range(2)], sems)
    weights[0].wait()
    acc[...] = mm_t(mid[:, 4 * ff : 5 * ff], w[0])
    weights[1].wait()
    acc[...] += mm_t(mid[:, 5 * ff :], w[1])
    kept = bring([(acc.at[pl.ds(0, toks)], own_far)], sems, 2)
    for r, ref in enumerate((b1, b2, b3)):
        ref[...] = acc[(r + 1) * toks : (r + 2) * toks].astype(bf16)
    wait(kept)


def ffn_grads_kernel(all_n, y0, y1, y2, y3, mid, own_ref, out_far, own_far, all_y, out, sems, out_sems):
    rows = out.shape[2]
    ff = out.shape[3] // 3
    copies = bring(stacked((y0, y1, y2, y3), all_y), sems)
    kept = bring([(own_ref, own_far)], sems, 4)
    for i in range(4):
        grads = outer_sum(all_n[:, i * rows : (i + 1) * rows], mid[:, : 4 * ff]).astype(bf16)
        for j in range(2):
            out[i, j, :, : 2 * ff] = grads[:, 2 * j * ff : 2 * (j + 1) * ff]
        if i == 0:
            wait(copies)
        grads = outer_sum(all_y[:, i * rows : (i + 1) * rows], mid[:, 4 * ff :]).astype(bf16)
        for j in range(2):
            out[i, j, :, 2 * ff :] = grads[:, j * ff : (j + 1) * ff]
        kept += bring([(out.at[i], out_far.at[i])], out_sems, i)
    wait(kept)


def split_halves(core, value, own, give):
    half = own.shape[1]
    first = core[0] == 0
    own[...] = jnp.where(first, value[:, :half], value[:, half:])
    give[...] = jnp.where(first, value[:, half:], value[:, :half])


def final_kernel(core, hidden_far, own_far, b1, b2, b3, own, give, hidden, part, sems):
    wait(bring([(hidden_far, hidden), (own_far, part)], sems))
    split_halves(core, (hidden[...] + total_of((part, b1, b2, b3))).astype(bf16), own, give)


def norm_back(x, grad):
    root = inverse_root(x)
    norm = x * root
    return root * (grad - norm * jnp.mean(grad * norm, axis=-1, keepdims=True))


def middle_back_kernel(hidden, grad_low, b0, b1, b2, b3, out, low):
    grad = grad_low[...].astype(f32) + norm_back(hidden[...], total_of((b0, b1, b2, b3)))
    out[...] = grad
    low[...] = grad.astype(bf16)


def leave_kernel(core, x, grad_hidden, b0, b1, b2, b3, out_own, out_give, own, give):
    half = out_own.shape[1]
    own[:, :half] = out_own[...]
    give[:, :half] = out_give[...]
    grad = grad_hidden[...] + norm_back(x[...].astype(f32), total_of((b0, b1, b2, b3)))
    split_halves(core, grad.astype(bf16), own.at[:, half:], give.at[:, half:])


def spread_kernel(core, slot_col, own, other, out):
    toks = own.shape[0]
    first = core[0] == 0
    token = lax.broadcasted_iota(jnp.int32, (slot_col.shape[0], toks), 1)
    low = (token == slot_col[...]).astype(bf16)
    high = ((token + toks) == slot_col[...]).astype(bf16)
    own, other = own[...], other[...]
    out[...] = (mm(low, jnp.where(first, own, other)) + mm(high, jnp.where(first, other, own))).astype(bf16)


def join_kernel(core, own, other, out, grad):
    half = own.shape[1] // 2
    first = core[0] == 0
    for ref, at in ((out, slice(0, half)), (grad, slice(half, 2 * half))):
        ref[:, :half] = jnp.where(first, own[:, at], other[:, at])
        ref[:, half:] = jnp.where(first, other[:, at], own[:, at])


def attn_grads_kernel(core, all_n, all_g, g0, g1, att, own, oth):
    hp = att.shape[1] // 2
    for j, out in enumerate((own, oth)):
        mine = core[0] == j
        out[:, : 3 * hp] = outer_sum(all_n[...], jnp.where(mine, g0[...], g1[...])).astype(bf16)
        out[:, 3 * hp :] = outer_sum(all_g[...], jnp.where(mine, att[:, :hp], att[:, hp:])).astype(bf16)


def core_sum_kernel(far, own, other, t0, t1, t2, t3):
    rows = t0.shape[0]
    for k, ref in enumerate((t0, t1, t2, t3)):
        at = pl.ds(pl.multiple_of(lax.rem(far[0] + k, 4) * rows, rows), rows)
        ref[...] = (own[at, :].astype(f32) + other[at, :].astype(f32)).astype(bf16)


def far_sum_kernel(me, t0, t1, t2, t3, s0, s1, s2, s3):
    rows = s0.shape[0]
    for k, ref in enumerate((s0, s1, s2, s3)):
        at = pl.ds(pl.multiple_of((me[0] ^ k) * rows, rows), rows)
        total = t0[at, :].astype(f32)
        for other in (t1, t2, t3):
            total = total + other[at, :].astype(f32)
        ref[...] = total.astype(bf16)


def pick_kernel(me, part, s0, s1, s2, s3, sems):
    rows = s0.shape[0]
    pairs = [(part.at[pl.ds(pl.multiple_of((me[0] ^ k) * rows, rows), rows)], ref) for k, ref in enumerate((s0, s1, s2, s3))]
    wait(bring(pairs, sems))


def unpack_kernel(part, me, gain, s0, s1, s2, s3, *refs):
    n = (len(refs) - 1) // 2
    weights, outs, gain_sum, blocks = refs[: n - 1], refs[n - 1 : 2 * n - 1], refs[2 * n - 1], refs[2 * n]
    for k, ref in enumerate((s0, s1, s2, s3)):
        blocks[me[0] ^ k] = ref[...]
    size = blocks.shape[2] // n
    total = jnp.zeros(gain_sum.shape, f32)
    for m, out in enumerate(outs):
        for i in range(4):
            raw = blocks[i, :, m * size : m * size + part].astype(f32)
            at = slice(i * part, (i + 1) * part)
            if m < n - 1:
                total = total + jnp.sum(raw * weights[m][:, at].astype(f32), axis=1, keepdims=True)
                raw = raw * gain[...]
            out[:, at] = raw
    gain_sum[...] = total


def natural_rows(weight, far_sizes, rows):
    nz, nyh, nxh = far_sizes
    if nyh * nxh == 1:
        return weight
    cols = weight.shape[-1]
    split = weight.reshape(nz, nyh, nxh, 2, 2, rows, cols)
    return split.transpose(0, 1, 3, 2, 4, 5, 6).reshape(-1, cols)


def far_rows(weight, far_sizes, rows):
    nz, nyh, nxh = far_sizes
    if nyh * nxh == 1:
        return weight
    cols = weight.shape[-1]
    split = weight.reshape(nz, nyh, 2, nxh, 2, rows, cols)
    return split.transpose(0, 1, 3, 2, 4, 5, 6).reshape(-1, cols)


def spread_pack(pieces):
    rows = pieces[0].shape[0]
    blocks = [p.reshape(rows, 4, -1) for p in pieces]
    return jnp.concatenate(blocks, axis=-1).transpose(1, 0, 2)


def near_exchange(blocks, my_near):
    got = jnp.zeros(blocks.shape, blocks.dtype)
    for k in range(4):
        give = lax.dynamic_index_in_dim(blocks, my_near ^ k, 0, keepdims=True)
        got = lax.dynamic_update_slice_in_dim(got, near(give, k) if k else give, my_near ^ k, 0)
    return got


def body(patches, counts, doc_ids, w_query, w_key, w_value, w_output, w_gate, w_up, w_down, gain_attn, gain_ffn, cotangent):
    core = lax.axis_index(CORE)
    my_row = lax.axis_index(DP)
    my_near = lax.axis_index(NEAR)
    my_far = lax.axis_index(FAR)
    core_ref, near_ref, far_ref = core.reshape(1), my_near.reshape(1), my_far.reshape(1)
    peers, slot_cap, width = patches.shape[1:]
    half_width = width // 2
    slot_count = peers * slot_cap
    tok_count = doc_ids.shape[1]
    toks = tok_count // 2
    group = 4 * toks
    rows = w_query.shape[0]
    far_sizes = tuple(lax.axis_size(a) for a in FAR)
    far = far_sizes[0] * far_sizes[1] * far_sizes[2]
    direct = far == 4 and rows % 16 == 0
    score_scale = DH ** (-0.5)
    hp = w_query.shape[1] // 4
    ff_part = w_gate.shape[1] // 4
    ff_pad = -(-ff_part // 128) * 128
    gain_a = gain_attn.astype(f32)[:, None]
    gain_f = gain_ffn.astype(f32)[:, None]

    def far_shift(value, k):
        return lax.ppermute(value, FAR, [(i, (i + k) % far) for i in range(far)])

    def half_features(blocks):
        return lax.dynamic_slice_in_dim(blocks[0], core * half_width, half_width, 2)

    both = jnp.concatenate([half_features(patches), half_features(cotangent)], axis=-1)
    received = lax.all_to_all(both, DP, 0, 0, tiled=True).reshape(slot_count, width)

    def packed(weights, gain, part, size, token):
        weights = after(weights, token)
        if direct:
            return call(
                functools.partial(pack_kernel, part),
                [((rows, size * len(weights)), bf16)] * 4,
                [near_ref, gain, *weights],
                [pltpu.VMEM((4, rows, size * len(weights)), bf16)],
            )
        scaled = [(w.astype(f32) * gain).astype(bf16) for w in weights[:-1]] + [weights[-1]]
        return [jnp.pad(w.reshape(rows, 4, part), ((0, 0), (0, 0), (0, size - part))).reshape(rows, -1) for w in scaled]

    attn_weights = [w_query, w_key, w_value, w_output.T]
    ffn_weights = [w_gate, w_up, w_down.T]
    def gathered(pack, *tokens):
        if direct:
            got = scatter_near(pack[1:])
            (flat,) = call(place_kernel, [((4,) + pack[0].shape, bf16)], [near_ref, pack[0], *got])
        else:
            flat = near_exchange(spread_pack(pack), my_near)
        cols = flat.shape[-1]
        flat = flat.reshape(4 * rows, cols)
        return flat, lambda operand: lax.all_gather(operand, (CORE,) + FAR, axis=0, tiled=True).reshape(2, width, cols)

    attn_pack = packed(attn_weights, gain_a, hp, hp, both)
    if direct:
        attn_flat = jnp.stack([attn_pack[0]] + scatter_near(attn_pack[1:]))
        shifted = [attn_flat] + [far_shift(attn_flat, k) for k in range(1, far)]
    else:
        attn_flat, gather_attn = gathered(attn_pack)
        attn_w = gather_attn(attn_flat)
        shifted = attn_w
    ffn_flat, gather_ffn = gathered(packed(ffn_weights, gain_f, ff_part, ff_pad, attn_flat))
    doc_rows = jnp.concatenate(gather_near(after(doc_ids, attn_flat)), axis=0)
    my_counts = lax.dynamic_index_in_dim(counts, my_row, 0, keepdims=False)
    offsets = jnp.cumsum(my_counts) - my_counts
    slots = jnp.arange(slot_cap, dtype=jnp.int32)
    slot_token = jnp.where(slots[None, :] < my_counts[:, None], offsets[:, None] + slots[None, :], -1).reshape(-1)
    slot_row, slot_col = slot_token[None, :], slot_token[:, None]
    received, slot_row, slot_col, doc_rows, ffn_flat, shifted = lax.optimization_barrier(
        (received, slot_row, slot_col, doc_rows, ffn_flat, shifted)
    )
    ffn_w = gather_ffn(after(ffn_flat, shifted))
    if direct:
        (attn_own,) = call(place_far_kernel, [((16, rows, 4 * hp), bf16)], [near_ref, far_ref, *shifted])
        attn_own = attn_own.reshape(width, 4 * hp)
        attn_near, attn_w = call(
            join_attn_kernel,
            [((2, width, 4 * hp), bf16)] * 2,
            [core_ref, attn_own, swap(attn_own)],
            [pltpu.SemaphoreType.DMA((3,))],
            far_outs=(1,),
        )
    else:
        attn_w, ffn_w = (jnp.stack([natural_rows(w[i], far_sizes, rows) for i in range(2)]) for w in (attn_w, ffn_w))
    doc_own = lax.dynamic_slice_in_dim(doc_rows, core * toks, toks, 1)
    doc_oth = lax.dynamic_slice_in_dim(doc_rows, (1 - core) * toks, toks, 1)

    docs = (doc_own, doc_own.T, doc_oth.T)
    slab = ((toks, width), f32), ((toks, width), bf16), ((toks, width), bf16), ((toks, width), bf16)
    token_low = ((toks, width), bf16)
    half_low = ((toks, half_width), bf16)
    whole = ((group, width), bf16)
    sems = pltpu.SemaphoreType.DMA
    slab_low, slab_full, all_low = pltpu.VMEM((toks, width), bf16), pltpu.VMEM((toks, width), f32), pltpu.VMEM(*whole)
    acc = pltpu.VMEM((group, width), f32)
    attn_cols = pltpu.VMEM((2, width, 3 * hp), bf16)
    out_cols = pltpu.VMEM((2, width, hp), bf16)
    q_shape, kv_shape = ((group, 2 * hp), bf16), ((group, 4 * hp), bf16)
    head_count = 4 * 2 * hp // DH
    probs_shape = ((head_count, 2 * toks, toks), bf16)
    ffn_w_shape = ((2, width, 3 * ff_pad), bf16)

    own, give = call(collect_kernel, [token_low, token_low], [core_ref, slot_row, received], us=1)
    x, grad_low, norm, x_far = call(
        enter_kernel, [token_low] * 4, [core_ref, own, swap(give)], [sems((1,))], far_outs=(3,)
    )
    norm_a = gather_near(norm)
    grad_y = gather_near(grad_low)
    if not direct:
        (attn_near,) = fetch([attn_w])
    q, kv, norm_a_all = call(
        project_kernel,
        [q_shape, kv_shape, whole],
        [after(norm, docs, ffn_flat), *norm_a[1:], attn_near],
        [all_low, sems((4,))],
        us=0,
        far_args=range(1, 4),
        far_outs=(2,),
    )
    probs, q_far, kv_far, kvf_far, attended, *branch = call(
        functools.partial(attend_kernel, score_scale),
        [probs_shape, q_shape, kv_shape, kv_shape, q_shape, *slab],
        [core_ref, q, kv, swap(kv), *docs, attn_w],
        [pltpu.VMEM(*probs_shape), pltpu.VMEM(*q_shape), out_cols, sems((9,)), sems((head_count,))],
        us=0,
        far_args=(7,),
        far_outs=range(5),
    )
    branch = after(branch, grad_y)
    hidden, norm = call(middle_kernel, [slab[0], token_low], [x, branch[0], *scatter_near(branch[1:])])
    norm_f = gather_near(norm)
    half_group = group // 2
    half_whole = ((half_group, width), bf16)
    y_first, y_second, ffn_near = call(
        fetch_ffn_kernel,
        [half_whole, half_whole, ffn_w_shape],
        [*grad_y, ffn_w],
        [sems((5,))],
        us=2,
        far_args=range(5),
    )
    mid_shape = ((group, 6 * ff_pad), bf16)
    half_acc = pltpu.VMEM((half_group, width), f32)
    mid, norm_f_all, hidden, grad_norm, *grad_norm_low = call(
        functools.partial(ffn_kernel, False),
        [mid_shape, whole, slab[0], slab[0], slab[1]],
        [*norm_f[:2], y_first, ffn_near, hidden],
        [half_acc, sems((1,))],
        8,
        3,
        (),
        (2,),
    )
    mid, norm_f_all, *more = call(
        functools.partial(ffn_kernel, True),
        [mid_shape, whole, slab[1], slab[1]],
        [*norm_f[2:], y_second, ffn_near, mid, norm_f_all],
        [half_acc],
        8,
        3,
        aliases={4: 0, 5: 1},
    )
    grad_norm_low += more
    branch = call(
        ffn_out_kernel,
        slab,
        [mid, ffn_w],
        [pltpu.VMEM((2, width, ff_pad), bf16), acc, sems((3,))],
        6,
        2,
        (1,),
        (0,),
    )
    ffn_grads_shape = ((4, 2, width // 4, 3 * ff_pad), bf16)
    ffn_grads, grad_norm = call(
        ffn_grads_kernel,
        [ffn_grads_shape, slab[0]],
        [norm_f_all, *grad_y, mid, grad_norm],
        [all_low, pltpu.VMEM(*ffn_grads_shape), sems((5,)), sems((4,))],
        12,
        4,
        range(1, 5),
        (0, 1),
    )
    grad_hidden, grad_hidden_low = call(
        middle_back_kernel,
        [slab[0], token_low],
        [*fetch([hidden, grad_low]), *fetch([after(grad_norm, branch[1:])]), *scatter_near(grad_norm_low)],
    )
    grad_branch = gather_near(grad_hidden_low)
    final_parts = scatter_near(after(branch[1:], grad_hidden_low))

    def reduced(grads):
        cols = grads.shape[-1]
        if not direct:
            halves = jnp.moveaxis(grads, 1, 0).reshape(2, width, cols)
            grads = jnp.stack([far_rows(half, far_sizes, rows).reshape(far, -1, cols) for half in halves], axis=1)
        return lax.psum_scatter(grads.reshape(-1, cols), FAR + (CORE,), scatter_dimension=0, tiled=True)

    ffn_part = reduced(ffn_grads)

    grad_q, grad_kv, far_give, attn_near, grad_branch_all, grad_hidden = call(
        functools.partial(attend_back_kernel, score_scale),
        [q_shape, ((group, 4 * hp), f32), kv_shape, ((2, width, 3 * hp), bf16), whole, slab[0]],
        [*grad_branch, *call(fetch_back_kernel, [((2, width, hp), bf16)], [attn_w], [sems((2,))], far_args=(0,)),
         *fetch([q_far, kv_far, kvf_far, probs]), grad_hidden, attn_w],
        [all_low, pltpu.VMEM(*q_shape), sems((4,))],
        us=7,
        far_args=(10,),
        far_outs=(4, 5),
    )
    out_own, out_give = call(
        final_kernel,
        [half_low, half_low],
        [core_ref, hidden, branch[0], *after(final_parts, grad_q)],
        [slab_full, slab_full, sems((2,))],
        far_args=(1, 2),
    )
    gqkv_own, gqkv_oth, own_norm, *grad_norm, n_all, g_all, att = call(
        project_back_kernel,
        [((group, 3 * hp), bf16), ((group, 3 * hp), bf16), *slab, whole, whole, q_shape],
        [grad_q, grad_kv, swap(after(far_give, final_parts)), attn_near, norm_a_all, grad_branch_all, attended],
        [acc, sems((3,))],
        us=2,
        far_args=(4, 5, 6),
    )
    arriving = scatter_near(grad_norm)
    grads_own, grads_oth = call(
        attn_grads_kernel,
        [((width, 4 * hp), bf16)] * 2,
        [core_ref, n_all, g_all, gqkv_own, gqkv_oth, att],
        us=3,
    )
    other = swap(grads_oth)
    planes = ()
    if direct:
        planes = call(core_sum_kernel, [((4 * rows, 4 * hp), bf16)] * 4, [far_ref, grads_own, other])
    own, give = call(
        leave_kernel,
        [token_low, token_low],
        [core_ref, *fetch([x_far, grad_hidden]), after(own_norm, planes), *arriving, out_own, out_give],
    )

    def finished(pieces, weights, gain, part, size):
        n = len(weights)
        return call(
            functools.partial(unpack_kernel, part),
            [((rows, 4 * part), f32)] * n + [((rows, 1), f32)],
            [near_ref, gain, *pieces, *weights[:-1]],
            [pltpu.VMEM((4, rows, n * size), bf16)],
        )

    def finished_plain(blocks, weights, gain, part, size):
        blocks = near_exchange(blocks.reshape(4, rows, -1), my_near)
        raws = []
        for m in range(len(weights)):
            piece = blocks[:, :, m * size : m * size + part].astype(f32)
            raws.append(piece.transpose(1, 0, 2).reshape(rows, 4 * part))
        total = sum(jnp.sum(r * w.astype(f32), axis=1, keepdims=True) for r, w in zip(raws[:-1], weights[:-1]))
        return [r * gain for r in raws[:-1]] + [raws[-1], total]

    def returned(own, *tokens):
        (spread,) = call(spread_kernel, [((slot_count, width), bf16)], [core_ref, slot_col, after(own, tokens), swap(give)])
        back = lax.all_to_all(spread.reshape(peers, slot_cap, width), DP, 0, 0, tiled=True)
        return back.reshape(slot_count, width)

    if direct:
        back = returned(own)
        planes = [planes[0]] + [far_shift(planes[k], k) for k in range(1, 4)]

        def pieces_of(part):
            pieces = call(pick_kernel, [((rows, part.shape[1]), bf16)] * 4, [near_ref, part], [sems((4,))], far_args=(1,))
            return [pieces[0]] + scatter_near(pieces[1:])

        *ffn_grads, sum_f = finished(pieces_of(after(ffn_part, planes[3])), ffn_weights, gain_f, ff_part, ff_pad)
        planes[0] = after(planes[0], ffn_grads)
        pieces = call(far_sum_kernel, [((rows, 4 * hp), bf16)] * 4, [near_ref, *planes], us=23)
        pieces = [pieces[0]] + scatter_near(pieces[1:])
        *attn_grads, sum_a = finished(pieces, attn_weights, gain_a, hp, hp)
        back = after(back, ffn_grads, attn_grads)
    else:
        back = returned(own)
        total = far_rows((grads_own.astype(f32) + other.astype(f32)).astype(bf16), far_sizes, rows)
        attn_part = lax.psum_scatter(total, FAR, scatter_dimension=0, tiled=True)
        *attn_grads, sum_a = finished_plain(attn_part, attn_weights, gain_a, hp, hp)
        *ffn_grads, sum_f = finished_plain(ffn_part, ffn_weights, gain_f, ff_part, ff_pad)
    gains = jnp.concatenate([sum_a, sum_f], axis=1).T
    gains = gains + swap(gains)
    outputs, input_grad = call(join_kernel, [((slot_count, width), bf16)] * 2, [core_ref, back, swap(back)])
    grad_q, grad_k, grad_v, grad_o = attn_grads
    grad_g, grad_u, grad_d = ffn_grads
    return (
        outputs.reshape(patches.shape),
        input_grad.reshape(patches.shape),
        grad_q,
        grad_k,
        grad_v,
        grad_o.T,
        grad_g,
        grad_u,
        grad_d.T,
        gains[0],
        gains[1],
    )


def solution(mesh):
    dp_size = mesh.shape["dp"]
    side = round((dp_size / 2) ** (1 / 3))
    grid = (2 * side, side // 2, 2, side // 2, 2, 2)
    inner = Mesh(np.asarray(mesh.devices).reshape(grid), ("z", "yh", "yl", "xh", "xl", "c"))
    rows_first = P(DP, "c")
    cols_first = P("c", DP)
    blocks = P(DP, None, None, None)
    weights = (rows_first, rows_first, rows_first, cols_first, rows_first, rows_first, cols_first, P(DP), P(DP))
    in_specs = (blocks, P(), P(DP, None)) + weights + (blocks,)
    out_specs = (blocks, blocks) + weights
    return jax.shard_map(body, mesh=inner, in_specs=in_specs, out_specs=out_specs, check_vma=False)
```
